32 devices in a mesh: gx: 4 (over z), gy: 4 (over x, core), layer: 2 (over y).
Axes of the slice: x: 2, y: 2, z: 4, core: 2. Of those that a mesh axis runs over, the one named last changes fastest.
Arguments:
- atom_feats: bfloat16 [2048, 128], P(('gx', 'gy', 'layer')), may hold values from -6 to 6
- bond_embed: bfloat16 [73728, 128], P(('gx', 'gy', 'layer')), may hold values from -6 to 6
- pair_dist: float32 [147456], P(('gx', 'gy', 'layer')), may hold values from 1.4 to 6.9
- neighbours: int32 [147456], P(('gx', 'gy', 'layer')), may hold values from 0 to 1151, as said below
- slot_kind: int32 [147456], P(('gx', 'gy', 'layer')), may hold values from 0 to 2
- own_rows: int32 [73728], P(('gx', 'gy', 'layer')), may hold values from 0 to 4607, as said below
- send_pos: int32 [73728], P(('gx', 'gy', 'layer')), may hold values from 0 to 2303, as said below
- recv_pos: int32 [147456], P(('gx', 'gy', 'layer')), may hold values from 0 to 2303, as said below
- w_left: bfloat16 [3, 128, 128], replicated, may hold values from -0.5 to 0.5
- w_right: bfloat16 [3, 128, 128], replicated, may hold values from -0.5 to 0.5
- w_edge_in: bfloat16 [3, 128, 128], replicated, may hold values from -0.5 to 0.5
- w_edge_out: bfloat16 [3, 128, 128], replicated, may hold values from -0.5 to 0.5
- w_msg: bfloat16 [2, 128, 128], replicated, may hold values from -0.5 to 0.5
- w_upd: bfloat16 [2, 128, 128], replicated, may hold values from -0.5 to 0.5
- node_gain: float32 [2, 128], replicated, may hold values from 0.1 to 1.9
- w_block: bfloat16 [128, 169], replicated, may hold values from -0.5 to 0.5
Outputs:
- blocks: bfloat16 [169, 147456], P(None, ('gx', 'gy', 'layer'))
The draws below stay inside these ranges and needn't reach their ends.
Inputs may be any that keep to these rules, and one draw needn't show every extreme that they name: `neighbours`: slots pair up: a slot of kind 1 or 2 and the slot of its partner atom that points back form one pair, one of kind 1 and the other of kind 2, with equal distance; empty slots pair with empty slots. Each atom has 4 slots towards each of the 18 offsets, half of them owned. `own_rows`: each domain's rows list its 2304 owned slots once each; the valid ones (kind 1) come first, at most 2112 of them, and some domain has exactly 2112. `send_pos`: within a domain every value occurs once; value // 128 is the offset of the partner's domain. `recv_pos`: for slots of kind 2: value // 128 is the reverse of the offset of the partner's domain.
All inputs are finite; a program needn't handle non-finite values.
Results may differ from the reference program's by a relative error of at most 0.019.
Values may be sent and summed in bfloat16 or wider, within the bound.
No kernel may reach another device: no remote copies, remote signals or barrier semaphores. Data moves between devices by JAX's collectives and lax.ppermute only.
A program may use at most 64 MiB of HBM per device.

```python
import jax
import jax.numpy as jnp
from jax import lax

C = 128
ORB = 13
BLOCK = 169
ATOM_DEV = 64
GROUPS = 4
NEIGH = 72
LAYERS = 3
OWN = 2304
VCAP = 2112
CAP = 128
ATOMS = 2048
OWNED = 73728
N_GX = 4
N_GY = 4
N_LAYER = 2


def partner_device_drawn(device, offset):
    sheet_step = offset // 9
    step_x = offset % 9 // 3 - 1
    step_y = offset % 3 - 1
    grid_x = device // (N_GY * N_LAYER)
    grid_y = device // N_LAYER % N_GY
    sheet_now = device % N_LAYER
    return ((grid_x + step_x) % N_GX * (N_GY * N_LAYER) + (grid_y + step_y) % N_GY * N_LAYER + (sheet_now + sheet_step) % N_LAYER).astype(jnp.int32)


def layout_tables(key):
    devices = N_GX * N_GY * N_LAYER
    half_groups = GROUPS // 2
    fanout = 18 * GROUPS
    capacity = half_groups * ATOM_DEV
    base_key = jax.random.fold_in(key, 4021)
    key_pairs, key_slots, key_order, key_count, key_pick, key_length = jax.random.split(base_key, 6)
    pair_base = jnp.broadcast_to(jnp.arange(ATOM_DEV, dtype=jnp.int32), (devices * 18 * half_groups, ATOM_DEV))
    forward = jax.random.permutation(key_pairs, pair_base, axis=1, independent=True).reshape(devices, 18, half_groups, ATOM_DEV)
    backward = jnp.argsort(forward, axis=-1).astype(jnp.int32)
    device_ids = jnp.arange(devices, dtype=jnp.int32)[:, None, None, None]
    offsets = jnp.arange(18, dtype=jnp.int32)[None, :, None, None]
    groups = jnp.arange(GROUPS, dtype=jnp.int32)[None, None, :, None]
    atom_ids = jnp.arange(ATOM_DEV, dtype=jnp.int32)[None, None, None, :]
    reverse = offsets // 9 * 9 + 8 - offsets % 9
    source = partner_device_drawn(device_ids, offsets)
    is_owner = groups < half_groups
    low_group = jnp.minimum(groups, half_groups - 1)
    high_group = jnp.maximum(groups - half_groups, 0)
    source_atom = backward[source, reverse, high_group, atom_ids]
    peer_atom = jnp.where(is_owner, forward[device_ids, offsets, low_group, atom_ids], source_atom)
    counts = jax.random.randint(key_count, (devices,), OWN * 78 // 100, VCAP + 1).astype(jnp.int32)
    counts = counts.at[jax.random.randint(key_pick, (), 0, devices)].set(VCAP)
    order_base = jnp.broadcast_to(jnp.arange(OWN, dtype=jnp.int32), (devices, OWN))
    ordering = jax.random.permutation(key_order, order_base, axis=1, independent=True).astype(jnp.int32)
    ranking = jnp.argsort(ordering, axis=1).astype(jnp.int32)
    owned_valid = (ranking < counts[:, None]).reshape(devices, 18, half_groups, ATOM_DEV)
    owned_code = jax.random.randint(key_length, (devices, 18, half_groups, ATOM_DEV), 0, 1048576)
    valid_full = jnp.where(is_owner, owned_valid[device_ids, offsets, low_group, atom_ids], owned_valid[source, reverse, high_group, source_atom])
    code_full = jnp.where(is_owner, owned_code[device_ids, offsets, low_group, atom_ids], owned_code[source, reverse, high_group, source_atom])
    slot_base = jnp.broadcast_to(jnp.arange(fanout, dtype=jnp.int32), (devices * ATOM_DEV, fanout))
    shuffle = jax.random.permutation(key_slots, slot_base, axis=1, independent=True).reshape(devices, ATOM_DEV, fanout).astype(jnp.int32)
    placing = jnp.argsort(shuffle, axis=-1).astype(jnp.int32)
    slot_offset = shuffle // GROUPS
    slot_group = shuffle % GROUPS
    device_index = jnp.arange(devices, dtype=jnp.int32)[:, None, None]
    atom_index = jnp.arange(ATOM_DEV, dtype=jnp.int32)[None, :, None]
    stored_peer = peer_atom[device_index, slot_offset, slot_group, atom_index]
    stored_valid = valid_full[device_index, slot_offset, slot_group, atom_index]
    stored_code = code_full[device_index, slot_offset, slot_group, atom_index]
    neighbour_ids = (slot_offset * ATOM_DEV + stored_peer).astype(jnp.int32)
    kinds = jnp.where(stored_valid, jnp.where(slot_group < half_groups, 1, 2), 0).astype(jnp.int32)
    stored_reverse = slot_offset // 9 * 9 + 8 - slot_offset % 9
    receive = jnp.where(slot_group >= half_groups, stored_reverse * capacity + (slot_group - half_groups) * ATOM_DEV + stored_peer, 0).astype(jnp.int32)
    own_offset = ordering // (half_groups * ATOM_DEV)
    own_group = ordering // ATOM_DEV % half_groups
    own_atom = ordering % ATOM_DEV
    device_column = jnp.arange(devices, dtype=jnp.int32)[:, None]
    rows_listed = (own_atom * fanout + placing[device_column, own_atom, own_offset * GROUPS + own_group]).astype(jnp.int32)
    sending = (own_offset * capacity + own_group * ATOM_DEV + own_atom).astype(jnp.int32)
    return (neighbour_ids.reshape(-1), kinds.reshape(-1), rows_listed.reshape(-1), sending.reshape(-1), receive.reshape(-1), stored_code.reshape(-1))


def draw_pair_dist(key, part):
    fraction = layout_tables(key)[5].astype(jnp.float32) / 1048576.0
    return 1.4 + 5.5 * fraction


def draw_neighbours(key, part):
    return layout_tables(key)[0]


def draw_slot_kind(key, part):
    return layout_tables(key)[1]


def draw_own_rows(key, part):
    return layout_tables(key)[2]


def draw_send_pos(key, part):
    return layout_tables(key)[3]


def draw_recv_pos(key, part):
    return layout_tables(key)[4]


def block_scale(own_key, dims, cuts, low, high):
    def one(axis_at, parts):
        steps = jax.random.uniform(jax.random.fold_in(jax.random.fold_in(own_key, 6), axis_at), (parts,), jnp.float32, low / len(cuts), high / len(cuts))
        return jnp.repeat(jnp.exp(steps), dims[axis_at] // parts).reshape((-1,) + (1,) * (len(dims) - axis_at - 1))

    loudness = one(*cuts[0])
    for cut in cuts[1:]:
        loudness = loudness * one(*cut)
    return loudness


def gaussian(stream_key, extent, scale, most, shards=(), held_as=jnp.bfloat16):
    loudness = block_scale(stream_key, extent, shards, -0.22, 0.18) if shards else 1.0
    entries = jax.random.normal(stream_key, extent, jnp.float32) * scale * loudness
    return jnp.minimum(jnp.maximum(entries, -most), most).astype(held_as)


def setup_inputs(seed: int = 0) -> dict:
    streams_of = jax.random.split(jax.random.key(seed), 17)
    atom_feats = gaussian(streams_of[0], (ATOMS, C), 1.0, 6.0, ((0, 32),))
    bond_embed = gaussian(streams_of[1], (OWNED, C), 1.0, 6.0, ((0, 32),))
    pair_dist = draw_pair_dist(jax.random.fold_in(streams_of[16], 71), 0)
    neighbours = draw_neighbours(jax.random.fold_in(streams_of[16], 71), 0)
    slot_kind = draw_slot_kind(jax.random.fold_in(streams_of[16], 71), 0)
    own_rows = draw_own_rows(jax.random.fold_in(streams_of[16], 71), 0)
    send_pos = draw_send_pos(jax.random.fold_in(streams_of[16], 71), 0)
    recv_pos = draw_recv_pos(jax.random.fold_in(streams_of[16], 71), 0)
    w_left = gaussian(streams_of[8], (LAYERS, C, C), C ** -0.5, 0.5)
    w_right = gaussian(streams_of[9], (LAYERS, C, C), C ** -0.5, 0.5)
    w_edge_in = gaussian(streams_of[10], (LAYERS, C, C), C ** -0.5, 0.5)
    w_edge_out = gaussian(streams_of[11], (LAYERS, C, C), C ** -0.5, 0.5)
    w_msg = gaussian(streams_of[12], (LAYERS - 1, C, C), C ** -0.5, 0.5)
    w_upd = gaussian(streams_of[13], (LAYERS - 1, C, C), C ** -0.5, 0.5)
    node_gain = jnp.clip(1.0 + 0.18 * jax.random.normal(streams_of[14], (LAYERS - 1, C), jnp.float32), 0.1, 1.9)
    w_block = gaussian(streams_of[15], (C, BLOCK), C ** -0.5, 0.5)
    return {"atom_feats": atom_feats, "bond_embed": bond_embed, "pair_dist": pair_dist, "neighbours": neighbours, "slot_kind": slot_kind, "own_rows": own_rows, "send_pos": send_pos, "recv_pos": recv_pos, "w_left": w_left, "w_right": w_right, "w_edge_in": w_edge_in, "w_edge_out": w_edge_out, "w_msg": w_msg, "w_upd": w_upd, "node_gain": node_gain, "w_block": w_block}


def partner_device(device, offset):
    sheet_step = offset // 9
    step_x = offset % 9 // 3 - 1
    step_y = offset % 3 - 1
    grid_x = device // (N_GY * N_LAYER)
    grid_y = device // N_LAYER % N_GY
    sheet_now = device % N_LAYER
    return ((grid_x + step_x) % N_GX * (N_GY * N_LAYER) + (grid_y + step_y) % N_GY * N_LAYER + (sheet_now + sheet_step) % N_LAYER).astype(jnp.int32)

def rms_norm(values):
    return values * lax.rsqrt(lax.optimization_barrier(jnp.mean(values * values, axis=-1, keepdims=True)) + 1e-06)

def cutoff(distance):
    scaled = distance / 7.0
    return (1.0 - scaled * scaled) ** 2

def reference(atom_feats, bond_embed, pair_dist, neighbours, slot_kind, own_rows, send_pos, recv_pos, w_left, w_right, w_edge_in, w_edge_out, w_msg, w_upd, node_gain, w_block):
    devices = N_GX * N_GY * N_LAYER
    slot_dev = ATOM_DEV * NEIGH
    channels = atom_feats.shape[1]
    slot_device = (jnp.arange(devices * slot_dev, dtype=jnp.int32) // slot_dev).astype(jnp.int32)
    peer_global = (partner_device(slot_device, neighbours // ATOM_DEV) * ATOM_DEV + neighbours % ATOM_DEV).astype(jnp.int32)
    row_device = (jnp.arange(devices * OWN, dtype=jnp.int32) // OWN).astype(jnp.int32)
    row_slot = (row_device * slot_dev + own_rows).astype(jnp.int32)
    row_atom = (row_slot // NEIGH).astype(jnp.int32)
    row_peer = peer_global[row_slot]
    envelope = cutoff(pair_dist) * (slot_kind > 0).astype(jnp.float32)
    hidden = atom_feats
    edge_state = bond_embed
    for layer_index in range(LAYERS):
        near_proj = jnp.dot(hidden, w_left[layer_index], preferred_element_type=jnp.float32).astype(jnp.bfloat16)
        far_proj = jnp.dot(hidden, w_right[layer_index], preferred_element_type=jnp.float32).astype(jnp.bfloat16)
        edge_in = w_edge_in[layer_index]
        edge_out = w_edge_out[layer_index]

        def edge_step(pieces):
            state_rows, atom_index, peer_index = pieces
            inner_proj = jnp.dot(state_rows, edge_in, preferred_element_type=jnp.float32)
            mixed_gate = jax.nn.silu(inner_proj * near_proj[atom_index].astype(jnp.float32) * far_proj[peer_index].astype(jnp.float32)).astype(jnp.bfloat16)
            renewed = state_rows.astype(jnp.float32) + jnp.dot(mixed_gate, edge_out, preferred_element_type=jnp.float32)
            return rms_norm(renewed).astype(jnp.bfloat16)
        new_state = lax.map(edge_step, (edge_state.reshape(devices, OWN, channels), row_atom.reshape(devices, OWN), row_peer.reshape(devices, OWN)))
        if layer_index + 1 < LAYERS:
            message = jnp.dot(hidden, w_msg[layer_index], preferred_element_type=jnp.float32).astype(jnp.bfloat16)

            def node_step(pieces):
                peer_ids, weights = pieces
                gathered = message[peer_ids].astype(jnp.float32) * weights[:, None]
                return (lax.optimization_barrier(jnp.sum(gathered.reshape(ATOM_DEV, NEIGH, channels), axis=1)) * 0.125).astype(jnp.bfloat16)
            summed = lax.map(node_step, (peer_global.reshape(devices, slot_dev), envelope.reshape(devices, slot_dev))).reshape(devices * ATOM_DEV, channels)
            updated = hidden.astype(jnp.float32) + jax.nn.silu(jnp.dot(summed, w_upd[layer_index], preferred_element_type=jnp.float32))
            hidden = (rms_norm(updated) * node_gain[layer_index].astype(jnp.float32)).astype(jnp.bfloat16)
        edge_state = new_state.reshape(devices * OWN, channels)
    swapped = w_block.reshape(channels, ORB, ORB).transpose(0, 2, 1).reshape(channels, ORB * ORB)
    device_rows = jnp.arange(devices, dtype=jnp.int32)[:, None]
    inverse_row = jnp.zeros((devices, 18 * CAP), jnp.int32).at[device_rows, send_pos.reshape(devices, OWN)].set(jnp.broadcast_to(jnp.arange(OWN, dtype=jnp.int32), (devices, OWN)))

    def block_step(device_index):
        start = (device_index * slot_dev).astype(jnp.int32)
        kind_here = lax.dynamic_slice_in_dim(slot_kind, start, slot_dev)
        nbr_here = lax.dynamic_slice_in_dim(neighbours, start, slot_dev)
        recv_here = lax.dynamic_slice_in_dim(recv_pos, start, slot_dev)
        row_start = (device_index * OWN).astype(jnp.int32)
        state_rows = lax.dynamic_slice_in_dim(edge_state, row_start, OWN)
        rows_here = lax.dynamic_slice_in_dim(own_rows, row_start, OWN)
        direct = lax.dot_general(w_block, state_rows, (((0,), (1,)), ((), ())), preferred_element_type=jnp.float32)
        own_part = jnp.zeros((ORB * ORB, slot_dev), jnp.float32).at[:, rows_here].set(direct)
        sender = partner_device(device_index, nbr_here // ATOM_DEV)
        sender_row = inverse_row[sender, recv_here]
        far_rows = edge_state[(sender * OWN + sender_row).astype(jnp.int32)]
        mirror = lax.dot_general(swapped, far_rows, (((0,), (1,)), ((), ())), preferred_element_type=jnp.float32)
        chosen = jnp.where(kind_here == 1, own_part, jnp.where(kind_here == 2, mirror, jnp.zeros_like(mirror)))
        return chosen.astype(jnp.bfloat16)
    per_device = lax.map(block_step, jnp.arange(devices, dtype=jnp.int32))
    return jnp.moveaxis(per_device, 0, 1).reshape(ORB * ORB, devices * slot_dev)
```

```python
import jax
import jax.numpy as jnp
from jax import lax
from jax.experimental import pallas as pl
from jax.experimental.pallas import tpu as pltpu
from jax.sharding import PartitionSpec as P

ORB = 13
GROUPS = 4
OFFS = 18
F32 = jnp.float32
BF16 = jnp.bfloat16
VMEM_LIMIT = 48 * 1024 * 1024


def swapped(value, axis):
    return lax.ppermute(value, axis, [(0, 1), (1, 0)])


def moved(value, axis, steps):
    count = lax.axis_size(axis)
    return lax.ppermute(value, axis, [(i, (i + steps) % count) for i in range(count)])


def with_halo(block, axis, dim):
    low = moved(block, axis, 1)
    high = moved(block, axis, -1)
    return jnp.concatenate([low, block, high], axis=dim)


def ghost_table(local):
    sheets = jnp.stack([local, swapped(local, "layer")])[:, None, None]
    framed = with_halo(with_halo(sheets, "gx", 1), "gy", 2)
    return framed.reshape(-1, local.shape[1])


def deliver(outgoing):
    sheets = jnp.stack([outgoing[0], swapped(outgoing[1], "layer")])
    rows = [moved(sheets[:, i], "gx", i - 1) if i != 1 else sheets[:, i] for i in range(3)]
    shifted = jnp.stack(rows, axis=1)
    cols = [moved(shifted[:, :, i], "gy", i - 1) if i != 1 else shifted[:, :, i] for i in range(3)]
    return jnp.stack(cols, axis=2)


def dot(a, b):
    return jnp.dot(a, b, preferred_element_type=F32)


def dot_nt(a, b):
    return lax.dot_general(a, b, (((1,), (1,)), ((), ())), preferred_element_type=F32)


def one_hot(mask):
    return jnp.where(mask, 1.0, 0.0).astype(BF16)


def silu(v):
    return v * (0.5 * jnp.tanh(0.5 * v) + 0.5)


def rms_norm(v):
    return v * lax.rsqrt(jnp.mean(v * v, axis=-1, keepdims=True) + 1e-06)


def iota(shape, dim):
    return lax.broadcasted_iota(jnp.int32, shape, dim)


def fiota(shape, dim):
    return iota(shape, dim).astype(F32)


def call(body, outs, *args, scratch=(), flops=1e8, nbytes=3e6):
    return pl.pallas_call(
        body,
        out_shape=outs,
        scratch_shapes=list(scratch),
        compiler_params=pltpu.CompilerParams(vmem_limit_bytes=VMEM_LIMIT),
        cost_estimate=pl.CostEstimate(
            flops=int(flops), bytes_accessed=int(nbytes), transcendentals=0
        ),
    )(*args)


def order_body(send_ref, bond_ref, out_ref):
    owned = bond_ref.shape[0]
    bond = bond_ref[...]
    step_rows = 256

    def step(i, carry):
        start = pl.multiple_of(i * step_rows, step_rows)
        pick = one_hot(iota((step_rows, owned), 0) + start == send_ref[...])
        out_ref[pl.ds(start, step_rows), :] = dot(pick, bond).astype(BF16)
        return carry

    lax.fori_loop(0, owned // step_rows, step, 0)


def prep_body(
    send_ref, own_ref, flat_ref, pack_ref, dist_ref, wb_ref,
    idx_own_ref, idx_mir_ref, adj_ref, src_ref, place_ref, wcat_ref,
):
    atoms, fan = pack_ref.shape
    owned = send_ref.shape[1]
    slots = flat_ref.shape[1]
    cap = owned // OFFS
    send = send_ref[...]
    own = own_ref[...].astype(F32)
    atom_r = jnp.floor((own + 0.5) * (1.0 / fan))
    slot_r = own - fan * atom_r
    off_r = (send >> 7).astype(F32)
    pos_r = (send & 127).astype(F32)
    pack = pack_ref[...]
    peer = (pack & 63).astype(F32)
    off = ((pack & 2047) >> 6).astype(F32)
    kind = (pack >> 11) & 3
    pos_in = ((pack >> 13) & 127).astype(F32)

    at_atom = fiota((atoms, owned), 0) == atom_r
    at_slot = fiota((fan, owned), 0) == slot_r
    slot_hot = one_hot(at_slot)
    place_own = dot_nt(jnp.where(at_atom, pos_r + 1.0, 0.0).astype(BF16), slot_hot)
    peer_t = jnp.transpose(
        jnp.concatenate([peer, jnp.zeros((atoms, 128 - fan), F32)], axis=1)
    )[:fan]
    peer_all = dot(peer_t.astype(BF16), one_hot(at_atom))
    peer_r = jnp.sum(jnp.where(at_slot, peer_all, 0.0), axis=0, keepdims=True)
    at_off = fiota((32, owned), 0) == off_r
    values = jnp.concatenate(
        [jnp.where(at_off, atom_r, 0.0), jnp.where(at_off, peer_r, 0.0)], axis=0
    ).astype(BF16)
    idx_own_ref[...] = dot_nt(one_hot(fiota((cap, owned), 0) == pos_r), values)

    flat = flat_ref[...]
    atom_s = jnp.floor((fiota((1, slots), 1) + 0.5) * (1.0 / fan))
    peer_s = (flat & 63).astype(F32)
    off_s = jnp.where(((flat >> 11) & 3) == 2, (flat & 2047) >> 6, -1).astype(F32)
    pos_s = ((flat >> 13) & 127).astype(F32)
    at_off = fiota((32, slots), 0) == off_s
    values = jnp.concatenate(
        [jnp.where(at_off, atom_s, 0.0), jnp.where(at_off, peer_s, 0.0)], axis=0
    ).astype(BF16)
    idx_mir_ref[...] = dot_nt(one_hot(fiota((cap, slots), 0) == pos_s), values)

    src = jnp.where(kind == 1, place_own - 1.0, jnp.where(kind == 2, pos_in + cap, -1.0))
    scaled = dist_ref[...] * (1.0 / 7.0)
    env = 1.0 - scaled * scaled
    env = jnp.where(kind > 0, env * env, 0.0)
    lane = fiota((atoms, fan), 1)
    rank = jnp.zeros((atoms, fan), F32)
    for s in range(fan - 1):
        rank += jnp.where((off == off[:, s : s + 1]) & (lane > float(s)), 1.0, 0.0)
    target = off * float(GROUPS) + rank
    place_ref[...] = jnp.transpose(
        jnp.concatenate([target, jnp.zeros((atoms, 128 - fan), F32)], axis=1)
    )[:fan]
    wide = fiota((atoms, 128), 1)
    src_sorted = jnp.full((atoms, 128), -1.0, F32)
    env_sorted = jnp.zeros((atoms, 128), F32)
    peer_sorted = jnp.zeros((atoms, 128), F32)
    for s in range(fan):
        here = target[:, s : s + 1] == wide
        src_sorted = jnp.where(here, src[:, s : s + 1], src_sorted)
        env_sorted = jnp.where(here, env[:, s : s + 1], env_sorted)
        peer_sorted = jnp.where(here, peer[:, s : s + 1], peer_sorted)
    src_ref[...] = src_sorted
    for m in range(OFFS // 2):
        tile = jnp.zeros((atoms, 128), F32)
        for u in range(2 * GROUPS):
            t = 2 * GROUPS * m + u
            column = peer_sorted[:, t : t + 1] + float(atoms * (u // GROUPS))
            tile += jnp.where(column == wide, env_sorted[:, t : t + 1], 0.0)
        adj_ref[:, 128 * m : 128 * (m + 1)] = tile.astype(BF16)

    block = wb_ref.shape[1]
    row = fiota((block, block), 0)
    col = fiota((block, block), 1)
    major = jnp.floor((row + 0.5) * (1.0 / ORB))
    wb = wb_ref[...]
    wcat_ref[:, :128] = dot_nt(one_hot(row == col), wb).astype(BF16)
    wcat_ref[:, 128:] = dot_nt(
        one_hot((row - ORB * major) * ORB + major == col), wb
    ).astype(BF16)


def node_body(layer):
    def body(adj_ref, ghost_ref, h_ref, wm_ref, wu_ref, gain_ref, out_ref):
        mixed = dot(adj_ref[...], ghost_ref[...]).astype(BF16)
        summed = (dot(mixed, wm_ref[layer]) * 0.125).astype(BF16)
        updated = h_ref[...].astype(F32) + silu(dot(summed, wu_ref[layer]))
        out_ref[...] = (rms_norm(updated) * gain_ref[layer : layer + 1, :]).astype(BF16)

    return body


def edge_block(state, atom_col, peer_col, local_table, ghost_block, w_in, w_out):
    rows, atoms = state.shape[0], local_table.shape[0]
    lane = fiota((rows, atoms), 1)
    first = dot(one_hot(atom_col == lane), local_table)
    second = dot(one_hot(peer_col == lane), ghost_block)
    gate = silu(dot(state, w_in) * first * second).astype(BF16)
    return rms_norm(state.astype(F32) + dot(gate, w_out)).astype(BF16)


def reverse(o):
    return o // 9 * 9 + 8 - o % 9


def edge_body(layer, mirrored):
    def body(e_ref, idx_ref, h_ref, ghost_ref, wl_ref, wg_ref, wi_ref, wo_ref, out_ref, table):
        atoms = h_ref.shape[0]
        cap = e_ref.shape[0] // OFFS
        local = dot(h_ref[...], wl_ref[layer]).astype(BF16)
        table[...] = dot(ghost_ref[...], wg_ref[layer]).astype(BF16)
        for o in range(OFFS):
            take = reverse(o) if mirrored and layer == 0 else o
            out_ref[cap * o : cap * (o + 1), :] = edge_block(
                e_ref[cap * take : cap * (take + 1), :],
                idx_ref[:, o : o + 1],
                idx_ref[:, 32 + o : 33 + o],
                local,
                table[atoms * o : atoms * (o + 1), :],
                wi_ref[layer],
                wo_ref[layer],
            )

    return body


def final_body(layer):
    def body(
        own_ref, mir_ref, io_ref, im_ref, h_ref, ghost_ref, wl_ref, wr_ref, wi_ref, wo_ref,
        src_ref, place_ref, wcat_ref, out_ref, left, right, z_own, z_mir, rows,
    ):
        atoms = h_ref.shape[0]
        cap = own_ref.shape[0] // OFFS
        fan = place_ref.shape[0]
        near = dot(h_ref[...], wl_ref[layer]).astype(BF16)
        far = dot(h_ref[...], wr_ref[layer]).astype(BF16)
        left[...] = dot(ghost_ref[...], wl_ref[layer]).astype(BF16)
        right[...] = dot(ghost_ref[...], wr_ref[layer]).astype(BF16)
        lane = fiota((atoms, 2 * cap), 1)
        for o in range(OFFS):
            span = slice(cap * o, cap * (o + 1))
            part = slice(atoms * o, atoms * (o + 1))
            e_own = edge_block(
                own_ref[span, :], io_ref[:, o : o + 1], io_ref[:, 32 + o : 33 + o],
                near, right[part, :], wi_ref[layer], wo_ref[layer],
            )
            e_mir = edge_block(
                mir_ref[span, :], im_ref[:, o : o + 1], im_ref[:, 32 + o : 33 + o],
                far, left[part, :], wi_ref[layer], wo_ref[layer],
            )
            hot = jnp.concatenate(
                [
                    jnp.where(src_ref[:, GROUPS * o + k : GROUPS * o + k + 1] == lane, 1.0, 0.0)
                    for k in range(GROUPS)
                ],
                axis=0,
            ).astype(BF16)
            x_own = dot(hot[:, :cap], e_own)
            x_mir = dot(hot[:, cap:], e_mir)
            for k in range(GROUPS):
                to = pl.ds(GROUPS * o + k, atoms, stride=fan)
                z_own[to, :] = x_own[atoms * k : atoms * (k + 1)]
                z_mir[to, :] = x_mir[atoms * k : atoms * (k + 1)]
        wide = fiota((fan, 2 * fan), 1)
        for m in range(atoms // 2):
            span = slice(2 * fan * m, 2 * fan * (m + 1))
            perm = jnp.concatenate(
                [
                    jnp.where(place_ref[:, 2 * m : 2 * m + 1] == wide, 1.0, 0.0),
                    jnp.where(place_ref[:, 2 * m + 1 : 2 * m + 2] + float(fan) == wide, 1.0, 0.0),
                ],
                axis=0,
            ).astype(BF16)
            rows[span, :128] = dot(perm, z_own[span, :].astype(BF16)).astype(BF16)
            rows[span, 128:] = dot(perm, z_mir[span, :].astype(BF16)).astype(BF16)
        step = 16 * fan
        for g in range(atoms // 16):
            out_ref[:, step * g : step * (g + 1)] = dot_nt(
                wcat_ref[...], rows[step * g : step * (g + 1), :]
            ).astype(BF16)

    return body


def shards(
    atom_feats, bond_embed, pair_dist, neighbours, slot_kind, own_rows, send_pos, recv_pos,
    w_left, w_right, w_edge_in, w_edge_out, w_msg, w_upd, node_gain, w_block,
):
    atoms, channels = atom_feats.shape
    slots = neighbours.shape[0]
    fan = slots // atoms
    owned = own_rows.shape[0]
    cap = owned // OFFS
    block = w_block.shape[1]
    ghosts = OFFS * atoms

    def array(*shape, dtype=F32):
        return jax.ShapeDtypeStruct(shape, dtype)

    send = send_pos.reshape(1, owned)
    pack = neighbours | (slot_kind << 11) | (recv_pos << 13)
    ordered = call(
        order_body, array(owned, channels, dtype=BF16), send, bond_embed, flops=1.4e9
    )
    idx_own, idx_mir, adjacency, source, place, w_cat = call(
        prep_body,
        (
            array(cap, 64),
            array(cap, 64),
            array(atoms, ghosts, dtype=BF16),
            array(atoms, 128),
            array(fan, atoms),
            array(block, 2 * channels, dtype=BF16),
        ),
        send,
        own_rows.reshape(1, owned),
        pack.reshape(1, slots),
        pack.reshape(atoms, fan),
        pair_dist.reshape(atoms, fan),
        w_block,
    )
    mirror = deliver(ordered.reshape(2, 3, 3, cap, channels)).reshape(owned, channels)
    hidden = atom_feats
    for layer in range(2):
        ghost = ghost_table(hidden)
        new_hidden = call(
            node_body(layer),
            array(atoms, channels, dtype=BF16),
            adjacency, ghost, hidden, w_msg, w_upd, node_gain,
            flops=2e7, nbytes=5e5,
        )
        state_shape = array(owned, channels, dtype=BF16)
        table = pltpu.VMEM((ghosts, channels), BF16)
        ordered = call(
            edge_body(layer, False), state_shape,
            ordered, idx_own, hidden, ghost, w_left, w_right, w_edge_in, w_edge_out,
            scratch=[table], flops=1e9,
        )
        mirror = call(
            edge_body(layer, True), state_shape,
            mirror, idx_mir, hidden, ghost, w_right, w_left, w_edge_in, w_edge_out,
            scratch=[table], flops=1e9,
        )
        hidden = new_hidden
    ghost = ghost_table(hidden)
    return call(
        final_body(2),
        array(block, slots, dtype=BF16),
        ordered, mirror, idx_own, idx_mir, hidden, ghost, w_left, w_right, w_edge_in, w_edge_out,
        source, place, w_cat,
        scratch=[
            pltpu.VMEM((ghosts, channels), BF16),
            pltpu.VMEM((ghosts, channels), BF16),
            pltpu.VMEM((slots, channels), F32),
            pltpu.VMEM((slots, channels), F32),
            pltpu.VMEM((slots, 2 * channels), BF16),
        ],
        flops=3e9,
    )


def solution(mesh):
    axes = ("gx", "gy", "layer")
    rows = P(axes, None)
    flat = P(axes)
    placed = (rows, rows) + (flat,) * 6 + (P(),) * 8
    return jax.shard_map(
        shards,
        mesh=mesh,
        in_specs=placed,
        out_specs=P(None, axes),
        check_vma=False,
    )
```

```python
import jax
import jax.numpy as jnp
from jax import lax
from jax.experimental import pallas as pl
from jax.experimental.pallas import tpu as pltpu
from jax.sharding import PartitionSpec as P

ORB = 13
GROUPS = 4
OFFS = 18
F32 = jnp.float32
BF16 = jnp.bfloat16
VMEM_LIMIT = 48 * 1024 * 1024


def swapped(value, axis):
    return lax.ppermute(value, axis, [(0, 1), (1, 0)])


def moved(value, axis, steps):
    count = lax.axis_size(axis)
    return lax.ppermute(value, axis, [(i, (i + steps) % count) for i in range(count)])


def with_halo(block, axis, dim):
    low = moved(block, axis, 1)
    high = moved(block, axis, -1)
    return jnp.concatenate([low, block, high], axis=dim)


def ghosts_of(sheets):
    framed = with_halo(with_halo(sheets, "gx", 1), "gy", 2)
    return framed.reshape(-1, sheets.shape[-1])


def deliver(outgoing):
    sheets = jnp.stack([outgoing[0], swapped(outgoing[1], "layer")])
    rows = [moved(sheets[:, i], "gx", i - 1) if i != 1 else sheets[:, i] for i in (2, 1, 0)]
    shifted = jnp.stack(rows, axis=1)
    cols = [moved(shifted[:, :, i], "gy", i - 1) if i != 1 else shifted[:, :, i] for i in (2, 1, 0)]
    return jnp.stack(cols, axis=2)


def dot(a, b):
    return jnp.dot(a, b, preferred_element_type=F32)


def dot_nt(a, b):
    return lax.dot_general(a, b, (((1,), (1,)), ((), ())), preferred_element_type=F32)


def one_hot(mask):
    return jnp.where(mask, 1.0, 0.0).astype(BF16)


def silu(v):
    return v * (0.5 * jnp.tanh(0.5 * v) + 0.5)


def rms_norm(v):
    return v * lax.rsqrt(jnp.mean(v * v, axis=-1, keepdims=True) + 1e-06)


def iota(shape, dim):
    return lax.broadcasted_iota(jnp.int32, shape, dim)


def fiota(shape, dim):
    return iota(shape, dim).astype(F32)


def call(body, outs, *args, scratch=(), us=1.0):
    return pl.pallas_call(
        body,
        out_shape=outs,
        scratch_shapes=list(scratch),
        compiler_params=pltpu.CompilerParams(vmem_limit_bytes=VMEM_LIMIT),
        cost_estimate=pl.CostEstimate(
            flops=int(us * 1.1e9), bytes_accessed=int(us * 3.6e6), transcendentals=0
        ),
    )(*args)


def as_row(tiles):
    return jnp.concatenate([tiles[i : i + 1] for i in range(tiles.shape[0])], axis=1)


def folded(row, count, fan):
    return jnp.concatenate([row[:, fan * n : fan * (n + 1)] for n in range(count)], axis=0)


def transposed(values):
    rows, cols = values.shape
    filler = jnp.zeros((rows, 128 - cols), F32)
    return jnp.transpose(jnp.concatenate([values, filler], axis=1))[:cols]


def order_body(send_ref, bond_ref, h_ref, out_ref, h_out_ref):
    owned = bond_ref.shape[0]
    cap = owned // OFFS
    bond = bond_ref[...]
    h_out_ref[...] = h_ref[...]
    send = as_row(send_ref[...])
    low = one_hot(iota((cap, owned), 0) == (send & 127))
    high = send >> 7

    def masked(o):
        mask = jnp.where(high == o, 1.0, 0.0)
        mask = jnp.broadcast_to(mask, (16, owned)).astype(BF16)
        return [low[16 * i : 16 * (i + 1)] * mask for i in range(cap // 16)]

    def step(i, carry):
        start = pl.multiple_of(2 * cap * i, 2 * cap)
        pick = jnp.concatenate(masked(2 * i) + masked(2 * i + 1), axis=0)
        out_ref[pl.ds(start, 2 * cap), :] = dot(pick, bond).astype(BF16)
        return carry

    lax.fori_loop(0, OFFS // 2, step, 0)


def slots_body(nb_ref, kind_ref, recv_ref, dist_ref, adj_ref, pack_ref, rank_ref):
    atoms, fan = pack_ref.shape
    flat = nb_ref[...] | (kind_ref[...] << 11) | (recv_ref[...] << 13)
    pack = folded(as_row(flat), atoms, fan)
    dist = folded(as_row(dist_ref[...]), atoms, fan)
    pack_ref[...] = pack
    peer = (pack & 63).astype(F32)
    off = ((pack & 2047) >> 6).astype(F32)
    scaled = dist * (1.0 / 7.0)
    env = 1.0 - scaled * scaled
    env = jnp.where(((pack >> 11) & 3) > 0, env * env, 0.0)
    lane = fiota((atoms, fan), 1)
    rank = jnp.zeros((atoms, fan), F32)
    for s in range(fan - 1):
        rank += jnp.where((off == off[:, s : s + 1]) & (lane > float(s)), 1.0, 0.0)
    rank_ref[...] = rank
    target = off * float(GROUPS) + rank
    wide = fiota((atoms, 128), 1)
    env_sorted = jnp.zeros((atoms, 128), F32)
    peer_sorted = jnp.zeros((atoms, 128), F32)
    for s in range(fan):
        here = target[:, s : s + 1] == wide
        env_sorted = jnp.where(here, env[:, s : s + 1], env_sorted)
        peer_sorted = jnp.where(here, peer[:, s : s + 1], peer_sorted)
    for m in range(OFFS // 2):
        tile = jnp.zeros((atoms, 128), F32)
        for u in range(2 * GROUPS):
            t = 2 * GROUPS * m + u
            column = peer_sorted[:, t : t + 1] + float(atoms * (u // GROUPS))
            tile += jnp.where(column == wide, env_sorted[:, t : t + 1], 0.0)
        adj_ref[:, 128 * m : 128 * (m + 1)] = tile.astype(BF16)


def write_hots(out_ref, index):
    cap = index.shape[0]
    lane = fiota((cap, 128), 1)
    for o in range(OFFS):
        hot = (lane == index[:, o : o + 1]) | (lane == index[:, 32 + o : 33 + o] + 64.0)
        out_ref[cap * o : cap * (o + 1), :] = one_hot(hot)


def pairs_body(
    send_ref, own_ref, nb_ref, kind_ref, recv_ref, pack_ref, hot_own_ref, hot_mir_ref, place_ref
):
    atoms, fan = pack_ref.shape
    cap = hot_own_ref.shape[0] // OFFS
    send = as_row(send_ref[...])
    own = as_row(own_ref[...]).astype(F32)
    owned = send.shape[1]
    atom_r = jnp.floor((own + 0.5) * (1.0 / fan))
    slot_r = own - fan * atom_r
    off_r = (send >> 7).astype(F32)
    pos_r = (send & 127).astype(F32)
    peer = (pack_ref[...] & 63).astype(F32)
    at_atom = fiota((atoms, owned), 0) == atom_r
    at_slot = fiota((fan, owned), 0) == slot_r
    place_ref[...] = dot_nt(
        jnp.where(at_atom, pos_r + 1.0, 0.0).astype(BF16), one_hot(at_slot)
    )
    peer_all = dot(transposed(peer).astype(BF16), one_hot(at_atom))
    peer_r = jnp.sum(jnp.where(at_slot, peer_all, 0.0), axis=0, keepdims=True)
    at_off = fiota((32, owned), 0) == off_r
    values = jnp.concatenate(
        [jnp.where(at_off, atom_r, 0.0), jnp.where(at_off, peer_r, 0.0)], axis=0
    ).astype(BF16)
    write_hots(hot_own_ref, dot_nt(one_hot(fiota((cap, owned), 0) == pos_r), values))

    ids = as_row(jnp.where(kind_ref[...] == 2, nb_ref[...], 64 * 31))
    slots = ids.shape[1]
    atom_s = jnp.floor((fiota((1, slots), 1) + 0.5) * (1.0 / fan))
    peer_s = (ids & 63).astype(F32)
    off_s = (ids >> 6).astype(F32)
    pos_s = as_row(recv_ref[...] & 127).astype(F32)
    at_off = fiota((32, slots), 0) == off_s
    values = jnp.concatenate(
        [jnp.where(at_off, atom_s, 0.0), jnp.where(at_off, peer_s, 0.0)], axis=0
    ).astype(BF16)
    write_hots(hot_mir_ref, dot_nt(one_hot(fiota((cap, slots), 0) == pos_s), values))


def places_body(pack_ref, rank_ref, place_ref, wb_ref, pick_ref, perm_ref, wcat_ref):
    atoms, fan = pack_ref.shape
    rows = pick_ref.shape[0] // OFFS
    cap = rows // 2
    pack = pack_ref[...]
    off = ((pack & 2047) >> 6).astype(F32)
    kind = (pack >> 11) & 3
    pos_in = ((pack >> 13) & 127).astype(F32)
    rank = rank_ref[...]
    src = jnp.where(kind == 1, place_ref[...], jnp.where(kind == 2, pos_in + (cap + 1.0), 0.0))
    target = off * float(GROUPS) + rank
    wide = fiota((atoms, 128), 1)
    sorted_src = jnp.zeros((atoms, 128), F32)
    for s in range(fan):
        sorted_src = jnp.where(target[:, s : s + 1] == wide, src[:, s : s + 1], sorted_src)
    row = iota((rows, atoms), 0)
    spread = one_hot((row >> 2) == iota((rows, atoms), 1))
    spread = dot(spread, sorted_src.astype(BF16))
    keep = (iota((rows, 128), 1) & 3) == (iota((rows, 128), 0) & 3)
    fold = one_hot((iota((128, 32), 0) >> 2) == iota((128, 32), 1))
    index = dot(jnp.where(keep, spread, 0.0).astype(BF16), fold) - 1.0
    lane = fiota((rows, rows), 1)
    for o in range(OFFS):
        pick_ref[rows * o : rows * (o + 1), :] = one_hot(index[:, o : o + 1] == lane)

    member = (iota((atoms, fan), 0) & 3).astype(F32)
    spot = transposed(off * 16.0 + member * 4.0 + rank)
    lane = fiota((fan, 4 * fan), 1)
    for q in range(atoms // 4):
        perm_ref[4 * fan * q : 4 * fan * (q + 1), :] = jnp.concatenate(
            [jnp.where(spot[:, 4 * q + i : 4 * q + i + 1] == lane, 1.0, 0.0) for i in range(4)],
            axis=0,
        ).astype(BF16)

    block = wb_ref.shape[0]
    row = fiota((block, block), 0)
    col = fiota((block, block), 1)
    major = jnp.floor((row + 0.5) * (1.0 / ORB))
    wcat_ref[:, :128] = wb_ref[...]
    wcat_ref[:, 128:] = dot(
        one_hot((row - ORB * major) * ORB + major == col), wb_ref[...]
    ).astype(BF16)


def node_body(layer):
    def body(adj_ref, other_ref, ghost_ref, wm_ref, wu_ref, gain_ref, out_ref):
        ghosts = ghost_ref.shape[0]
        half = ghosts // 2
        atoms = ghosts // OFFS
        mixed = dot(adj_ref[...], ghost_ref[...])
        other = dot(other_ref[:, :half], ghost_ref[half:, :])
        other += dot(other_ref[:, half:], ghost_ref[:half, :])
        mixed = jnp.concatenate([mixed, other], axis=0).astype(BF16)
        hidden = jnp.concatenate(
            [ghost_ref[atoms * 4 : atoms * 5, :], ghost_ref[atoms * 13 : atoms * 14, :]], axis=0
        )
        summed = (dot(mixed, wm_ref[layer]) * 0.125).astype(BF16)
        updated = hidden.astype(F32) + silu(dot(summed, wu_ref[layer]))
        out_ref[...] = (rms_norm(updated) * gain_ref[layer : layer + 1, :]).astype(BF16)

    return body


CHUNK = 6


def edge_all(e_ref, hot_ref, ghost_ref, w_local, w_ghost, w_in, w_out, table, out_ref):
    atoms = ghost_ref.shape[0] // OFFS
    cap = e_ref.shape[0] // OFFS
    local = dot(ghost_ref[atoms * 4 : atoms * 5, :], w_local).astype(BF16)
    distant = dot(ghost_ref[...], w_ghost).astype(BF16)
    blank = jnp.zeros((atoms, 128), BF16)
    for o in range(OFFS):
        base = 2 * atoms * o
        table[base : base + atoms, :128] = local
        table[base : base + atoms, 128:] = blank
        table[base + atoms : base + 2 * atoms, :128] = blank
        table[base + atoms : base + 2 * atoms, 128:] = distant[atoms * o : atoms * (o + 1)]
    for c in range(OFFS // CHUNK):
        span = slice(CHUNK * cap * c, CHUNK * cap * (c + 1))
        chosen = jnp.concatenate(
            [
                dot(
                    hot_ref[cap * o : cap * (o + 1), :],
                    table[2 * atoms * o : 2 * atoms * (o + 1), :],
                )
                for o in range(CHUNK * c, CHUNK * (c + 1))
            ],
            axis=0,
        )
        state = e_ref[span, :]
        gate = silu(dot(state, w_in) * chosen[:, :128] * chosen[:, 128:]).astype(BF16)
        out_ref[span, :] = rms_norm(state.astype(F32) + dot(gate, w_out)).astype(BF16)


def edge_body(layer):
    def body(e_ref, hot_ref, ghost_ref, wl_ref, wg_ref, wi_ref, wo_ref, out_ref, table):
        edge_all(
            e_ref, hot_ref, ghost_ref, wl_ref[layer], wg_ref[layer], wi_ref[layer], wo_ref[layer],
            table, out_ref,
        )

    return body


def final_body(layer):
    def body(
        own_ref, mir_ref, ho_ref, hm_ref, ghost_ref, wl_ref, wr_ref, wi_ref, wo_ref,
        pick_ref, perm_ref, wcat_ref, out_ref, table_own, table_mir, e_own, e_mir, ranked, rows,
    ):
        atoms = ghost_ref.shape[0] // OFFS
        cap = own_ref.shape[0] // OFFS
        fan = out_ref.shape[1] // atoms
        w_in, w_out = wi_ref[layer], wo_ref[layer]
        edge_all(
            own_ref, ho_ref, ghost_ref, wl_ref[layer], wr_ref[layer], w_in, w_out, table_own, e_own
        )
        edge_all(
            mir_ref, hm_ref, ghost_ref, wr_ref[layer], wl_ref[layer], w_in, w_out, table_mir, e_mir
        )
        for o in range(OFFS):
            span = slice(cap * o, cap * (o + 1))
            wide = slice(2 * cap * o, 2 * cap * (o + 1))
            ranked[wide, :128] = dot(pick_ref[wide, :cap], e_own[span, :]).astype(BF16)
            ranked[wide, 128:] = dot(pick_ref[wide, cap:], e_mir[span, :]).astype(BF16)
        for q in range(atoms // 4):
            span = slice(4 * fan * q, 4 * fan * (q + 1))
            tiles = jnp.concatenate(
                [
                    ranked[2 * cap * o + 16 * q : 2 * cap * o + 16 * (q + 1), :]
                    for o in range(OFFS)
                ],
                axis=0,
            )
            rows[span, :] = dot(perm_ref[span, :], tiles).astype(BF16)
        step = 16 * fan
        for g in range(atoms // 16):
            out_ref[:, step * g : step * (g + 1)] = dot_nt(
                wcat_ref[...], rows[step * g : step * (g + 1), :]
            ).astype(BF16)

    return body


def shards(
    atom_feats, bond_embed, pair_dist, neighbours, slot_kind, own_rows, send_pos, recv_pos,
    w_left, w_right, w_edge_in, w_edge_out, w_msg, w_upd, node_gain, w_block,
):
    atoms, channels = atom_feats.shape
    slots = neighbours.shape[0]
    fan = slots // atoms
    owned = own_rows.shape[0]
    cap = owned // OFFS
    block = w_block.shape[1]
    ghosts = OFFS * atoms

    def array(*shape, dtype=BF16):
        return jax.ShapeDtypeStruct(shape, dtype)

    def tiles(values):
        return values.reshape(-1, 128)

    send, own = tiles(send_pos), tiles(own_rows)
    nb, kind, recv, dist = map(tiles, (neighbours, slot_kind, recv_pos, pair_dist))
    opposite = swapped(atom_feats, "layer")
    ordered, hidden = call(
        order_body,
        (array(owned, channels), array(atoms, channels)),
        send, bond_embed, atom_feats,
        us=3.5,
    )
    adjacency, pack, rank = call(
        slots_body,
        (array(atoms, ghosts), array(atoms, fan, dtype=jnp.int32), array(atoms, fan, dtype=F32)),
        nb, kind, recv, dist,
        us=2.0,
    )
    hot_own, hot_mir, place = call(
        pairs_body,
        (array(owned, 128), array(owned, 128), array(atoms, fan, dtype=F32)),
        send, own, nb, kind, recv, pack,
        us=2.5,
    )
    pick, perm, w_cat = call(
        places_body,
        (array(2 * owned, 2 * cap), array(slots, 4 * fan), array(block, 2 * channels)),
        pack, rank, place, w_block.T,
        us=2.5,
    )
    mirror = deliver(ordered.reshape(2, 3, 3, cap, channels)).reshape(owned, channels)
    other = swapped(adjacency, "layer")
    sheets = jnp.stack([hidden, opposite])
    table = pltpu.VMEM((2 * ghosts, 2 * channels), BF16)
    state = pltpu.VMEM((owned, channels), BF16)
    for layer in range(2):
        ghost = ghosts_of(sheets.reshape(2, 1, 1, atoms, channels))
        sheets = call(
            node_body(layer),
            array(2 * atoms, channels),
            adjacency, other, ghost, w_msg, w_upd, node_gain,
            us=0.6,
        )
        ordered = call(
            edge_body(layer),
            array(owned, channels),
            ordered, hot_own, ghost, w_left, w_right, w_edge_in, w_edge_out,
            scratch=[table],
            us=2.5,
        )
        mirror = call(
            edge_body(layer),
            array(owned, channels),
            mirror, hot_mir, ghost, w_right, w_left, w_edge_in, w_edge_out,
            scratch=[table],
            us=2.5,
        )
    ghost = ghosts_of(sheets.reshape(2, 1, 1, atoms, channels))
    wide = pltpu.VMEM((slots, 2 * channels), BF16)
    return call(
        final_body(2),
        array(block, slots),
        ordered, mirror, hot_own, hot_mir, ghost, w_left, w_right, w_edge_in, w_edge_out,
        pick, perm, w_cat,
        scratch=[table, table, state, state, wide, wide],
        us=8.0,
    )


def solution(mesh):
    axes = ("gx", "gy", "layer")
    rows = P(axes, None)
    flat = P(axes)
    placed = (rows, rows) + (flat,) * 6 + (P(),) * 8
    return jax.shard_map(
        shards,
        mesh=mesh,
        in_specs=placed,
        out_specs=P(None, axes),
        check_vma=False,
    )
```

```python
import jax
import jax.numpy as jnp
from jax import lax
from jax.experimental import pallas as pl
from jax.experimental.pallas import tpu as pltpu
from jax.sharding import PartitionSpec as P

ORB = 13
GROUPS = 4
OFFS = 18
F32 = jnp.float32
BF16 = jnp.bfloat16
VMEM_LIMIT = 24 * 1024 * 1024


def swapped(value, axis):
    return lax.ppermute(value, axis, [(0, 1), (1, 0)])


def moved(value, axis, steps):
    count = lax.axis_size(axis)
    return lax.ppermute(value, axis, [(i, (i + steps) % count) for i in range(count)])


def with_halo(block, axis, dim):
    low = moved(block, axis, 1)
    high = moved(block, axis, -1)
    return jnp.concatenate([low, block, high], axis=dim)


def ghosts_of(sheets, centre=None):
    low, high = moved(sheets, "gx", 1), moved(sheets, "gx", -1)
    centre = sheets if centre is None else centre
    framed = with_halo(jnp.concatenate([low, centre, high], axis=1), "gy", 2)
    return framed.reshape(-1, sheets.shape[-1])


def across_rows(outgoing, crossed):
    sheets = jnp.stack([outgoing[0], crossed])
    rows = [moved(sheets[:, i], "gx", i - 1) if i != 1 else sheets[:, i] for i in (2, 1, 0)]
    return jnp.stack(rows, axis=1)


def across_columns(shifted):
    cols = [moved(shifted[:, :, i], "gy", i - 1) if i != 1 else shifted[:, :, i] for i in (2, 1, 0)]
    return jnp.stack(cols, axis=2)


def dot(a, b):
    return jnp.dot(a, b, preferred_element_type=F32)


def dot_nt(a, b):
    return lax.dot_general(a, b, (((1,), (1,)), ((), ())), preferred_element_type=F32)


def one_hot(mask):
    return jnp.where(mask, 1.0, 0.0).astype(BF16)


def silu(v):
    return v * (0.5 * jnp.tanh(0.5 * v) + 0.5)


def rms_norm(v):
    return v * lax.rsqrt(jnp.mean(v * v, axis=-1, keepdims=True) + 1e-06)


def iota(shape, dim):
    return lax.broadcasted_iota(jnp.int32, shape, dim)


def fiota(shape, dim):
    return iota(shape, dim).astype(F32)


def call(body, outs, *args, after=(), scratch=(), us=1.0):
    used = len(args)

    def ordered_body(*refs):
        body(*refs[:used], *refs[used + len(after) :])

    return pl.pallas_call(
        ordered_body if after else body,
        out_shape=outs,
        in_specs=[pl.BlockSpec(memory_space=pltpu.VMEM)] * used
        + [pl.BlockSpec(memory_space=pl.ANY)] * len(after),
        scratch_shapes=list(scratch),
        compiler_params=pltpu.CompilerParams(vmem_limit_bytes=VMEM_LIMIT),
        cost_estimate=pl.CostEstimate(
            flops=int(us * 1.1e9), bytes_accessed=int(us * 3.6e6), transcendentals=0
        ),
    )(*args, *after)


def as_row(tiles):
    return jnp.concatenate([tiles[i : i + 1] for i in range(tiles.shape[0])], axis=1)


def folded(row, count, fan):
    return jnp.concatenate([row[:, fan * n : fan * (n + 1)] for n in range(count)], axis=0)


def transposed(values):
    rows, cols = values.shape
    filler = jnp.zeros((rows, 128 - cols), F32)
    return jnp.transpose(jnp.concatenate([values, filler], axis=1))[:cols]


def order_body(send_ref, bond_ref, h_ref, out_ref, h_out_ref):
    owned = bond_ref.shape[0]
    half = owned // 2
    cap = owned // OFFS
    h_out_ref[...] = h_ref[...]
    bond = jnp.concatenate([bond_ref[:half, :], bond_ref[half:, :]], axis=1)
    send = as_row(send_ref[...])
    low = one_hot(iota((cap, owned), 0) == (send & 127))
    high = send >> 7
    late = iota((32, owned), 1) >= half
    late = dot_nt(low, one_hot((iota((32, owned), 0) == high) & late))

    def masked(o):
        mask = jnp.where(high == o, 1.0, 0.0)
        mask = jnp.broadcast_to(mask, (16, owned)).astype(BF16)
        kept = [low[16 * i : 16 * (i + 1)] * mask for i in range(cap // 16)]
        return [k[:, :half] + k[:, half:] for k in kept]

    for i in range(OFFS // 2):
        both = dot(jnp.concatenate(masked(2 * i) + masked(2 * i + 1), axis=0), bond)
        column = jnp.concatenate([late[:, 2 * i : 2 * i + 1], late[:, 2 * i + 1 : 2 * i + 2]], axis=0)
        out_ref[2 * cap * i : 2 * cap * (i + 1), :] = jnp.where(
            column > 0.5, both[:, 128:], both[:, :128]
        ).astype(BF16)


def slots_body(nb_ref, kind_ref, recv_ref, dist_ref, h_ref, adj_ref, pack_ref, h_out_ref):
    fan, atoms = pack_ref.shape
    h_out_ref[...] = h_ref[...]
    flat = nb_ref[...] | (kind_ref[...] << 11) | ((recv_ref[...] & 127) << 13)
    pack = transposed(folded(as_row(flat.astype(F32)), atoms, fan)).astype(jnp.int32)
    dist = transposed(folded(as_row(dist_ref[...]), atoms, fan))
    pack_ref[...] = pack
    peer = (pack & 63).astype(F32)
    off = ((pack & 2047) >> 6).astype(F32)
    scaled = dist * (1.0 / 7.0)
    env = 1.0 - scaled * scaled
    env = jnp.where(((pack >> 11) & 3) > 0, env * env, 0.0)
    row = fiota((fan, atoms), 0)
    target = off * float(GROUPS) + ranked_among(off)
    env_sorted = jnp.zeros((fan, atoms), F32)
    peer_sorted = jnp.zeros((fan, atoms), F32)
    for s in range(fan):
        here = target[s : s + 1, :] == row
        env_sorted = jnp.where(here, env[s : s + 1, :], env_sorted)
        peer_sorted = jnp.where(here, peer[s : s + 1, :], peer_sorted)
    which = fiota((atoms, atoms), 0)
    parts = []
    for o in range(OFFS):
        part = jnp.zeros((atoms, atoms), F32)
        for t in range(GROUPS * o, GROUPS * (o + 1)):
            part += jnp.where(peer_sorted[t : t + 1, :] == which, env_sorted[t : t + 1, :], 0.0)
        parts.append(part)
    for m in range(OFFS // 2):
        pair = jnp.concatenate([parts[2 * m], parts[2 * m + 1]], axis=0)
        pair = jnp.concatenate([pair, jnp.zeros_like(pair)], axis=1)
        adj_ref[:, 128 * m : 128 * (m + 1)] = jnp.transpose(pair)[:atoms].astype(BF16)


def ranked_among(key):
    fan = key.shape[0]
    row = fiota(key.shape, 0)
    rank = jnp.zeros(key.shape, F32)
    for s in range(fan - 1):
        rank += jnp.where((key == key[s : s + 1, :]) & (row > float(s)), 1.0, 0.0)
    return rank


def write_hots(out_ref, index):
    cap = index.shape[0]
    lane = fiota((cap, 128), 1)
    for o in range(OFFS):
        hot = (lane == index[:, o : o + 1]) | (lane == index[:, 32 + o : 33 + o] + 64.0)
        out_ref[cap * o : cap * (o + 1), :] = one_hot(hot)


def pairs_body(
    send_ref, own_ref, nb_ref, kind_ref, recv_ref, pack_ref, hot_own_ref, hot_mir_ref, place_ref
):
    fan, atoms = pack_ref.shape
    cap = hot_own_ref.shape[0] // OFFS
    send = as_row(send_ref[...])
    own = as_row(own_ref[...]).astype(F32)
    owned = send.shape[1]
    atom_r = jnp.floor((own + 0.5) * (1.0 / fan))
    slot_r = own - fan * atom_r
    off_r = (send >> 7).astype(F32)
    pos_r = (send & 127).astype(F32)
    peer = (pack_ref[...] & 63).astype(F32)
    at_atom = fiota((atoms, owned), 0) == atom_r
    at_slot = fiota((fan, owned), 0) == slot_r
    place_ref[...] = dot_nt(
        one_hot(at_slot), jnp.where(at_atom, pos_r + 1.0, 0.0).astype(BF16)
    )
    peer_all = dot(peer.astype(BF16), one_hot(at_atom))
    peer_r = jnp.sum(jnp.where(at_slot, peer_all, 0.0), axis=0, keepdims=True)
    at_off = fiota((32, owned), 0) == off_r
    values = jnp.concatenate(
        [jnp.where(at_off, atom_r, 0.0), jnp.where(at_off, peer_r, 0.0)], axis=0
    ).astype(BF16)
    write_hots(hot_own_ref, dot_nt(one_hot(fiota((cap, owned), 0) == pos_r), values))

    ids = as_row(jnp.where(kind_ref[...] == 2, nb_ref[...], 64 * 31))
    slots = ids.shape[1]
    atom_s = jnp.floor((fiota((1, slots), 1) + 0.5) * (1.0 / fan))
    peer_s = (ids & 63).astype(F32)
    off_s = (ids >> 6).astype(F32)
    pos_s = as_row(recv_ref[...] & 127).astype(F32)
    at_off = fiota((32, slots), 0) == off_s
    values = jnp.concatenate(
        [jnp.where(at_off, atom_s, 0.0), jnp.where(at_off, peer_s, 0.0)], axis=0
    ).astype(BF16)
    write_hots(hot_mir_ref, dot_nt(one_hot(fiota((cap, slots), 0) == pos_s), values))


def places_body(
    pack_ref, place_ref, wb_ref, pick_own_ref, pick_mir_ref, perm_ref, owned_ref, wcat_ref
):
    fan, atoms = pack_ref.shape
    cap = pick_own_ref.shape[0] // OFFS
    pack = pack_ref[...]
    off = ((pack & 2047) >> 6).astype(F32)
    kind = (pack >> 11) & 3
    pos_in = (pack >> 13).astype(F32)
    place = place_ref[...]
    owned = jnp.where(place > 0.5, 1.0, 0.0)
    owned_ref[...] = owned
    src = jnp.where(kind == 1, place, jnp.where(kind == 2, pos_in + 1.0, 0.0))
    rank = ranked_among(off * 2.0 + owned)
    target = off * float(GROUPS) + (2.0 - 2.0 * owned) + rank
    row = fiota((fan, atoms), 0)
    sorted_src = jnp.zeros((fan, atoms), F32)
    for s in range(fan):
        sorted_src = jnp.where(target[s : s + 1, :] == row, src[s : s + 1, :], sorted_src)
    spread = one_hot((iota((cap, atoms), 0) >> 1) == iota((cap, atoms), 1))
    spread = dot_nt(spread, sorted_src.astype(BF16))
    member = iota((cap, fan), 1) & 3
    parity = iota((cap, fan), 0) & 1
    fold = one_hot((iota((fan, 32), 0) >> 2) == iota((fan, 32), 1))
    lane = fiota((cap, cap), 1)
    for shift, pick_ref in ((0, pick_own_ref), (2, pick_mir_ref)):
        kept = jnp.where(member == parity + shift, spread, 0.0).astype(BF16)
        index = dot(kept, fold) - 1.0
        for o in range(OFFS):
            pick_ref[cap * o : cap * (o + 1), :] = one_hot(index[:, o : o + 1] == lane)

    spot = off * 8.0 + (iota((fan, atoms), 1) & 3).astype(F32) * 2.0 + rank
    lane = fiota((fan, 2 * fan), 1)
    for q in range(atoms // 4):
        perm_ref[4 * fan * q : 4 * fan * (q + 1), :] = jnp.concatenate(
            [jnp.where(spot[:, 4 * q + i : 4 * q + i + 1] == lane, 1.0, 0.0) for i in range(4)],
            axis=0,
        ).astype(BF16)

    block = wb_ref.shape[0]
    row = fiota((block, block), 0)
    col = fiota((block, block), 1)
    major = jnp.floor((row + 0.5) * (1.0 / ORB))
    wcat_ref[:, :128] = wb_ref[...]
    wcat_ref[:, 128:] = dot(
        one_hot((row - ORB * major) * ORB + major == col), wb_ref[...]
    ).astype(BF16)


def node_body(layer):
    def body(adj_ref, other_ref, ghost_ref, wm_ref, wu_ref, gain_ref, out_ref):
        ghosts = ghost_ref.shape[0]
        half = ghosts // 2
        atoms = ghosts // OFFS
        mixed = dot(adj_ref[...], ghost_ref[...])
        other = dot(other_ref[:, :half], ghost_ref[half:, :])
        other += dot(other_ref[:, half:], ghost_ref[:half, :])
        mixed = jnp.concatenate([mixed, other], axis=0).astype(BF16)
        hidden = jnp.concatenate(
            [ghost_ref[atoms * 4 : atoms * 5, :], ghost_ref[atoms * 13 : atoms * 14, :]], axis=0
        )
        summed = (dot(mixed, wm_ref[layer]) * 0.125).astype(BF16)
        updated = hidden.astype(F32) + silu(dot(summed, wu_ref[layer]))
        out_ref[...] = (rms_norm(updated) * gain_ref[layer : layer + 1, :]).astype(BF16)

    return body


CHUNK = 6


def fill_table(ghost_ref, w_local, w_ghost, table):
    atoms = ghost_ref.shape[0] // OFFS
    local = dot(ghost_ref[atoms * 4 : atoms * 5, :], w_local).astype(BF16)
    distant = dot(ghost_ref[...], w_ghost).astype(BF16)
    blank = jnp.zeros((atoms, 128), BF16)
    for o in range(OFFS):
        base = 2 * atoms * o
        table[base : base + atoms, :128] = local
        table[base : base + atoms, 128:] = blank
        table[base + atoms : base + 2 * atoms, :128] = blank
        table[base + atoms : base + 2 * atoms, 128:] = distant[atoms * o : atoms * (o + 1)]


def chosen_product(hot_ref, table, c):
    cap = hot_ref.shape[0] // OFFS
    chosen = jnp.concatenate(
        [
            dot(hot_ref[cap * o : cap * (o + 1), :], table[cap * o : cap * (o + 1), :])
            for o in range(CHUNK * c, CHUNK * (c + 1))
        ],
        axis=0,
    )
    return chosen[:, :128] * chosen[:, 128:]


def edge_all(e_ref, hot_ref, ghost_ref, w_local, w_ghost, w_in, w_out, table, out_ref):
    cap = e_ref.shape[0] // OFFS
    fill_table(ghost_ref, w_local, w_ghost, table)
    for c in range(OFFS // CHUNK):
        span = slice(CHUNK * cap * c, CHUNK * cap * (c + 1))
        state = e_ref[span, :]
        gate = silu(dot(state, w_in) * chosen_product(hot_ref, table, c)).astype(BF16)
        out_ref[span, :] = rms_norm(state.astype(F32) + dot(gate, w_out)).astype(BF16)


def edge_body(layer):
    def body(e_ref, hot_ref, ghost_ref, wl_ref, wg_ref, wi_ref, wo_ref, out_ref, table):
        edge_all(
            e_ref, hot_ref, ghost_ref, wl_ref[layer], wg_ref[layer], wi_ref[layer], wo_ref[layer],
            table, out_ref,
        )

    return body


def twice(weight):
    blank = jnp.zeros_like(weight)
    return jnp.concatenate(
        [
            jnp.concatenate([weight, blank], axis=1),
            jnp.concatenate([blank, weight], axis=1),
        ],
        axis=0,
    )


def final_body(layer):
    def body(
        own_ref, mir_ref, ho_ref, hm_ref, ghost_ref, wl_ref, wr_ref, wi_ref, wo_ref,
        po_ref, pm_ref, perm_ref, owned_ref, wcat_ref,
        out_ref, table_own, table_mir, ranked, rows,
    ):
        atoms = ghost_ref.shape[0] // OFFS
        cap = own_ref.shape[0] // OFFS
        fan = out_ref.shape[1] // atoms
        w_in, w_out = twice(wi_ref[layer]), twice(wo_ref[layer])
        fill_table(ghost_ref, wl_ref[layer], wr_ref[layer], table_own)
        fill_table(ghost_ref, wr_ref[layer], wl_ref[layer], table_mir)
        for c in range(OFFS // CHUNK):
            span = slice(CHUNK * cap * c, CHUNK * cap * (c + 1))
            state = jnp.concatenate([own_ref[span, :], mir_ref[span, :]], axis=1)
            chosen = jnp.concatenate(
                [chosen_product(ho_ref, table_own, c), chosen_product(hm_ref, table_mir, c)],
                axis=1,
            )
            gate = silu(dot(state, w_in) * chosen).astype(BF16)
            renewed = state.astype(F32) + dot(gate, w_out)
            e_own = rms_norm(renewed[:, :128]).astype(BF16)
            e_mir = rms_norm(renewed[:, 128:]).astype(BF16)
            for i in range(CHUNK):
                o = CHUNK * c + i
                here = slice(cap * i, cap * (i + 1))
                span = slice(cap * o, cap * (o + 1))
                ranked[span, :128] = dot(po_ref[span, :], e_own[here])
                ranked[span, 128:] = dot(pm_ref[span, :], e_mir[here])
        for q in range(atoms // 4):
            span = slice(4 * fan * q, 4 * fan * (q + 1))
            tiles = jnp.concatenate(
                [ranked[cap * o + 8 * q : cap * o + 8 * (q + 1), :] for o in range(OFFS)], axis=0
            ).astype(BF16)
            spread = dot(perm_ref[span, :], tiles)
            mine = jnp.concatenate(
                [owned_ref[:, 4 * q + i : 4 * q + i + 1] for i in range(4)], axis=0
            )
            mine = mine > 0.5
            rows[span, :128] = jnp.where(mine, spread[:, :128], 0.0).astype(BF16)
            rows[span, 128:] = jnp.where(mine, 0.0, spread[:, 128:]).astype(BF16)
        step = 16 * fan
        for g in range(atoms // 16):
            out_ref[:, step * g : step * (g + 1)] = dot_nt(
                wcat_ref[...], rows[step * g : step * (g + 1), :]
            ).astype(BF16)

    return body


def shards(
    atom_feats, bond_embed, pair_dist, neighbours, slot_kind, own_rows, send_pos, recv_pos,
    w_left, w_right, w_edge_in, w_edge_out, w_msg, w_upd, node_gain, w_block,
):
    atoms, channels = atom_feats.shape
    slots = neighbours.shape[0]
    fan = slots // atoms
    owned = own_rows.shape[0]
    cap = owned // OFFS
    block = w_block.shape[1]
    ghosts = OFFS * atoms

    def array(*shape, dtype=BF16):
        return jax.ShapeDtypeStruct(shape, dtype)

    def tiles(values):
        return values.reshape(-1, 128)

    send, own = tiles(send_pos), tiles(own_rows)
    nb, kind, recv, dist = map(tiles, (neighbours, slot_kind, recv_pos, pair_dist))
    opposite = swapped(atom_feats, "layer")
    adjacency, pack, hidden = call(
        slots_body,
        (array(atoms, ghosts), array(fan, atoms, dtype=jnp.int32), array(atoms, channels)),
        nb, kind, recv, dist, atom_feats,
        us=3.0,
    )
    other = swapped(adjacency, "layer")
    sheets = jnp.concatenate([hidden, opposite], axis=0)
    ordered, centre = call(
        order_body,
        (array(owned, channels), array(2 * atoms, channels)),
        send, bond_embed, sheets,
        us=3.5,
    )
    outgoing = ordered.reshape(2, 3, 3, cap, channels)
    crossed = swapped(outgoing[1], "layer")
    shifted = across_rows(outgoing, crossed)
    mirror = across_columns(shifted).reshape(owned, channels)
    hot_own, hot_mir, place = call(
        pairs_body,
        (array(owned, 128), array(owned, 128), array(fan, atoms, dtype=F32)),
        send, own, nb, kind, recv, pack,
        us=2.5,
    )
    pick_own, pick_mir, perm, mine, w_cat = call(
        places_body,
        (
            array(owned, cap),
            array(owned, cap),
            array(slots, 2 * fan),
            array(fan, atoms, dtype=F32),
            array(block, 2 * channels),
        ),
        pack, place, w_block.T,
        us=2.5,
    )
    centre = centre.reshape(2, 1, 1, atoms, channels)
    table = pltpu.VMEM((2 * ghosts, 2 * channels), BF16)
    for layer in range(2):
        ghost = ghosts_of(sheets.reshape(2, 1, 1, atoms, channels), centre)
        centre = None
        sheets = call(
            node_body(layer),
            array(2 * atoms, channels),
            adjacency, other, ghost, w_msg, w_upd, node_gain,
            after=(shifted, perm) if layer else (crossed,),
            us=0.6,
        )
        ordered = call(
            edge_body(layer),
            array(owned, channels),
            ordered, hot_own, ghost, w_left, w_right, w_edge_in, w_edge_out,
            scratch=[table],
            us=1.4,
        )
        mirror = call(
            edge_body(layer),
            array(owned, channels),
            mirror, hot_mir, ghost, w_right, w_left, w_edge_in, w_edge_out,
            scratch=[table],
            us=1.4,
        )
    ghost = ghosts_of(sheets.reshape(2, 1, 1, atoms, channels))
    return call(
        final_body(2),
        array(block, slots),
        ordered, mirror, hot_own, hot_mir, ghost, w_left, w_right, w_edge_in, w_edge_out,
        pick_own, pick_mir, perm, mine, w_cat,
        scratch=[
            table,
            table,
            pltpu.VMEM((owned, 2 * channels), F32),
            pltpu.VMEM((slots, 2 * channels), BF16),
        ],
        us=7.0,
    )


def solution(mesh):
    axes = ("gx", "gy", "layer")
    rows = P(axes, None)
    flat = P(axes)
    placed = (rows, rows) + (flat,) * 6 + (P(),) * 8
    return jax.shard_map(
        shards,
        mesh=mesh,
        in_specs=placed,
        out_specs=P(None, axes),
        check_vma=False,
    )
```

```python
import jax
import jax.numpy as jnp
from jax import lax
from jax.experimental import pallas as pl
from jax.experimental.pallas import tpu as pltpu
from jax.sharding import PartitionSpec as P

ORB = 13
GROUPS = 4
OFFS = 18
F32 = jnp.float32
BF16 = jnp.bfloat16
VMEM_LIMIT = 24 * 1024 * 1024


def swapped(value, axis):
    return lax.ppermute(value, axis, [(0, 1), (1, 0)])


def moved(value, row_step, col_step):
    rows, cols = lax.axis_size("gx"), lax.axis_size("gy")
    pairs = [
        (x * cols + y, (x + row_step) % rows * cols + (y + col_step) % cols)
        for x in range(rows)
        for y in range(cols)
    ]
    return lax.ppermute(value, ("gx", "gy"), pairs)


STEPS = [(1, 1), (1, -1), (-1, 1), (-1, -1), (1, 0), (-1, 0), (0, 1), (0, -1)]


def framed(pieces, centre):
    pieces = {**pieces, (0, 0): centre}
    return jnp.stack(
        [jnp.stack([pieces[(i, j)] for j in (1, 0, -1)], axis=1) for i in (1, 0, -1)], axis=1
    )


def ghosts_of(sheets, centre=None):
    pieces = {step: moved(sheets, *step) for step in STEPS}
    centre = sheets if centre is None else centre
    apart = {step: p.reshape(2, -1, p.shape[1]) for step, p in pieces.items()}
    table = framed(apart, centre.reshape(2, -1, centre.shape[1]))
    return table.reshape(-1, sheets.shape[1])


def deliver(outgoing, crossed):
    sheets = jnp.stack([outgoing[0], crossed])
    pieces = {(i, j): moved(sheets[:, i + 1, j + 1], i, j) for i, j in STEPS}
    return framed(pieces, sheets[:, 1, 1])


def dot(a, b):
    return jnp.dot(a, b, preferred_element_type=F32)


def dot_nt(a, b):
    return lax.dot_general(a, b, (((1,), (1,)), ((), ())), preferred_element_type=F32)


def one_hot(mask):
    return jnp.where(mask, 1.0, 0.0).astype(BF16)


def silu(v):
    return v * (0.5 * jnp.tanh(0.5 * v) + 0.5)


def rms_norm(v):
    return v * lax.rsqrt(jnp.mean(v * v, axis=-1, keepdims=True) + 1e-06)


def iota(shape, dim):
    return lax.broadcasted_iota(jnp.int32, shape, dim)


def fiota(shape, dim):
    return iota(shape, dim).astype(F32)


def call(body, outs, *args, after=(), space=pltpu.VMEM, scratch=(), us=1.0):
    used = len(args)

    def ordered_body(*refs):
        body(*refs[:used], *refs[used + len(after) :])

    return pl.pallas_call(
        ordered_body if after else body,
        out_shape=outs,
        in_specs=[pl.BlockSpec(memory_space=space)] * used
        + [pl.BlockSpec(memory_space=pl.ANY)] * len(after),
        scratch_shapes=list(scratch),
        compiler_params=pltpu.CompilerParams(vmem_limit_bytes=VMEM_LIMIT),
        cost_estimate=pl.CostEstimate(
            flops=int(us * 1.1e9), bytes_accessed=int(us * 3.6e6), transcendentals=0
        ),
    )(*args, *after)


def as_row(tiles):
    return jnp.concatenate([tiles[i : i + 1] for i in range(tiles.shape[0])], axis=1)


def folded(row, count, fan):
    return jnp.concatenate([row[:, fan * n : fan * (n + 1)] for n in range(count)], axis=0)


def transposed(values):
    rows, cols = values.shape
    filler = jnp.zeros((rows, 128 - cols), F32)
    return jnp.transpose(jnp.concatenate([values, filler], axis=1))[:cols]


def order_body(send_ref, bond_ref, h_ref, out_ref, h_out_ref):
    owned = bond_ref.shape[0]
    half = owned // 2
    cap = owned // OFFS
    h_out_ref[...] = h_ref[...]
    bond = jnp.concatenate([bond_ref[:half, :], bond_ref[half:, :]], axis=1)
    send = as_row(send_ref[...])
    low = one_hot(iota((cap, owned), 0) == (send & 127))
    high = send >> 7
    late = iota((32, owned), 1) >= half
    late = dot_nt(low, one_hot((iota((32, owned), 0) == high) & late))

    def masked(o):
        mask = jnp.where(high == o, 1.0, 0.0)
        mask = jnp.broadcast_to(mask, (16, owned)).astype(BF16)
        kept = [low[16 * i : 16 * (i + 1)] * mask for i in range(cap // 16)]
        return [k[:, :half] + k[:, half:] for k in kept]

    for i in range(OFFS // 2):
        both = dot(jnp.concatenate(masked(2 * i) + masked(2 * i + 1), axis=0), bond)
        column = jnp.concatenate([late[:, 2 * i : 2 * i + 1], late[:, 2 * i + 1 : 2 * i + 2]], axis=0)
        out_ref[2 * cap * i : 2 * cap * (i + 1), :] = jnp.where(
            column > 0.5, both[:, 128:], both[:, :128]
        ).astype(BF16)


def slots_body(both_ref, adj_ref, pack_ref):
    fan, atoms = pack_ref.shape
    half = both_ref.shape[0] // 2
    pack = transposed(folded(as_row(both_ref[:half, :]), atoms, fan)).astype(jnp.int32)
    dist = transposed(folded(as_row(both_ref[half:, :]), atoms, fan))
    pack_ref[...] = pack
    peer = (pack & 63).astype(F32)
    off = ((pack & 2047) >> 6).astype(F32)
    scaled = dist * (1.0 / 7.0)
    env = 1.0 - scaled * scaled
    env = jnp.where(((pack >> 11) & 3) > 0, env * env, 0.0)
    row = fiota((fan, atoms), 0)
    target = off * float(GROUPS) + ranked_among(off)
    env_sorted = jnp.zeros((fan, atoms), F32)
    peer_sorted = jnp.zeros((fan, atoms), F32)
    for s in range(fan):
        here = target[s : s + 1, :] == row
        env_sorted = jnp.where(here, env[s : s + 1, :], env_sorted)
        peer_sorted = jnp.where(here, peer[s : s + 1, :], peer_sorted)
    which = fiota((atoms, atoms), 0)
    parts = []
    for o in range(OFFS):
        part = jnp.zeros((atoms, atoms), F32)
        for t in range(GROUPS * o, GROUPS * (o + 1)):
            part += jnp.where(peer_sorted[t : t + 1, :] == which, env_sorted[t : t + 1, :], 0.0)
        parts.append(part)
    for m in range(OFFS // 2):
        pair = jnp.concatenate([parts[2 * m], parts[2 * m + 1]], axis=0)
        pair = jnp.concatenate([pair, jnp.zeros_like(pair)], axis=1)
        adj_ref[:, 128 * m : 128 * (m + 1)] = jnp.transpose(pair)[:atoms].astype(BF16)


def ranked_among(key):
    fan = key.shape[0]
    row = fiota(key.shape, 0)
    rank = jnp.zeros(key.shape, F32)
    for s in range(fan - 1):
        rank += jnp.where((key == key[s : s + 1, :]) & (row > float(s)), 1.0, 0.0)
    return rank


def write_hots(out_ref, index):
    cap = index.shape[0]
    lane = fiota((cap, 128), 1)
    for o in range(OFFS):
        hot = (lane == index[:, o : o + 1]) | (lane == index[:, 32 + o : 33 + o] + 64.0)
        out_ref[cap * o : cap * (o + 1), :] = one_hot(hot)


def pairs_body(
    send_ref, own_ref, nb_ref, kind_ref, recv_ref, pack_ref, hot_own_ref, hot_mir_ref, place_ref
):
    fan, atoms = pack_ref.shape
    cap = hot_own_ref.shape[0] // OFFS
    send = as_row(send_ref[...])
    own = as_row(own_ref[...]).astype(F32)
    owned = send.shape[1]
    atom_r = jnp.floor((own + 0.5) * (1.0 / fan))
    slot_r = own - fan * atom_r
    off_r = (send >> 7).astype(F32)
    pos_r = (send & 127).astype(F32)
    peer = (pack_ref[...] & 63).astype(F32)
    at_atom = fiota((atoms, owned), 0) == atom_r
    at_slot = fiota((fan, owned), 0) == slot_r
    place_ref[...] = dot_nt(
        one_hot(at_slot), jnp.where(at_atom, pos_r + 1.0, 0.0).astype(BF16)
    )
    peer_all = dot(peer.astype(BF16), one_hot(at_atom))
    peer_r = jnp.sum(jnp.where(at_slot, peer_all, 0.0), axis=0, keepdims=True)
    at_off = fiota((32, owned), 0) == off_r
    values = jnp.concatenate(
        [jnp.where(at_off, atom_r, 0.0), jnp.where(at_off, peer_r, 0.0)], axis=0
    ).astype(BF16)
    write_hots(hot_own_ref, dot_nt(one_hot(fiota((cap, owned), 0) == pos_r), values))

    ids = as_row(jnp.where(kind_ref[...] == 2, nb_ref[...], 64 * 31))
    slots = ids.shape[1]
    atom_s = jnp.floor((fiota((1, slots), 1) + 0.5) * (1.0 / fan))
    peer_s = (ids & 63).astype(F32)
    off_s = (ids >> 6).astype(F32)
    pos_s = as_row(recv_ref[...] & 127).astype(F32)
    at_off = fiota((32, slots), 0) == off_s
    values = jnp.concatenate(
        [jnp.where(at_off, atom_s, 0.0), jnp.where(at_off, peer_s, 0.0)], axis=0
    ).astype(BF16)
    write_hots(hot_mir_ref, dot_nt(one_hot(fiota((cap, slots), 0) == pos_s), values))


def places_body(
    pack_ref, place_ref, wb_ref, pick_own_ref, pick_mir_ref, perm_ref, owned_ref, wcat_ref
):
    fan, atoms = pack_ref.shape
    cap = pick_own_ref.shape[0] // OFFS
    pack = pack_ref[...]
    off = ((pack & 2047) >> 6).astype(F32)
    kind = (pack >> 11) & 3
    pos_in = (pack >> 13).astype(F32)
    place = place_ref[...]
    owned = jnp.where(place > 0.5, 1.0, 0.0)
    owned_ref[...] = owned
    src = jnp.where(kind == 1, place, jnp.where(kind == 2, pos_in + 1.0, 0.0))
    rank = ranked_among(off * 2.0 + owned)
    target = off * float(GROUPS) + (2.0 - 2.0 * owned) + rank
    row = fiota((fan, atoms), 0)
    sorted_src = jnp.zeros((fan, atoms), F32)
    for s in range(fan):
        sorted_src = jnp.where(target[s : s + 1, :] == row, src[s : s + 1, :], sorted_src)
    spread = one_hot((iota((cap, atoms), 0) >> 1) == iota((cap, atoms), 1))
    spread = dot_nt(spread, sorted_src.astype(BF16))
    member = iota((cap, fan), 1) & 3
    parity = iota((cap, fan), 0) & 1
    fold = one_hot((iota((fan, 32), 0) >> 2) == iota((fan, 32), 1))
    lane = fiota((cap, cap), 1)
    for shift, pick_ref in ((0, pick_own_ref), (2, pick_mir_ref)):
        kept = jnp.where(member == parity + shift, spread, 0.0).astype(BF16)
        index = dot(kept, fold) - 1.0
        for o in range(OFFS):
            pick_ref[cap * o : cap * (o + 1), :] = one_hot(index[:, o : o + 1] == lane)

    spot = off * 8.0 + (iota((fan, atoms), 1) & 3).astype(F32) * 2.0 + rank
    lane = fiota((fan, 2 * fan), 1)
    for q in range(atoms // 4):
        perm_ref[4 * fan * q : 4 * fan * (q + 1), :] = jnp.concatenate(
            [jnp.where(spot[:, 4 * q + i : 4 * q + i + 1] == lane, 1.0, 0.0) for i in range(4)],
            axis=0,
        ).astype(BF16)

    block = wb_ref.shape[0]
    row = fiota((block, block), 0)
    col = fiota((block, block), 1)
    major = jnp.floor((row + 0.5) * (1.0 / ORB))
    wcat_ref[:, :128] = wb_ref[...]
    wcat_ref[:, 128:] = dot(
        one_hot((row - ORB * major) * ORB + major == col), wb_ref[...]
    ).astype(BF16)


def node_body(layer):
    def body(adj_ref, other_ref, ghost_ref, wm_ref, wu_ref, gain_ref, out_ref):
        ghosts = ghost_ref.shape[0]
        half = ghosts // 2
        atoms = ghosts // OFFS
        mixed = dot(adj_ref[...], ghost_ref[...])
        other = dot(other_ref[:, :half], ghost_ref[half:, :])
        other += dot(other_ref[:, half:], ghost_ref[:half, :])
        mixed = jnp.concatenate([mixed, other], axis=0).astype(BF16)
        hidden = jnp.concatenate(
            [ghost_ref[atoms * 4 : atoms * 5, :], ghost_ref[atoms * 13 : atoms * 14, :]], axis=0
        )
        summed = (dot(mixed, wm_ref[layer]) * 0.125).astype(BF16)
        updated = hidden.astype(F32) + silu(dot(summed, wu_ref[layer]))
        out_ref[...] = (rms_norm(updated) * gain_ref[layer : layer + 1, :]).astype(BF16)

    return body


CHUNK = 6


def fill_table(ghost_ref, w_local, w_ghost, table):
    atoms = ghost_ref.shape[0] // OFFS
    local = dot(ghost_ref[atoms * 4 : atoms * 5, :], w_local).astype(BF16)
    distant = dot(ghost_ref[...], w_ghost).astype(BF16)
    blank = jnp.zeros((atoms, 128), BF16)
    for o in range(OFFS):
        base = 2 * atoms * o
        table[base : base + atoms, :128] = local
        table[base : base + atoms, 128:] = blank
        table[base + atoms : base + 2 * atoms, :128] = blank
        table[base + atoms : base + 2 * atoms, 128:] = distant[atoms * o : atoms * (o + 1)]


def chosen_product(hot_ref, table, c):
    cap = hot_ref.shape[0] // OFFS
    chosen = jnp.concatenate(
        [
            dot(hot_ref[cap * o : cap * (o + 1), :], table[cap * o : cap * (o + 1), :])
            for o in range(CHUNK * c, CHUNK * (c + 1))
        ],
        axis=0,
    )
    return chosen[:, :128] * chosen[:, 128:]


def edge_all(e_ref, hot_ref, ghost_ref, w_local, w_ghost, w_in, w_out, table, out_ref):
    cap = e_ref.shape[0] // OFFS
    fill_table(ghost_ref, w_local, w_ghost, table)
    for c in range(OFFS // CHUNK):
        span = slice(CHUNK * cap * c, CHUNK * cap * (c + 1))
        state = e_ref[span, :]
        gate = silu(dot(state, w_in) * chosen_product(hot_ref, table, c)).astype(BF16)
        out_ref[span, :] = rms_norm(state.astype(F32) + dot(gate, w_out)).astype(BF16)


def edge_body(layer, hand_on=False):
    def body(e_ref, hot_ref, ghost_ref, wl_ref, wg_ref, wi_ref, wo_ref, *refs):
        if hand_on:
            refs[2][...] = refs[0][...]
            refs = (refs[1], refs[3])
        out_ref, table = refs
        edge_all(
            e_ref, hot_ref, ghost_ref, wl_ref[layer], wg_ref[layer], wi_ref[layer], wo_ref[layer],
            table, out_ref,
        )

    return body


def twice(weight):
    blank = jnp.zeros_like(weight)
    return jnp.concatenate(
        [
            jnp.concatenate([weight, blank], axis=1),
            jnp.concatenate([blank, weight], axis=1),
        ],
        axis=0,
    )


def final_body(layer):
    def body(
        own_ref, mir_ref, ho_ref, hm_ref, ghost_ref, wl_ref, wr_ref, wi_ref, wo_ref,
        po_ref, pm_ref, perm_ref, owned_ref, wcat_ref,
        out_ref, table_own, table_mir, ranked, rows,
    ):
        atoms = ghost_ref.shape[0] // OFFS
        cap = own_ref.shape[0] // OFFS
        fan = out_ref.shape[1] // atoms
        w_in, w_out = twice(wi_ref[layer]), twice(wo_ref[layer])
        fill_table(ghost_ref, wl_ref[layer], wr_ref[layer], table_own)
        fill_table(ghost_ref, wr_ref[layer], wl_ref[layer], table_mir)
        for c in range(OFFS // CHUNK):
            span = slice(CHUNK * cap * c, CHUNK * cap * (c + 1))
            state = jnp.concatenate([own_ref[span, :], mir_ref[span, :]], axis=1)
            chosen = jnp.concatenate(
                [chosen_product(ho_ref, table_own, c), chosen_product(hm_ref, table_mir, c)],
                axis=1,
            )
            gate = silu(dot(state, w_in) * chosen).astype(BF16)
            renewed = state.astype(F32) + dot(gate, w_out)
            e_own = rms_norm(renewed[:, :128]).astype(BF16)
            e_mir = rms_norm(renewed[:, 128:]).astype(BF16)
            for i in range(CHUNK):
                o = CHUNK * c + i
                here = slice(cap * i, cap * (i + 1))
                span = slice(cap * o, cap * (o + 1))
                ranked[span, :128] = dot(po_ref[span, :], e_own[here])
                ranked[span, 128:] = dot(pm_ref[span, :], e_mir[here])
        for q in range(atoms // 4):
            span = slice(4 * fan * q, 4 * fan * (q + 1))
            tiles = jnp.concatenate(
                [ranked[cap * o + 8 * q : cap * o + 8 * (q + 1), :] for o in range(OFFS)], axis=0
            ).astype(BF16)
            spread = dot(perm_ref[span, :], tiles)
            mine = jnp.concatenate(
                [owned_ref[:, 4 * q + i : 4 * q + i + 1] for i in range(4)], axis=0
            )
            mine = mine > 0.5
            rows[span, :128] = jnp.where(mine, spread[:, :128], 0.0).astype(BF16)
            rows[span, 128:] = jnp.where(mine, 0.0, spread[:, 128:]).astype(BF16)
        step = 16 * fan
        for g in range(atoms // 16):
            out_ref[:, step * g : step * (g + 1)] = dot_nt(
                wcat_ref[...], rows[step * g : step * (g + 1), :]
            ).astype(BF16)

    return body


def shards(
    atom_feats, bond_embed, pair_dist, neighbours, slot_kind, own_rows, send_pos, recv_pos,
    w_left, w_right, w_edge_in, w_edge_out, w_msg, w_upd, node_gain, w_block,
):
    atoms, channels = atom_feats.shape
    slots = neighbours.shape[0]
    fan = slots // atoms
    owned = own_rows.shape[0]
    cap = owned // OFFS
    block = w_block.shape[1]
    ghosts = OFFS * atoms

    def array(*shape, dtype=BF16):
        return jax.ShapeDtypeStruct(shape, dtype)

    def tiles(values):
        return values.reshape(-1, 128)

    send, own = tiles(send_pos), tiles(own_rows)
    nb, kind, recv, dist = map(tiles, (neighbours, slot_kind, recv_pos, pair_dist))
    opposite = swapped(atom_feats, "layer")
    both = jnp.concatenate(
        [(nb | (kind << 11) | ((recv & 127) << 13)).astype(F32), dist], axis=0
    )
    adjacency, pack = call(
        slots_body,
        (array(atoms, ghosts), array(fan, atoms, dtype=jnp.int32)),
        both,
        us=2.0,
    )
    ordered, hidden = call(
        order_body,
        (array(owned, channels), array(atoms, channels)),
        send, bond_embed, atom_feats,
        after=(pack,),
        us=2.0,
    )
    other = swapped(adjacency, "layer")
    sheets = jnp.concatenate([hidden, opposite], axis=0)
    outgoing = ordered.reshape(2, 3, 3, cap, channels)
    crossed = swapped(outgoing[1], "layer")
    mirror = deliver(outgoing, crossed).reshape(owned, channels)
    hot_own, hot_mir, place = call(
        pairs_body,
        (array(owned, 128), array(owned, 128), array(fan, atoms, dtype=F32)),
        send, own, nb, kind, recv, pack,
        us=2.5,
    )
    pick_own, pick_mir, perm, mine, w_cat = call(
        places_body,
        (
            array(owned, cap),
            array(owned, cap),
            array(slots, 2 * fan),
            array(fan, atoms, dtype=F32),
            array(block, 2 * channels),
        ),
        pack, place, w_block.T,
        us=2.5,
    )
    table = pltpu.VMEM((2 * ghosts, 2 * channels), BF16)
    mirror_ghosts = []
    for layer in range(2):
        ghost = ghosts_of(sheets)
        mirror_ghosts.append(ghost)
        sheets = call(
            node_body(layer),
            array(2 * atoms, channels),
            adjacency, other, ghost, w_msg, w_upd, node_gain,
            after=(perm,) if layer else (crossed,),
            us=0.6,
        )
        ordered = call(
            edge_body(layer),
            array(owned, channels),
            ordered, hot_own, ghost, w_left, w_right, w_edge_in, w_edge_out,
            scratch=[table],
            us=1.4,
        )
    centre = sheets
    for layer in range(2):
        mirror, centre = call(
            edge_body(layer, True),
            (array(owned, channels), array(2 * atoms, channels)),
            mirror, hot_mir, mirror_ghosts[layer], w_right, w_left, w_edge_in, w_edge_out, centre,
            scratch=[table],
            us=1.4,
        )
    ghost = ghosts_of(sheets, centre)
    return call(
        final_body(2),
        array(block, slots),
        ordered, mirror, hot_own, hot_mir, ghost, w_left, w_right, w_edge_in, w_edge_out,
        pick_own, pick_mir, perm, mine, w_cat,
        scratch=[
            table,
            table,
            pltpu.VMEM((owned, 2 * channels), F32),
            pltpu.VMEM((slots, 2 * channels), BF16),
        ],
        us=7.0,
    )


def solution(mesh):
    axes = ("gx", "gy", "layer")
    rows = P(axes, None)
    flat = P(axes)
    placed = (rows, rows) + (flat,) * 6 + (P(),) * 8
    return jax.shard_map(
        shards,
        mesh=mesh,
        in_specs=placed,
        out_specs=P(None, axes),
        check_vma=False,
    )
```

```python
import jax
import jax.numpy as jnp
from jax import lax
from jax.experimental import pallas as pl
from jax.experimental.pallas import tpu as pltpu
from jax.sharding import PartitionSpec as P

ORB = 13
GROUPS = 4
OFFS = 18
AXES = ("gx", "gy", "layer")
F32 = jnp.float32
BF16 = jnp.bfloat16
VMEM_LIMIT = 24 * 1024 * 1024


def swapped(value, axis):
    return lax.ppermute(value, axis, [(0, 1), (1, 0)])


def moved(value, axis, steps):
    count = lax.axis_size(axis)
    return lax.ppermute(value, axis, [(i, (i + steps) % count) for i in range(count)])


def across_rows(outgoing, crossed):
    sheets = jnp.stack([outgoing[0], crossed])
    rows = [moved(sheets[:, i], "gx", i - 1) if i != 1 else sheets[:, i] for i in (2, 1, 0)]
    return jnp.stack(rows, axis=1)


def across_columns(shifted):
    cols = [moved(shifted[:, :, i], "gy", i - 1) if i != 1 else shifted[:, :, i] for i in (2, 1, 0)]
    return jnp.stack(cols, axis=2)


def partner_domains():
    offset = jnp.arange(OFFS, dtype=jnp.int32)
    rows, cols, sheets = (lax.axis_size(a) for a in AXES)
    x, y, sheet = (lax.axis_index(a) for a in AXES)
    x = (x + offset % 9 // 3 - 1) % rows
    y = (y + offset % 3 - 1) % cols
    return ((x * cols + y) * sheets + (sheet + offset // 9) % sheets).astype(jnp.int32)


def dot(a, b):
    return jnp.dot(a, b, preferred_element_type=F32)


def dot_nt(a, b):
    return lax.dot_general(a, b, (((1,), (1,)), ((), ())), preferred_element_type=F32)


def one_hot(mask):
    return jnp.where(mask, 1.0, 0.0).astype(BF16)


def silu(v):
    return v * (0.5 * jnp.tanh(0.5 * v) + 0.5)


def rms_norm(v):
    return v * lax.rsqrt(jnp.mean(v * v, axis=-1, keepdims=True) + 1e-06)


def iota(shape, dim):
    return lax.broadcasted_iota(jnp.int32, shape, dim)


def fiota(shape, dim):
    return iota(shape, dim).astype(F32)


def call(body, outs, *args, after=(), domains=None, scratch=(), us=1.0):
    head = () if domains is None else (domains,)
    used = len(head) + len(args)

    def ordered_body(*refs):
        body(*refs[:used], *refs[used + len(after) :])

    return pl.pallas_call(
        ordered_body if after else body,
        out_shape=outs,
        in_specs=[pl.BlockSpec(memory_space=pltpu.SMEM)] * len(head)
        + [pl.BlockSpec(memory_space=pltpu.VMEM)] * len(args)
        + [pl.BlockSpec(memory_space=pl.ANY)] * len(after),
        scratch_shapes=list(scratch),
        compiler_params=pltpu.CompilerParams(vmem_limit_bytes=VMEM_LIMIT),
        cost_estimate=pl.CostEstimate(
            flops=int(us * 1.1e9), bytes_accessed=int(us * 3.6e6), transcendentals=0
        ),
    )(*head, *args, *after)


def as_row(tiles):
    return jnp.concatenate([tiles[i : i + 1] for i in range(tiles.shape[0])], axis=1)


def folded(row, count, fan):
    return jnp.concatenate([row[:, fan * n : fan * (n + 1)] for n in range(count)], axis=0)


def transposed(values):
    rows, cols = values.shape
    filler = jnp.zeros((rows, 128 - cols), F32)
    return jnp.transpose(jnp.concatenate([values, filler], axis=1))[:cols]


def order_body(send_ref, bond_ref, out_ref):
    owned = bond_ref.shape[0]
    half = owned // 2
    cap = owned // OFFS
    bond = jnp.concatenate([bond_ref[:half, :], bond_ref[half:, :]], axis=1)
    send = as_row(send_ref[...])
    low = one_hot(iota((cap, owned), 0) == (send & 127))
    high = send >> 7
    late = iota((32, owned), 1) >= half
    late = dot_nt(low, one_hot((iota((32, owned), 0) == high) & late))

    def masked(o):
        mask = jnp.where(high == o, 1.0, 0.0)
        mask = jnp.broadcast_to(mask, (16, owned)).astype(BF16)
        kept = [low[16 * i : 16 * (i + 1)] * mask for i in range(cap // 16)]
        return [k[:, :half] + k[:, half:] for k in kept]

    for i in range(OFFS // 2):
        both = dot(jnp.concatenate(masked(2 * i) + masked(2 * i + 1), axis=0), bond)
        column = jnp.concatenate([late[:, 2 * i : 2 * i + 1], late[:, 2 * i + 1 : 2 * i + 2]], axis=0)
        out_ref[2 * cap * i : 2 * cap * (i + 1), :] = jnp.where(
            column > 0.5, both[:, 128:], both[:, :128]
        ).astype(BF16)


def slots_body(both_ref, adj_ref, pack_ref):
    fan, atoms = pack_ref.shape
    half = both_ref.shape[0] // 2
    pack = transposed(folded(as_row(both_ref[:half, :]), atoms, fan)).astype(jnp.int32)
    dist = transposed(folded(as_row(both_ref[half:, :]), atoms, fan))
    pack_ref[...] = pack
    peer = (pack & 63).astype(F32)
    off = ((pack & 2047) >> 6).astype(F32)
    scaled = dist * (1.0 / 7.0)
    env = 1.0 - scaled * scaled
    env = jnp.where(((pack >> 11) & 3) > 0, env * env, 0.0)
    row = fiota((fan, atoms), 0)
    target = off * float(GROUPS) + ranked_among(off)
    env_sorted = jnp.zeros((fan, atoms), F32)
    peer_sorted = jnp.zeros((fan, atoms), F32)
    for s in range(fan):
        here = target[s : s + 1, :] == row
        env_sorted = jnp.where(here, env[s : s + 1, :], env_sorted)
        peer_sorted = jnp.where(here, peer[s : s + 1, :], peer_sorted)
    which = fiota((atoms, atoms), 0)
    parts = []
    for o in range(OFFS):
        part = jnp.zeros((atoms, atoms), F32)
        for t in range(GROUPS * o, GROUPS * (o + 1)):
            part += jnp.where(peer_sorted[t : t + 1, :] == which, env_sorted[t : t + 1, :], 0.0)
        parts.append(part)
    for m in range(OFFS // 2):
        pair = jnp.concatenate([parts[2 * m], parts[2 * m + 1]], axis=0)
        pair = jnp.concatenate([pair, jnp.zeros_like(pair)], axis=1)
        adj_ref[:, 128 * m : 128 * (m + 1)] = jnp.transpose(pair)[:atoms].astype(BF16)


def ranked_among(key):
    fan = key.shape[0]
    row = fiota(key.shape, 0)
    rank = jnp.zeros(key.shape, F32)
    for s in range(fan - 1):
        rank += jnp.where((key == key[s : s + 1, :]) & (row > float(s)), 1.0, 0.0)
    return rank


def write_hots(out_ref, index):
    cap = index.shape[0]
    lane = fiota((cap, 128), 1)
    for o in range(OFFS):
        hot = (lane == index[:, o : o + 1]) | (lane == index[:, 32 + o : 33 + o] + 64.0)
        out_ref[cap * o : cap * (o + 1), :] = one_hot(hot)


def pairs_body(
    send_ref, own_ref, nb_ref, kind_ref, recv_ref, pack_ref, hot_own_ref, hot_mir_ref, place_ref
):
    fan, atoms = pack_ref.shape
    cap = hot_own_ref.shape[0] // OFFS
    send = as_row(send_ref[...])
    own = as_row(own_ref[...]).astype(F32)
    owned = send.shape[1]
    atom_r = jnp.floor((own + 0.5) * (1.0 / fan))
    slot_r = own - fan * atom_r
    off_r = (send >> 7).astype(F32)
    pos_r = (send & 127).astype(F32)
    peer = (pack_ref[...] & 63).astype(F32)
    at_atom = fiota((atoms, owned), 0) == atom_r
    at_slot = fiota((fan, owned), 0) == slot_r
    place_ref[...] = dot_nt(
        one_hot(at_slot), jnp.where(at_atom, pos_r + 1.0, 0.0).astype(BF16)
    )
    peer_all = dot(peer.astype(BF16), one_hot(at_atom))
    peer_r = jnp.sum(jnp.where(at_slot, peer_all, 0.0), axis=0, keepdims=True)
    at_off = fiota((32, owned), 0) == off_r
    values = jnp.concatenate(
        [jnp.where(at_off, atom_r, 0.0), jnp.where(at_off, peer_r, 0.0)], axis=0
    ).astype(BF16)
    write_hots(hot_own_ref, dot_nt(one_hot(fiota((cap, owned), 0) == pos_r), values))

    ids = as_row(jnp.where(kind_ref[...] == 2, nb_ref[...], 64 * 31))
    slots = ids.shape[1]
    atom_s = jnp.floor((fiota((1, slots), 1) + 0.5) * (1.0 / fan))
    peer_s = (ids & 63).astype(F32)
    off_s = (ids >> 6).astype(F32)
    pos_s = as_row(recv_ref[...] & 127).astype(F32)
    at_off = fiota((32, slots), 0) == off_s
    values = jnp.concatenate(
        [jnp.where(at_off, atom_s, 0.0), jnp.where(at_off, peer_s, 0.0)], axis=0
    ).astype(BF16)
    write_hots(hot_mir_ref, dot_nt(one_hot(fiota((cap, slots), 0) == pos_s), values))


def places_body(
    pack_ref, place_ref, wb_ref, pick_own_ref, pick_mir_ref, perm_ref, owned_ref, wcat_ref
):
    fan, atoms = pack_ref.shape
    cap = pick_own_ref.shape[0] // OFFS
    pack = pack_ref[...]
    off = ((pack & 2047) >> 6).astype(F32)
    kind = (pack >> 11) & 3
    pos_in = (pack >> 13).astype(F32)
    place = place_ref[...]
    owned = jnp.where(place > 0.5, 1.0, 0.0)
    owned_ref[...] = owned
    src = jnp.where(kind == 1, place, jnp.where(kind == 2, pos_in + 1.0, 0.0))
    rank = ranked_among(off * 2.0 + owned)
    target = off * float(GROUPS) + (2.0 - 2.0 * owned) + rank
    row = fiota((fan, atoms), 0)
    sorted_src = jnp.zeros((fan, atoms), F32)
    for s in range(fan):
        sorted_src = jnp.where(target[s : s + 1, :] == row, src[s : s + 1, :], sorted_src)
    spread = one_hot((iota((cap, atoms), 0) >> 1) == iota((cap, atoms), 1))
    spread = dot_nt(spread, sorted_src.astype(BF16))
    member = iota((cap, fan), 1) & 3
    parity = iota((cap, fan), 0) & 1
    fold = one_hot((iota((fan, 32), 0) >> 2) == iota((fan, 32), 1))
    lane = fiota((cap, cap), 1)
    for shift, pick_ref in ((0, pick_own_ref), (2, pick_mir_ref)):
        kept = jnp.where(member == parity + shift, spread, 0.0).astype(BF16)
        index = dot(kept, fold) - 1.0
        for o in range(OFFS):
            pick_ref[cap * o : cap * (o + 1), :] = one_hot(index[:, o : o + 1] == lane)

    spot = off * 8.0 + (iota((fan, atoms), 1) & 3).astype(F32) * 2.0 + rank
    lane = fiota((fan, 2 * fan), 1)
    for q in range(atoms // 4):
        perm_ref[4 * fan * q : 4 * fan * (q + 1), :] = jnp.concatenate(
            [jnp.where(spot[:, 4 * q + i : 4 * q + i + 1] == lane, 1.0, 0.0) for i in range(4)],
            axis=0,
        ).astype(BF16)

    block = wb_ref.shape[0]
    row = fiota((block, block), 0)
    col = fiota((block, block), 1)
    major = jnp.floor((row + 0.5) * (1.0 / ORB))
    wcat_ref[:, :128] = wb_ref[...]
    wcat_ref[:, 128:] = dot(
        one_hot((row - ORB * major) * ORB + major == col), wb_ref[...]
    ).astype(BF16)


def blocks_of(domain_ref, all_ref, atoms=64):
    return [
        all_ref[pl.ds(pl.multiple_of(domain_ref[o] * atoms, atoms), atoms), :] for o in range(OFFS)
    ]


def node_body(layer):
    def body(domain_ref, adj_ref, all_ref, wm_ref, wu_ref, gain_ref, out_ref):
        ghosts = blocks_of(domain_ref, all_ref)
        mixed = dot(adj_ref[...], jnp.concatenate(ghosts, axis=0)).astype(BF16)
        summed = (dot(mixed, wm_ref[layer]) * 0.125).astype(BF16)
        updated = ghosts[4].astype(F32) + silu(dot(summed, wu_ref[layer]))
        out_ref[...] = (rms_norm(updated) * gain_ref[layer : layer + 1, :]).astype(BF16)

    return body


CHUNK = 6


def fill_table(ghosts, w_local, w_ghost, table):
    atoms = ghosts[0].shape[0]
    local = dot(ghosts[4], w_local).astype(BF16)
    distant = dot(jnp.concatenate(ghosts, axis=0), w_ghost).astype(BF16)
    blank = jnp.zeros((atoms, 128), BF16)
    for o in range(OFFS):
        base = 2 * atoms * o
        table[base : base + atoms, :128] = local
        table[base : base + atoms, 128:] = blank
        table[base + atoms : base + 2 * atoms, :128] = blank
        table[base + atoms : base + 2 * atoms, 128:] = distant[atoms * o : atoms * (o + 1)]


def chosen_product(hot_ref, table, c):
    cap = hot_ref.shape[0] // OFFS
    chosen = jnp.concatenate(
        [
            dot(hot_ref[cap * o : cap * (o + 1), :], table[cap * o : cap * (o + 1), :])
            for o in range(CHUNK * c, CHUNK * (c + 1))
        ],
        axis=0,
    )
    return chosen[:, :128] * chosen[:, 128:]


def edge_all(e_ref, hot_ref, ghosts, w_local, w_ghost, w_in, w_out, table, out_ref):
    cap = e_ref.shape[0] // OFFS
    fill_table(ghosts, w_local, w_ghost, table)
    for c in range(OFFS // CHUNK):
        span = slice(CHUNK * cap * c, CHUNK * cap * (c + 1))
        state = e_ref[span, :]
        gate = silu(dot(state, w_in) * chosen_product(hot_ref, table, c)).astype(BF16)
        out_ref[span, :] = rms_norm(state.astype(F32) + dot(gate, w_out)).astype(BF16)


def edge_body(layer):
    def body(
        domain_ref, e_ref, hot_ref, all_ref, wl_ref, wg_ref, wi_ref, wo_ref, out_ref, table
    ):
        edge_all(
            e_ref, hot_ref, blocks_of(domain_ref, all_ref), wl_ref[layer], wg_ref[layer],
            wi_ref[layer], wo_ref[layer], table, out_ref,
        )

    return body


def twice(weight):
    blank = jnp.zeros_like(weight)
    return jnp.concatenate(
        [
            jnp.concatenate([weight, blank], axis=1),
            jnp.concatenate([blank, weight], axis=1),
        ],
        axis=0,
    )


def final_body(layer):
    def body(
        domain_ref, own_ref, mir_ref, ho_ref, hm_ref, all_ref, wl_ref, wr_ref, wi_ref, wo_ref,
        po_ref, pm_ref, perm_ref, owned_ref, wcat_ref,
        out_ref, table_own, table_mir, ranked, rows,
    ):
        ghosts = blocks_of(domain_ref, all_ref)
        atoms = ghosts[0].shape[0]
        cap = own_ref.shape[0] // OFFS
        fan = out_ref.shape[1] // atoms
        w_in, w_out = twice(wi_ref[layer]), twice(wo_ref[layer])
        fill_table(ghosts, wl_ref[layer], wr_ref[layer], table_own)
        fill_table(ghosts, wr_ref[layer], wl_ref[layer], table_mir)
        for c in range(OFFS // CHUNK):
            span = slice(CHUNK * cap * c, CHUNK * cap * (c + 1))
            state = jnp.concatenate([own_ref[span, :], mir_ref[span, :]], axis=1)
            chosen = jnp.concatenate(
                [chosen_product(ho_ref, table_own, c), chosen_product(hm_ref, table_mir, c)],
                axis=1,
            )
            gate = silu(dot(state, w_in) * chosen).astype(BF16)
            renewed = state.astype(F32) + dot(gate, w_out)
            e_own = rms_norm(renewed[:, :128]).astype(BF16)
            e_mir = rms_norm(renewed[:, 128:]).astype(BF16)
            for i in range(CHUNK):
                o = CHUNK * c + i
                here = slice(cap * i, cap * (i + 1))
                span = slice(cap * o, cap * (o + 1))
                ranked[span, :128] = dot(po_ref[span, :], e_own[here])
                ranked[span, 128:] = dot(pm_ref[span, :], e_mir[here])
        for q in range(atoms // 4):
            span = slice(4 * fan * q, 4 * fan * (q + 1))
            tiles = jnp.concatenate(
                [ranked[cap * o + 8 * q : cap * o + 8 * (q + 1), :] for o in range(OFFS)], axis=0
            ).astype(BF16)
            spread = dot(perm_ref[span, :], tiles)
            mine = jnp.concatenate(
                [owned_ref[:, 4 * q + i : 4 * q + i + 1] for i in range(4)], axis=0
            )
            mine = mine > 0.5
            rows[span, :128] = jnp.where(mine, spread[:, :128], 0.0).astype(BF16)
            rows[span, 128:] = jnp.where(mine, 0.0, spread[:, 128:]).astype(BF16)
        step = 16 * fan
        for g in range(atoms // 16):
            out_ref[:, step * g : step * (g + 1)] = dot_nt(
                wcat_ref[...], rows[step * g : step * (g + 1), :]
            ).astype(BF16)

    return body


def shards(
    atom_feats, bond_embed, pair_dist, neighbours, slot_kind, own_rows, send_pos, recv_pos,
    w_left, w_right, w_edge_in, w_edge_out, w_msg, w_upd, node_gain, w_block,
):
    atoms, channels = atom_feats.shape
    slots = neighbours.shape[0]
    fan = slots // atoms
    owned = own_rows.shape[0]
    cap = owned // OFFS
    block = w_block.shape[1]
    ghosts = OFFS * atoms

    def array(*shape, dtype=BF16):
        return jax.ShapeDtypeStruct(shape, dtype)

    def tiles(values):
        return values.reshape(-1, 128)

    send, own = tiles(send_pos), tiles(own_rows)
    nb, kind, recv, dist = map(tiles, (neighbours, slot_kind, recv_pos, pair_dist))
    gathered = lax.all_gather(atom_feats, AXES, tiled=True)
    domains = partner_domains()
    both = jnp.concatenate(
        [(nb | (kind << 11) | ((recv & 127) << 13)).astype(F32), dist], axis=0
    )
    adjacency, pack = call(
        slots_body,
        (array(atoms, ghosts), array(fan, atoms, dtype=jnp.int32)),
        both,
        us=2.0,
    )
    ordered = call(
        order_body,
        array(owned, channels),
        send, bond_embed,
        after=(pack,),
        us=2.0,
    )
    outgoing = ordered.reshape(2, 3, 3, cap, channels)
    crossed = swapped(outgoing[1], "layer")
    shifted = across_rows(outgoing, crossed)
    mirror = across_columns(shifted).reshape(owned, channels)
    hot_own, hot_mir, place = call(
        pairs_body,
        (array(owned, 128), array(owned, 128), array(fan, atoms, dtype=F32)),
        send, own, nb, kind, recv, pack,
        us=2.5,
    )
    pick_own, pick_mir, perm, mine, w_cat = call(
        places_body,
        (
            array(owned, cap),
            array(owned, cap),
            array(slots, 2 * fan),
            array(fan, atoms, dtype=F32),
            array(block, 2 * channels),
        ),
        pack, place, w_block.T,
        us=2.5,
    )
    table = pltpu.VMEM((2 * ghosts, 2 * channels), BF16)
    for layer in range(2):
        hidden = call(
            node_body(layer),
            array(atoms, channels),
            adjacency, gathered, w_msg, w_upd, node_gain,
            domains=domains,
            after=(shifted, perm) if layer else (crossed,),
            us=0.6,
        )
        ordered = call(
            edge_body(layer),
            array(owned, channels),
            ordered, hot_own, gathered, w_left, w_right, w_edge_in, w_edge_out,
            domains=domains,
            scratch=[table],
            us=1.4,
        )
        mirror = call(
            edge_body(layer),
            array(owned, channels),
            mirror, hot_mir, gathered, w_right, w_left, w_edge_in, w_edge_out,
            domains=domains,
            scratch=[table],
            us=1.4,
        )
        gathered = lax.all_gather(hidden, AXES, tiled=True)
    return call(
        final_body(2),
        array(block, slots),
        ordered, mirror, hot_own, hot_mir, gathered, w_left, w_right, w_edge_in, w_edge_out,
        pick_own, pick_mir, perm, mine, w_cat,
        domains=domains,
        scratch=[
            table,
            table,
            pltpu.VMEM((owned, 2 * channels), F32),
            pltpu.VMEM((slots, 2 * channels), BF16),
        ],
        us=7.0,
    )


def solution(mesh):
    axes = ("gx", "gy", "layer")
    rows = P(axes, None)
    flat = P(axes)
    placed = (rows, rows) + (flat,) * 6 + (P(),) * 8
    return jax.shard_map(
        shards,
        mesh=mesh,
        in_specs=placed,
        out_specs=P(None, axes),
        check_vma=False,
    )
```

```python
import jax
import jax.numpy as jnp
from jax import lax
from jax.experimental import pallas as pl
from jax.experimental.pallas import tpu as pltpu
from jax.sharding import PartitionSpec as P

ORB = 13
GROUPS = 4
OFFS = 18
F32 = jnp.float32
BF16 = jnp.bfloat16
VMEM_LIMIT = 24 * 1024 * 1024


def swapped(value, axis):
    return lax.ppermute(value, axis, [(0, 1), (1, 0)])


def moved(value, axis, steps):
    count = lax.axis_size(axis)
    return lax.ppermute(value, axis, [(i, (i + steps) % count) for i in range(count)])


def with_halo(block, axis, dim):
    low = moved(block, axis, 1)
    high = moved(block, axis, -1)
    return jnp.concatenate([low, block, high], axis=dim)


def ghosts_of(sheets, centre=None):
    low, high = moved(sheets, "gx", 1), moved(sheets, "gx", -1)
    centre = sheets if centre is None else centre
    framed = with_halo(jnp.concatenate([low, centre, high], axis=1), "gy", 2)
    return framed.reshape(-1, sheets.shape[-1])


def across_rows(outgoing, crossed):
    sheets = jnp.stack([outgoing[0], crossed])
    rows = [moved(sheets[:, i], "gx", i - 1) if i != 1 else sheets[:, i] for i in (2, 1, 0)]
    return jnp.stack(rows, axis=1)


def across_columns(shifted):
    cols = [moved(shifted[:, :, i], "gy", i - 1) if i != 1 else shifted[:, :, i] for i in (2, 1, 0)]
    return jnp.stack(cols, axis=2)


def dot(a, b):
    return jnp.dot(a, b, preferred_element_type=F32)


def dot_nt(a, b):
    return lax.dot_general(a, b, (((1,), (1,)), ((), ())), preferred_element_type=F32)


def one_hot(mask):
    return jnp.where(mask, 1.0, 0.0).astype(BF16)


def silu(v):
    return v * (0.5 * jnp.tanh(0.5 * v) + 0.5)


def rms_norm(v):
    return v * lax.rsqrt(jnp.mean(v * v, axis=-1, keepdims=True) + 1e-06)


def iota(shape, dim):
    return lax.broadcasted_iota(jnp.int32, shape, dim)


def fiota(shape, dim):
    return iota(shape, dim).astype(F32)


def call(body, outs, *args, after=(), scratch=(), us=1.0):
    used = len(args)

    def ordered_body(*refs):
        body(*refs[:used], *refs[used + len(after) :])

    return pl.pallas_call(
        ordered_body if after else body,
        out_shape=outs,
        in_specs=[pl.BlockSpec(memory_space=pltpu.VMEM)] * used
        + [pl.BlockSpec(memory_space=pl.ANY)] * len(after),
        scratch_shapes=list(scratch),
        compiler_params=pltpu.CompilerParams(vmem_limit_bytes=VMEM_LIMIT),
        cost_estimate=pl.CostEstimate(
            flops=int(us * 1.1e9), bytes_accessed=int(us * 3.6e6), transcendentals=0
        ),
    )(*args, *after)


def as_row(tiles):
    return jnp.concatenate([tiles[i : i + 1] for i in range(tiles.shape[0])], axis=1)


def folded(row, count, fan):
    return jnp.concatenate([row[:, fan * n : fan * (n + 1)] for n in range(count)], axis=0)


def transposed(values):
    rows, cols = values.shape
    filler = jnp.zeros((rows, 128 - cols), F32)
    return jnp.transpose(jnp.concatenate([values, filler], axis=1))[:cols]


def order_body(send_ref, bond_ref, h_ref, out_ref, h_out_ref):
    owned = bond_ref.shape[0]
    half = owned // 2
    cap = owned // OFFS
    h_out_ref[...] = h_ref[...]
    bond = jnp.concatenate([bond_ref[:half, :], bond_ref[half:, :]], axis=1)
    send = as_row(send_ref[...])
    low = one_hot(iota((cap, owned), 0) == (send & 127))
    high = send >> 7
    late = iota((32, owned), 1) >= half
    late = dot_nt(low, one_hot((iota((32, owned), 0) == high) & late))

    def masked(o):
        mask = jnp.where(high == o, 1.0, 0.0)
        mask = jnp.broadcast_to(mask, (16, owned)).astype(BF16)
        kept = [low[16 * i : 16 * (i + 1)] * mask for i in range(cap // 16)]
        return [k[:, :half] + k[:, half:] for k in kept]

    for i in range(OFFS // 2):
        both = dot(jnp.concatenate(masked(2 * i) + masked(2 * i + 1), axis=0), bond)
        column = jnp.concatenate([late[:, 2 * i : 2 * i + 1], late[:, 2 * i + 1 : 2 * i + 2]], axis=0)
        out_ref[2 * cap * i : 2 * cap * (i + 1), :] = jnp.where(
            column > 0.5, both[:, 128:], both[:, :128]
        ).astype(BF16)


def slots_body(both_ref, h_ref, adj_ref, pack_ref, h_out_ref):
    fan, atoms = pack_ref.shape
    half = both_ref.shape[0] // 2
    h_out_ref[...] = h_ref[...]
    pack = transposed(folded(as_row(both_ref[:half, :]), atoms, fan)).astype(jnp.int32)
    dist = transposed(folded(as_row(both_ref[half:, :]), atoms, fan))
    pack_ref[...] = pack
    peer = (pack & 63).astype(F32)
    off = ((pack & 2047) >> 6).astype(F32)
    scaled = dist * (1.0 / 7.0)
    env = 1.0 - scaled * scaled
    env = jnp.where(((pack >> 11) & 3) > 0, env * env, 0.0)
    row = fiota((fan, atoms), 0)
    target = off * float(GROUPS) + ranked_among(off)
    env_sorted = jnp.zeros((fan, atoms), F32)
    peer_sorted = jnp.zeros((fan, atoms), F32)
    for s in range(fan):
        here = target[s : s + 1, :] == row
        env_sorted = jnp.where(here, env[s : s + 1, :], env_sorted)
        peer_sorted = jnp.where(here, peer[s : s + 1, :], peer_sorted)
    which = fiota((atoms, atoms), 0)
    parts = []
    for o in range(OFFS):
        part = jnp.zeros((atoms, atoms), F32)
        for t in range(GROUPS * o, GROUPS * (o + 1)):
            part += jnp.where(peer_sorted[t : t + 1, :] == which, env_sorted[t : t + 1, :], 0.0)
        parts.append(part)
    for m in range(OFFS // 2):
        pair = jnp.concatenate([parts[2 * m], parts[2 * m + 1]], axis=0)
        pair = jnp.concatenate([pair, jnp.zeros_like(pair)], axis=1)
        adj_ref[:, 128 * m : 128 * (m + 1)] = jnp.transpose(pair)[:atoms].astype(BF16)


def ranked_among(key):
    fan = key.shape[0]
    row = fiota(key.shape, 0)
    rank = jnp.zeros(key.shape, F32)
    for s in range(fan - 1):
        rank += jnp.where((key == key[s : s + 1, :]) & (row > float(s)), 1.0, 0.0)
    return rank


def write_hots(out_ref, index):
    cap = index.shape[0]
    lane = fiota((cap, 128), 1)
    for o in range(OFFS):
        hot = (lane == index[:, o : o + 1]) | (lane == index[:, 32 + o : 33 + o] + 64.0)
        out_ref[cap * o : cap * (o + 1), :] = one_hot(hot)


def pairs_body(
    send_ref, own_ref, nb_ref, kind_ref, recv_ref, pack_ref, hot_own_ref, hot_mir_ref, place_ref
):
    fan, atoms = pack_ref.shape
    cap = hot_own_ref.shape[0] // OFFS
    send = as_row(send_ref[...])
    own = as_row(own_ref[...]).astype(F32)
    owned = send.shape[1]
    atom_r = jnp.floor((own + 0.5) * (1.0 / fan))
    slot_r = own - fan * atom_r
    off_r = (send >> 7).astype(F32)
    pos_r = (send & 127).astype(F32)
    peer = (pack_ref[...] & 63).astype(F32)
    at_atom = fiota((atoms, owned), 0) == atom_r
    at_slot = fiota((fan, owned), 0) == slot_r
    place_ref[...] = dot_nt(
        one_hot(at_slot), jnp.where(at_atom, pos_r + 1.0, 0.0).astype(BF16)
    )
    peer_all = dot(peer.astype(BF16), one_hot(at_atom))
    peer_r = jnp.sum(jnp.where(at_slot, peer_all, 0.0), axis=0, keepdims=True)
    at_off = fiota((32, owned), 0) == off_r
    values = jnp.concatenate(
        [jnp.where(at_off, atom_r, 0.0), jnp.where(at_off, peer_r, 0.0)], axis=0
    ).astype(BF16)
    write_hots(hot_own_ref, dot_nt(one_hot(fiota((cap, owned), 0) == pos_r), values))

    ids = as_row(jnp.where(kind_ref[...] == 2, nb_ref[...], 64 * 31))
    slots = ids.shape[1]
    atom_s = jnp.floor((fiota((1, slots), 1) + 0.5) * (1.0 / fan))
    peer_s = (ids & 63).astype(F32)
    off_s = (ids >> 6).astype(F32)
    pos_s = as_row(recv_ref[...] & 127).astype(F32)
    at_off = fiota((32, slots), 0) == off_s
    values = jnp.concatenate(
        [jnp.where(at_off, atom_s, 0.0), jnp.where(at_off, peer_s, 0.0)], axis=0
    ).astype(BF16)
    write_hots(hot_mir_ref, dot_nt(one_hot(fiota((cap, slots), 0) == pos_s), values))


def places_body(
    pack_ref, place_ref, wb_ref, pick_own_ref, pick_mir_ref, perm_ref, owned_ref, wcat_ref
):
    fan, atoms = pack_ref.shape
    cap = pick_own_ref.shape[0] // OFFS
    pack = pack_ref[...]
    off = ((pack & 2047) >> 6).astype(F32)
    kind = (pack >> 11) & 3
    pos_in = (pack >> 13).astype(F32)
    place = place_ref[...]
    owned = jnp.where(place > 0.5, 1.0, 0.0)
    owned_ref[...] = owned
    src = jnp.where(kind == 1, place, jnp.where(kind == 2, pos_in + 1.0, 0.0))
    rank = ranked_among(off * 2.0 + owned)
    target = off * float(GROUPS) + (2.0 - 2.0 * owned) + rank
    row = fiota((fan, atoms), 0)
    sorted_src = jnp.zeros((fan, atoms), F32)
    for s in range(fan):
        sorted_src = jnp.where(target[s : s + 1, :] == row, src[s : s + 1, :], sorted_src)
    spread = one_hot((iota((cap, atoms), 0) >> 1) == iota((cap, atoms), 1))
    spread = dot_nt(spread, sorted_src.astype(BF16))
    member = iota((cap, fan), 1) & 3
    parity = iota((cap, fan), 0) & 1
    fold = one_hot((iota((fan, 32), 0) >> 2) == iota((fan, 32), 1))
    lane = fiota((cap, cap), 1)
    for shift, pick_ref in ((0, pick_own_ref), (2, pick_mir_ref)):
        kept = jnp.where(member == parity + shift, spread, 0.0).astype(BF16)
        index = dot(kept, fold) - 1.0
        for o in range(OFFS):
            pick_ref[cap * o : cap * (o + 1), :] = one_hot(index[:, o : o + 1] == lane)

    spot = off * 8.0 + (iota((fan, atoms), 1) & 3).astype(F32) * 2.0 + rank
    lane = fiota((fan, 2 * fan), 1)
    for q in range(atoms // 4):
        perm_ref[4 * fan * q : 4 * fan * (q + 1), :] = jnp.concatenate(
            [jnp.where(spot[:, 4 * q + i : 4 * q + i + 1] == lane, 1.0, 0.0) for i in range(4)],
            axis=0,
        ).astype(BF16)

    block = wb_ref.shape[0]
    row = fiota((block, block), 0)
    col = fiota((block, block), 1)
    major = jnp.floor((row + 0.5) * (1.0 / ORB))
    wcat_ref[:, :128] = wb_ref[...]
    wcat_ref[:, 128:] = dot(
        one_hot((row - ORB * major) * ORB + major == col), wb_ref[...]
    ).astype(BF16)


def node_body(layer):
    def body(adj_ref, other_ref, ghost_ref, wm_ref, wu_ref, gain_ref, out_ref):
        ghosts = ghost_ref.shape[0]
        half = ghosts // 2
        atoms = ghosts // OFFS
        mixed = dot(adj_ref[...], ghost_ref[...])
        other = dot(other_ref[:, :half], ghost_ref[half:, :])
        other += dot(other_ref[:, half:], ghost_ref[:half, :])
        mixed = jnp.concatenate([mixed, other], axis=0).astype(BF16)
        hidden = jnp.concatenate(
            [ghost_ref[atoms * 4 : atoms * 5, :], ghost_ref[atoms * 13 : atoms * 14, :]], axis=0
        )
        summed = (dot(mixed, wm_ref[layer]) * 0.125).astype(BF16)
        updated = hidden.astype(F32) + silu(dot(summed, wu_ref[layer]))
        out_ref[...] = (rms_norm(updated) * gain_ref[layer : layer + 1, :]).astype(BF16)

    return body


CHUNK = 6


def fill_table(ghost_ref, w_local, w_ghost, table):
    atoms = ghost_ref.shape[0] // OFFS
    local = dot(ghost_ref[atoms * 4 : atoms * 5, :], w_local).astype(BF16)
    distant = dot(ghost_ref[...], w_ghost).astype(BF16)
    blank = jnp.zeros((atoms, 128), BF16)
    for o in range(OFFS):
        base = 2 * atoms * o
        table[base : base + atoms, :128] = local
        table[base : base + atoms, 128:] = blank
        table[base + atoms : base + 2 * atoms, :128] = blank
        table[base + atoms : base + 2 * atoms, 128:] = distant[atoms * o : atoms * (o + 1)]


def chosen_product(hot_ref, table, c):
    cap = hot_ref.shape[0] // OFFS
    chosen = jnp.concatenate(
        [
            dot(hot_ref[cap * o : cap * (o + 1), :], table[cap * o : cap * (o + 1), :])
            for o in range(CHUNK * c, CHUNK * (c + 1))
        ],
        axis=0,
    )
    return chosen[:, :128] * chosen[:, 128:]


def edge_all(e_ref, hot_ref, ghost_ref, w_local, w_ghost, w_in, w_out, table, out_ref):
    cap = e_ref.shape[0] // OFFS
    fill_table(ghost_ref, w_local, w_ghost, table)
    for c in range(OFFS // CHUNK):
        span = slice(CHUNK * cap * c, CHUNK * cap * (c + 1))
        state = e_ref[span, :]
        gate = silu(dot(state, w_in) * chosen_product(hot_ref, table, c)).astype(BF16)
        out_ref[span, :] = rms_norm(state.astype(F32) + dot(gate, w_out)).astype(BF16)


def edge_body(layer, hand_on=False):
    def body(e_ref, hot_ref, ghost_ref, wl_ref, wg_ref, wi_ref, wo_ref, *refs):
        if hand_on:
            refs[2][...] = refs[0][...]
            refs = (refs[1], refs[3])
        out_ref, table = refs
        edge_all(
            e_ref, hot_ref, ghost_ref, wl_ref[layer], wg_ref[layer], wi_ref[layer], wo_ref[layer],
            table, out_ref,
        )

    return body


def twice(weight):
    blank = jnp.zeros_like(weight)
    return jnp.concatenate(
        [
            jnp.concatenate([weight, blank], axis=1),
            jnp.concatenate([blank, weight], axis=1),
        ],
        axis=0,
    )


def final_body(layer):
    def body(
        own_ref, mir_ref, ho_ref, hm_ref, ghost_ref, wl_ref, wr_ref, wi_ref, wo_ref,
        po_ref, pm_ref, perm_ref, owned_ref, wcat_ref,
        out_ref, table_own, table_mir, ranked, rows,
    ):
        atoms = ghost_ref.shape[0] // OFFS
        cap = own_ref.shape[0] // OFFS
        fan = out_ref.shape[1] // atoms
        w_in, w_out = twice(wi_ref[layer]), twice(wo_ref[layer])
        fill_table(ghost_ref, wl_ref[layer], wr_ref[layer], table_own)
        fill_table(ghost_ref, wr_ref[layer], wl_ref[layer], table_mir)
        for c in range(OFFS // CHUNK):
            span = slice(CHUNK * cap * c, CHUNK * cap * (c + 1))
            state = jnp.concatenate([own_ref[span, :], mir_ref[span, :]], axis=1)
            chosen = jnp.concatenate(
                [chosen_product(ho_ref, table_own, c), chosen_product(hm_ref, table_mir, c)],
                axis=1,
            )
            gate = silu(dot(state, w_in) * chosen).astype(BF16)
            renewed = state.astype(F32) + dot(gate, w_out)
            e_own = rms_norm(renewed[:, :128]).astype(BF16)
            e_mir = rms_norm(renewed[:, 128:]).astype(BF16)
            for i in range(CHUNK):
                o = CHUNK * c + i
                here = slice(cap * i, cap * (i + 1))
                span = slice(cap * o, cap * (o + 1))
                ranked[span, :128] = dot(po_ref[span, :], e_own[here])
                ranked[span, 128:] = dot(pm_ref[span, :], e_mir[here])
        for q in range(atoms // 4):
            span = slice(4 * fan * q, 4 * fan * (q + 1))
            tiles = jnp.concatenate(
                [ranked[cap * o + 8 * q : cap * o + 8 * (q + 1), :] for o in range(OFFS)], axis=0
            ).astype(BF16)
            spread = dot(perm_ref[span, :], tiles)
            mine = jnp.concatenate(
                [owned_ref[:, 4 * q + i : 4 * q + i + 1] for i in range(4)], axis=0
            )
            mine = mine > 0.5
            rows[span, :128] = jnp.where(mine, spread[:, :128], 0.0).astype(BF16)
            rows[span, 128:] = jnp.where(mine, 0.0, spread[:, 128:]).astype(BF16)
        step = 16 * fan
        for g in range(atoms // 16):
            out_ref[:, step * g : step * (g + 1)] = dot_nt(
                wcat_ref[...], rows[step * g : step * (g + 1), :]
            ).astype(BF16)

    return body


def shards(
    atom_feats, bond_embed, pair_dist, neighbours, slot_kind, own_rows, send_pos, recv_pos,
    w_left, w_right, w_edge_in, w_edge_out, w_msg, w_upd, node_gain, w_block,
):
    atoms, channels = atom_feats.shape
    slots = neighbours.shape[0]
    fan = slots // atoms
    owned = own_rows.shape[0]
    cap = owned // OFFS
    block = w_block.shape[1]
    ghosts = OFFS * atoms

    def array(*shape, dtype=BF16):
        return jax.ShapeDtypeStruct(shape, dtype)

    def tiles(values):
        return values.reshape(-1, 128)

    send, own = tiles(send_pos), tiles(own_rows)
    nb, kind, recv, dist = map(tiles, (neighbours, slot_kind, recv_pos, pair_dist))
    opposite = swapped(atom_feats, "layer")
    both = jnp.concatenate(
        [(nb | (kind << 11) | ((recv & 127) << 13)).astype(F32), dist], axis=0
    )
    adjacency, pack, hidden = call(
        slots_body,
        (array(atoms, ghosts), array(fan, atoms, dtype=jnp.int32), array(atoms, channels)),
        both, atom_feats,
        us=2.0,
    )
    other = swapped(adjacency, "layer")
    sheets = jnp.concatenate([hidden, opposite], axis=0)
    ordered, centre = call(
        order_body,
        (array(owned, channels), array(2 * atoms, channels)),
        send, bond_embed, sheets,
        us=2.0,
    )
    outgoing = ordered.reshape(2, 3, 3, cap, channels)
    crossed = swapped(outgoing[1], "layer")
    shifted = across_rows(outgoing, crossed)
    mirror = across_columns(shifted).reshape(owned, channels)
    hot_own, hot_mir, place = call(
        pairs_body,
        (array(owned, 128), array(owned, 128), array(fan, atoms, dtype=F32)),
        send, own, nb, kind, recv, pack,
        after=(ordered,),
        us=2.5,
    )
    pick_own, pick_mir, perm, mine, w_cat = call(
        places_body,
        (
            array(owned, cap),
            array(owned, cap),
            array(slots, 2 * fan),
            array(fan, atoms, dtype=F32),
            array(block, 2 * channels),
        ),
        pack, place, w_block.T,
        us=2.5,
    )
    table = pltpu.VMEM((2 * ghosts, 2 * channels), BF16)
    state = array(owned, channels)

    def framed_sheets(value):
        return value.reshape(2, 1, 1, atoms, channels)

    def edge(layer, own, after=(), hand_on=()):
        values = (ordered, hot_own) if own else (mirror, hot_mir)
        weights = (w_left, w_right) if own else (w_right, w_left)
        outs = (state, array(2 * atoms, channels)) if hand_on else state
        return call(
            edge_body(layer, bool(hand_on)),
            outs,
            *values, ghosts_at[layer], *weights, w_edge_in, w_edge_out, *hand_on,
            after=after,
            scratch=[table],
            us=1.4,
        )

    def node(layer, after):
        return call(
            node_body(layer),
            array(2 * atoms, channels),
            adjacency, other, ghosts_at[layer], w_msg, w_upd, node_gain,
            after=after,
            us=0.6,
        )

    ghosts_at = [ghosts_of(framed_sheets(sheets), framed_sheets(centre))]
    sheets = node(0, (crossed,))
    ghosts_at.append(ghosts_of(framed_sheets(sheets)))
    ordered = edge(0, True)
    sheets = node(1, (perm, ordered, shifted))
    ordered = edge(1, True)
    mirror, centre = edge(0, False, hand_on=(sheets,))
    mirror = edge(1, False)
    ghost = ghosts_of(framed_sheets(sheets), framed_sheets(centre))
    return call(
        final_body(2),
        array(block, slots),
        ordered, mirror, hot_own, hot_mir, ghost, w_left, w_right, w_edge_in, w_edge_out,
        pick_own, pick_mir, perm, mine, w_cat,
        scratch=[
            table,
            table,
            pltpu.VMEM((owned, 2 * channels), F32),
            pltpu.VMEM((slots, 2 * channels), BF16),
        ],
        us=7.0,
    )


def solution(mesh):
    axes = ("gx", "gy", "layer")
    rows = P(axes, None)
    flat = P(axes)
    placed = (rows, rows) + (flat,) * 6 + (P(),) * 8
    return jax.shard_map(
        shards,
        mesh=mesh,
        in_specs=placed,
        out_specs=P(None, axes),
        check_vma=False,
    )
```

```python
import jax
import jax.numpy as jnp
from jax import lax
from jax.experimental import pallas as pl
from jax.experimental.pallas import tpu as pltpu
from jax.sharding import PartitionSpec as P

ORB = 13
GROUPS = 4
OFFS = 18
F32 = jnp.float32
BF16 = jnp.bfloat16
VMEM_LIMIT = 24 * 1024 * 1024


def swapped(value, axis):
    return lax.ppermute(value, axis, [(0, 1), (1, 0)])


def moved(value, axis, steps):
    count = lax.axis_size(axis)
    return lax.ppermute(value, axis, [(i, (i + steps) % count) for i in range(count)])


def with_halo(block, axis, dim):
    low = moved(block, axis, 1)
    high = moved(block, axis, -1)
    return jnp.concatenate([low, block, high], axis=dim)


def ghosts_of(sheets, centre=None):
    low, high = moved(sheets, "gx", 1), moved(sheets, "gx", -1)
    centre = sheets if centre is None else centre
    framed = with_halo(jnp.concatenate([low, centre, high], axis=1), "gy", 2)
    return framed.reshape(-1, sheets.shape[-1])


def across_rows(outgoing, crossed):
    sheets = jnp.stack([outgoing[0], crossed])
    rows = [moved(sheets[:, i], "gx", i - 1) if i != 1 else sheets[:, i] for i in (2, 1, 0)]
    return jnp.stack(rows, axis=1)


def across_columns(shifted):
    cols = [moved(shifted[:, :, i], "gy", i - 1) if i != 1 else shifted[:, :, i] for i in (2, 1, 0)]
    return jnp.stack(cols, axis=2)


def dot(a, b):
    return jnp.dot(a, b, preferred_element_type=F32)


def dot_nt(a, b):
    return lax.dot_general(a, b, (((1,), (1,)), ((), ())), preferred_element_type=F32)


def one_hot(mask):
    return jnp.where(mask, 1.0, 0.0).astype(BF16)


def silu(v):
    return v * (0.5 * jnp.tanh(0.5 * v) + 0.5)


def rms_norm(v):
    return v * lax.rsqrt(jnp.mean(v * v, axis=-1, keepdims=True) + 1e-06)


def iota(shape, dim):
    return lax.broadcasted_iota(jnp.int32, shape, dim)


def fiota(shape, dim):
    return iota(shape, dim).astype(F32)


def call(body, outs, *args, after=(), scratch=(), us=1.0):
    used = len(args)

    def ordered_body(*refs):
        body(*refs[:used], *refs[used + len(after) :])

    return pl.pallas_call(
        ordered_body if after else body,
        out_shape=outs,
        in_specs=[pl.BlockSpec(memory_space=pltpu.VMEM)] * used
        + [pl.BlockSpec(memory_space=pl.ANY)] * len(after),
        scratch_shapes=list(scratch),
        compiler_params=pltpu.CompilerParams(vmem_limit_bytes=VMEM_LIMIT),
        cost_estimate=pl.CostEstimate(
            flops=int(us * 1.1e9), bytes_accessed=int(us * 3.6e6), transcendentals=0
        ),
    )(*args, *after)


def as_row(tiles):
    return jnp.concatenate([tiles[i : i + 1] for i in range(tiles.shape[0])], axis=1)


def folded(row, count, fan):
    return jnp.concatenate([row[:, fan * n : fan * (n + 1)] for n in range(count)], axis=0)


def transposed(values):
    rows, cols = values.shape
    filler = jnp.zeros((rows, 128 - cols), F32)
    return jnp.transpose(jnp.concatenate([values, filler], axis=1))[:cols]


def order_body(send_ref, bond_ref, h_ref, out_ref, h_out_ref):
    owned = bond_ref.shape[0]
    half = owned // 2
    cap = owned // OFFS
    h_out_ref[...] = h_ref[...]
    bond = jnp.concatenate([bond_ref[:half, :], bond_ref[half:, :]], axis=1)
    send = as_row(send_ref[...])
    low = one_hot(iota((cap, owned), 0) == (send & 127))
    high = send >> 7
    late = iota((32, owned), 1) >= half
    late = dot_nt(low, one_hot((iota((32, owned), 0) == high) & late))

    def masked(o):
        mask = jnp.where(high == o, 1.0, 0.0)
        mask = jnp.broadcast_to(mask, (16, owned)).astype(BF16)
        kept = [low[16 * i : 16 * (i + 1)] * mask for i in range(cap // 16)]
        return [k[:, :half] + k[:, half:] for k in kept]

    for i in range(OFFS // 2):
        both = dot(jnp.concatenate(masked(2 * i) + masked(2 * i + 1), axis=0), bond)
        column = jnp.concatenate([late[:, 2 * i : 2 * i + 1], late[:, 2 * i + 1 : 2 * i + 2]], axis=0)
        out_ref[2 * cap * i : 2 * cap * (i + 1), :] = jnp.where(
            column > 0.5, both[:, 128:], both[:, :128]
        ).astype(BF16)


def slots_body(both_ref, h_ref, adj_ref, pack_ref, h_out_ref):
    fan, atoms = pack_ref.shape
    half = both_ref.shape[0] // 2
    h_out_ref[...] = h_ref[...]
    pack = transposed(folded(as_row(both_ref[:half, :]), atoms, fan)).astype(jnp.int32)
    dist = transposed(folded(as_row(both_ref[half:, :]), atoms, fan))
    pack_ref[...] = pack
    peer = (pack & 63).astype(F32)
    off = ((pack & 2047) >> 6).astype(F32)
    scaled = dist * (1.0 / 7.0)
    env = 1.0 - scaled * scaled
    env = jnp.where(((pack >> 11) & 3) > 0, env * env, 0.0)
    row = fiota((fan, atoms), 0)
    target = off * float(GROUPS) + ranked_among(off)
    env_sorted = jnp.zeros((fan, atoms), F32)
    peer_sorted = jnp.zeros((fan, atoms), F32)
    for s in range(fan):
        here = target[s : s + 1, :] == row
        env_sorted = jnp.where(here, env[s : s + 1, :], env_sorted)
        peer_sorted = jnp.where(here, peer[s : s + 1, :], peer_sorted)
    which = fiota((atoms, atoms), 0)
    parts = []
    for o in range(OFFS):
        part = jnp.zeros((atoms, atoms), F32)
        for t in range(GROUPS * o, GROUPS * (o + 1)):
            part += jnp.where(peer_sorted[t : t + 1, :] == which, env_sorted[t : t + 1, :], 0.0)
        parts.append(part)
    for m in range(OFFS // 2):
        pair = jnp.concatenate([parts[2 * m], parts[2 * m + 1]], axis=0)
        pair = jnp.concatenate([pair, jnp.zeros_like(pair)], axis=1)
        adj_ref[:, 128 * m : 128 * (m + 1)] = jnp.transpose(pair)[:atoms].astype(BF16)


def ranked_among(key):
    fan = key.shape[0]
    row = fiota(key.shape, 0)
    rank = jnp.zeros(key.shape, F32)
    for s in range(fan - 1):
        rank += jnp.where((key == key[s : s + 1, :]) & (row > float(s)), 1.0, 0.0)
    return rank


def write_hots(out_ref, index):
    cap = index.shape[0]
    lane = fiota((cap, 128), 1)
    for o in range(OFFS):
        hot = (lane == index[:, o : o + 1]) | (lane == index[:, 32 + o : 33 + o] + 64.0)
        out_ref[cap * o : cap * (o + 1), :] = one_hot(hot)


def pairs_body(
    send_ref, own_ref, nb_ref, kind_ref, recv_ref, pack_ref, hot_own_ref, hot_mir_ref, place_ref
):
    fan, atoms = pack_ref.shape
    cap = hot_own_ref.shape[0] // OFFS
    send = as_row(send_ref[...])
    own = as_row(own_ref[...]).astype(F32)
    owned = send.shape[1]
    atom_r = jnp.floor((own + 0.5) * (1.0 / fan))
    slot_r = own - fan * atom_r
    off_r = (send >> 7).astype(F32)
    pos_r = (send & 127).astype(F32)
    peer = (pack_ref[...] & 63).astype(F32)
    at_atom = fiota((atoms, owned), 0) == atom_r
    at_slot = fiota((fan, owned), 0) == slot_r
    place_ref[...] = dot_nt(
        one_hot(at_slot), jnp.where(at_atom, pos_r + 1.0, 0.0).astype(BF16)
    )
    peer_all = dot(peer.astype(BF16), one_hot(at_atom))
    peer_r = jnp.sum(jnp.where(at_slot, peer_all, 0.0), axis=0, keepdims=True)
    at_off = fiota((32, owned), 0) == off_r
    values = jnp.concatenate(
        [jnp.where(at_off, atom_r, 0.0), jnp.where(at_off, peer_r, 0.0)], axis=0
    ).astype(BF16)
    write_hots(hot_own_ref, dot_nt(one_hot(fiota((cap, owned), 0) == pos_r), values))

    ids = as_row(jnp.where(kind_ref[...] == 2, nb_ref[...], 64 * 31))
    slots = ids.shape[1]
    atom_s = jnp.floor((fiota((1, slots), 1) + 0.5) * (1.0 / fan))
    peer_s = (ids & 63).astype(F32)
    off_s = (ids >> 6).astype(F32)
    pos_s = as_row(recv_ref[...] & 127).astype(F32)
    at_off = fiota((32, slots), 0) == off_s
    values = jnp.concatenate(
        [jnp.where(at_off, atom_s, 0.0), jnp.where(at_off, peer_s, 0.0)], axis=0
    ).astype(BF16)
    write_hots(hot_mir_ref, dot_nt(one_hot(fiota((cap, slots), 0) == pos_s), values))


def places_body(
    pack_ref, place_ref, wb_ref, pick_own_ref, pick_mir_ref, perm_ref, owned_ref, wcat_ref
):
    fan, atoms = pack_ref.shape
    cap = pick_own_ref.shape[0] // OFFS
    pack = pack_ref[...]
    off = ((pack & 2047) >> 6).astype(F32)
    kind = (pack >> 11) & 3
    pos_in = (pack >> 13).astype(F32)
    place = place_ref[...]
    owned = jnp.where(place > 0.5, 1.0, 0.0)
    owned_ref[...] = owned
    src = jnp.where(kind == 1, place, jnp.where(kind == 2, pos_in + 1.0, 0.0))
    rank = ranked_among(off * 2.0 + owned)
    target = off * float(GROUPS) + (2.0 - 2.0 * owned) + rank
    row = fiota((fan, atoms), 0)
    sorted_src = jnp.zeros((fan, atoms), F32)
    for s in range(fan):
        sorted_src = jnp.where(target[s : s + 1, :] == row, src[s : s + 1, :], sorted_src)
    spread = one_hot((iota((cap, atoms), 0) >> 1) == iota((cap, atoms), 1))
    spread = dot_nt(spread, sorted_src.astype(BF16))
    member = iota((cap, fan), 1) & 3
    parity = iota((cap, fan), 0) & 1
    fold = one_hot((iota((fan, 32), 0) >> 2) == iota((fan, 32), 1))
    lane = fiota((cap, cap), 1)
    for shift, pick_ref in ((0, pick_own_ref), (2, pick_mir_ref)):
        kept = jnp.where(member == parity + shift, spread, 0.0).astype(BF16)
        index = dot(kept, fold) - 1.0
        for o in range(OFFS):
            pick_ref[cap * o : cap * (o + 1), :] = one_hot(index[:, o : o + 1] == lane)

    spot = off * 8.0 + (iota((fan, atoms), 1) & 3).astype(F32) * 2.0 + rank
    lane = fiota((fan, 2 * fan), 1)
    for q in range(atoms // 4):
        perm_ref[4 * fan * q : 4 * fan * (q + 1), :] = jnp.concatenate(
            [jnp.where(spot[:, 4 * q + i : 4 * q + i + 1] == lane, 1.0, 0.0) for i in range(4)],
            axis=0,
        ).astype(BF16)

    block = wb_ref.shape[0]
    row = fiota((block, block), 0)
    col = fiota((block, block), 1)
    major = jnp.floor((row + 0.5) * (1.0 / ORB))
    wcat_ref[:, :128] = wb_ref[...]
    wcat_ref[:, 128:] = dot(
        one_hot((row - ORB * major) * ORB + major == col), wb_ref[...]
    ).astype(BF16)


def node_body(layer):
    def body(adj_ref, other_ref, ghost_ref, wm_ref, wu_ref, gain_ref, out_ref):
        ghosts = ghost_ref.shape[0]
        half = ghosts // 2
        atoms = ghosts // OFFS
        mixed = dot(adj_ref[...], ghost_ref[...])
        other = dot(other_ref[:, :half], ghost_ref[half:, :])
        other += dot(other_ref[:, half:], ghost_ref[:half, :])
        mixed = jnp.concatenate([mixed, other], axis=0).astype(BF16)
        hidden = jnp.concatenate(
            [ghost_ref[atoms * 4 : atoms * 5, :], ghost_ref[atoms * 13 : atoms * 14, :]], axis=0
        )
        summed = (dot(mixed, wm_ref[layer]) * 0.125).astype(BF16)
        updated = hidden.astype(F32) + silu(dot(summed, wu_ref[layer]))
        out_ref[...] = (rms_norm(updated) * gain_ref[layer : layer + 1, :]).astype(BF16)

    return body


CHUNK = 6


def fill_table(ghost_ref, w_local, w_ghost, table):
    atoms = ghost_ref.shape[0] // OFFS
    local = dot(ghost_ref[atoms * 4 : atoms * 5, :], w_local).astype(BF16)
    distant = dot(ghost_ref[...], w_ghost).astype(BF16)
    blank = jnp.zeros((atoms, 128), BF16)
    for o in range(OFFS):
        base = 2 * atoms * o
        table[base : base + atoms, :128] = local
        table[base : base + atoms, 128:] = blank
        table[base + atoms : base + 2 * atoms, :128] = blank
        table[base + atoms : base + 2 * atoms, 128:] = distant[atoms * o : atoms * (o + 1)]


def chosen_product(hot_ref, table, c):
    cap = hot_ref.shape[0] // OFFS
    chosen = jnp.concatenate(
        [
            dot(hot_ref[cap * o : cap * (o + 1), :], table[cap * o : cap * (o + 1), :])
            for o in range(CHUNK * c, CHUNK * (c + 1))
        ],
        axis=0,
    )
    return chosen[:, :128] * chosen[:, 128:]


def edge_all(e_ref, hot_ref, ghost_ref, w_local, w_ghost, w_in, w_out, table, out_ref):
    cap = e_ref.shape[0] // OFFS
    fill_table(ghost_ref, w_local, w_ghost, table)
    for c in range(OFFS // CHUNK):
        span = slice(CHUNK * cap * c, CHUNK * cap * (c + 1))
        state = e_ref[span, :]
        gate = silu(dot(state, w_in) * chosen_product(hot_ref, table, c)).astype(BF16)
        out_ref[span, :] = rms_norm(state.astype(F32) + dot(gate, w_out)).astype(BF16)


def edge_body(layer, hand_on=False):
    def body(e_ref, hot_ref, ghost_ref, wl_ref, wg_ref, wi_ref, wo_ref, *refs):
        if hand_on:
            refs[2][...] = refs[0][...]
            refs = (refs[1], refs[3])
        out_ref, table = refs
        edge_all(
            e_ref, hot_ref, ghost_ref, wl_ref[layer], wg_ref[layer], wi_ref[layer], wo_ref[layer],
            table, out_ref,
        )

    return body


def twice(weight):
    blank = jnp.zeros_like(weight)
    return jnp.concatenate(
        [
            jnp.concatenate([weight, blank], axis=1),
            jnp.concatenate([blank, weight], axis=1),
        ],
        axis=0,
    )


def final_body(layer):
    def body(
        own_ref, mir_ref, ho_ref, hm_ref, ghost_ref, wl_ref, wr_ref, wi_ref, wo_ref,
        po_ref, pm_ref, perm_ref, owned_ref, wcat_ref,
        out_ref, table_own, table_mir, ranked, rows,
    ):
        atoms = ghost_ref.shape[0] // OFFS
        cap = own_ref.shape[0] // OFFS
        fan = out_ref.shape[1] // atoms
        w_in, w_out = twice(wi_ref[layer]), twice(wo_ref[layer])
        fill_table(ghost_ref, wl_ref[layer], wr_ref[layer], table_own)
        fill_table(ghost_ref, wr_ref[layer], wl_ref[layer], table_mir)
        for c in range(OFFS // CHUNK):
            span = slice(CHUNK * cap * c, CHUNK * cap * (c + 1))
            state = jnp.concatenate([own_ref[span, :], mir_ref[span, :]], axis=1)
            chosen = jnp.concatenate(
                [chosen_product(ho_ref, table_own, c), chosen_product(hm_ref, table_mir, c)],
                axis=1,
            )
            gate = silu(dot(state, w_in) * chosen).astype(BF16)
            renewed = state.astype(F32) + dot(gate, w_out)
            e_own = rms_norm(renewed[:, :128]).astype(BF16)
            e_mir = rms_norm(renewed[:, 128:]).astype(BF16)
            for i in range(CHUNK):
                o = CHUNK * c + i
                here = slice(cap * i, cap * (i + 1))
                span = slice(cap * o, cap * (o + 1))
                ranked[span, :128] = dot(po_ref[span, :], e_own[here])
                ranked[span, 128:] = dot(pm_ref[span, :], e_mir[here])
        for q in range(atoms // 4):
            span = slice(4 * fan * q, 4 * fan * (q + 1))
            tiles = jnp.concatenate(
                [ranked[cap * o + 8 * q : cap * o + 8 * (q + 1), :] for o in range(OFFS)], axis=0
            ).astype(BF16)
            spread = dot(perm_ref[span, :], tiles)
            mine = jnp.concatenate(
                [owned_ref[:, 4 * q + i : 4 * q + i + 1] for i in range(4)], axis=0
            )
            mine = mine > 0.5
            rows[span, :128] = jnp.where(mine, spread[:, :128], 0.0).astype(BF16)
            rows[span, 128:] = jnp.where(mine, 0.0, spread[:, 128:]).astype(BF16)
        step = 16 * fan
        for g in range(atoms // 16):
            out_ref[:, step * g : step * (g + 1)] = dot_nt(
                wcat_ref[...], rows[step * g : step * (g + 1), :]
            ).astype(BF16)

    return body


def shards(
    atom_feats, bond_embed, pair_dist, neighbours, slot_kind, own_rows, send_pos, recv_pos,
    w_left, w_right, w_edge_in, w_edge_out, w_msg, w_upd, node_gain, w_block,
):
    atoms, channels = atom_feats.shape
    slots = neighbours.shape[0]
    fan = slots // atoms
    owned = own_rows.shape[0]
    cap = owned // OFFS
    block = w_block.shape[1]
    ghosts = OFFS * atoms

    def array(*shape, dtype=BF16):
        return jax.ShapeDtypeStruct(shape, dtype)

    def tiles(values):
        return values.reshape(-1, 128)

    send, own = tiles(send_pos), tiles(own_rows)
    nb, kind, recv, dist = map(tiles, (neighbours, slot_kind, recv_pos, pair_dist))
    opposite = swapped(atom_feats, "layer")
    both = jnp.concatenate(
        [(nb | (kind << 11) | ((recv & 127) << 13)).astype(F32), dist], axis=0
    )
    adjacency, pack, hidden = call(
        slots_body,
        (array(atoms, ghosts), array(fan, atoms, dtype=jnp.int32), array(atoms, channels)),
        both, atom_feats,
        us=2.0,
    )
    other = swapped(adjacency, "layer")
    sheets = jnp.concatenate([hidden, opposite], axis=0)
    ordered, centre = call(
        order_body,
        (array(owned, channels), array(2 * atoms, channels)),
        send, bond_embed, sheets,
        us=2.0,
    )
    outgoing = ordered.reshape(2, 3, 3, cap, channels)
    crossed = swapped(outgoing[1], "layer")
    shifted = across_rows(outgoing, crossed)
    mirror = across_columns(shifted).reshape(owned, channels)
    hot_own, hot_mir, place = call(
        pairs_body,
        (array(owned, 128), array(owned, 128), array(fan, atoms, dtype=F32)),
        send, own, nb, kind, recv, pack,
        after=(ordered,),
        us=2.5,
    )
    pick_own, pick_mir, perm, mine, w_cat = call(
        places_body,
        (
            array(owned, cap),
            array(owned, cap),
            array(slots, 2 * fan),
            array(fan, atoms, dtype=F32),
            array(block, 2 * channels),
        ),
        pack, place, w_block.T,
        us=2.5,
    )
    table = pltpu.VMEM((2 * ghosts, 2 * channels), BF16)
    state = array(owned, channels)

    def framed_sheets(value):
        return value.reshape(2, 1, 1, atoms, channels)

    def edge(layer, own, after=(), hand_on=()):
        values = (ordered, hot_own) if own else (mirror, hot_mir)
        weights = (w_left, w_right) if own else (w_right, w_left)
        outs = (state, array(2 * atoms, channels)) if hand_on else state
        return call(
            edge_body(layer, bool(hand_on)),
            outs,
            *values, ghosts_at[layer], *weights, w_edge_in, w_edge_out, *hand_on,
            after=after,
            scratch=[table],
            us=1.4,
        )

    def node(layer, after):
        return call(
            node_body(layer),
            array(2 * atoms, channels),
            adjacency, other, ghosts_at[layer], w_msg, w_upd, node_gain,
            after=after,
            us=0.6,
        )

    ghosts_at = [ghosts_of(framed_sheets(sheets), framed_sheets(centre))]
    sheets = node(0, (crossed,))
    ghosts_at.append(ghosts_of(framed_sheets(sheets)))
    ordered = edge(0, True)
    sheets = node(1, (perm, ordered))
    ordered, centre = edge(1, True, after=(shifted,), hand_on=(sheets,))
    mirror = edge(0, False)
    mirror = edge(1, False)
    ghost = ghosts_of(framed_sheets(sheets), framed_sheets(centre))
    return call(
        final_body(2),
        array(block, slots),
        ordered, mirror, hot_own, hot_mir, ghost, w_left, w_right, w_edge_in, w_edge_out,
        pick_own, pick_mir, perm, mine, w_cat,
        scratch=[
            table,
            table,
            pltpu.VMEM((owned, 2 * channels), F32),
            pltpu.VMEM((slots, 2 * channels), BF16),
        ],
        us=7.0,
    )


def solution(mesh):
    axes = ("gx", "gy", "layer")
    rows = P(axes, None)
    flat = P(axes)
    placed = (rows, rows) + (flat,) * 6 + (P(),) * 8
    return jax.shard_map(
        shards,
        mesh=mesh,
        in_specs=placed,
        out_specs=P(None, axes),
        check_vma=False,
    )
```

```python
import jax
import jax.numpy as jnp
from jax import lax
from jax.experimental import pallas as pl
from jax.experimental.pallas import tpu as pltpu
from jax.sharding import PartitionSpec as P

ORB = 13
GROUPS = 4
OFFS = 18
F32 = jnp.float32
BF16 = jnp.bfloat16
VMEM_LIMIT = 24 * 1024 * 1024


def swapped(value, axis):
    return lax.ppermute(value, axis, [(0, 1), (1, 0)])


def moved(value, axis, steps):
    count = lax.axis_size(axis)
    return lax.ppermute(value, axis, [(i, (i + steps) % count) for i in range(count)])


def with_halo(block, axis, dim):
    low = moved(block, axis, 1)
    high = moved(block, axis, -1)
    return jnp.concatenate([low, block, high], axis=dim)


def rows_of(sheets, centre):
    low, high = moved(sheets, "gx", 1), moved(sheets, "gx", -1)
    return jnp.concatenate([low, centre, high], axis=1)


def columns_of(rows, middle=None):
    low, high = moved(rows, "gy", 1), moved(rows, "gy", -1)
    table = jnp.concatenate([low, rows if middle is None else middle, high], axis=2)
    return table.reshape(-1, rows.shape[-1])


def ghosts_of(sheets, centre):
    return columns_of(rows_of(sheets, centre))


def across_rows(sheets):
    rows = [moved(sheets[:, i], "gx", i - 1) if i != 1 else sheets[:, i] for i in (2, 1, 0)]
    return jnp.stack(rows, axis=1)


def across_columns(shifted):
    cols = [moved(shifted[:, :, i], "gy", i - 1) if i != 1 else shifted[:, :, i] for i in (2, 1, 0)]
    return jnp.stack(cols, axis=2)


def dot(a, b):
    return jnp.dot(a, b, preferred_element_type=F32)


def dot_nt(a, b):
    return lax.dot_general(a, b, (((1,), (1,)), ((), ())), preferred_element_type=F32)


def one_hot(mask):
    return jnp.where(mask, 1.0, 0.0).astype(BF16)


def silu(v):
    return v * (0.5 * jnp.tanh(0.5 * v) + 0.5)


def rms_norm(v):
    return v * lax.rsqrt(jnp.mean(v * v, axis=-1, keepdims=True) + 1e-06)


def iota(shape, dim):
    return lax.broadcasted_iota(jnp.int32, shape, dim)


def fiota(shape, dim):
    return iota(shape, dim).astype(F32)


def call(body, outs, *args, after=(), scratch=(), us=1.0):
    used = len(args)

    def ordered_body(*refs):
        body(*refs[:used], *refs[used + len(after) :])

    return pl.pallas_call(
        ordered_body if after else body,
        out_shape=outs,
        in_specs=[pl.BlockSpec(memory_space=pltpu.VMEM)] * used
        + [pl.BlockSpec(memory_space=pl.ANY)] * len(after),
        scratch_shapes=list(scratch),
        compiler_params=pltpu.CompilerParams(vmem_limit_bytes=VMEM_LIMIT),
        cost_estimate=pl.CostEstimate(
            flops=int(us * 1.1e9), bytes_accessed=int(us * 3.6e6), transcendentals=0
        ),
    )(*args, *after)


def as_row(tiles):
    return jnp.concatenate([tiles[i : i + 1] for i in range(tiles.shape[0])], axis=1)


def folded(row, count, fan):
    return jnp.concatenate([row[:, fan * n : fan * (n + 1)] for n in range(count)], axis=0)


def transposed(values):
    rows, cols = values.shape
    filler = jnp.zeros((rows, 128 - cols), F32)
    return jnp.transpose(jnp.concatenate([values, filler], axis=1))[:cols]


def order_body(send_ref, bond_ref, h_ref, out_ref, h_out_ref):
    owned = bond_ref.shape[0]
    half = owned // 2
    cap = owned // OFFS
    h_out_ref[...] = h_ref[...]
    bond = jnp.concatenate([bond_ref[:half, :], bond_ref[half:, :]], axis=1)
    send = as_row(send_ref[...])
    low = one_hot(iota((cap, owned), 0) == (send & 127))
    high = send >> 7
    late = iota((32, owned), 1) >= half
    late = dot_nt(low, one_hot((iota((32, owned), 0) == high) & late))

    def masked(o):
        mask = jnp.where(high == o, 1.0, 0.0)
        mask = jnp.broadcast_to(mask, (16, owned)).astype(BF16)
        kept = [low[16 * i : 16 * (i + 1)] * mask for i in range(cap // 16)]
        return [k[:, :half] + k[:, half:] for k in kept]

    for i in range(OFFS // 2):
        both = dot(jnp.concatenate(masked(2 * i) + masked(2 * i + 1), axis=0), bond)
        column = jnp.concatenate([late[:, 2 * i : 2 * i + 1], late[:, 2 * i + 1 : 2 * i + 2]], axis=0)
        out_ref[2 * cap * i : 2 * cap * (i + 1), :] = jnp.where(
            column > 0.5, both[:, 128:], both[:, :128]
        ).astype(BF16)


def slots_body(both_ref, h_ref, adj_ref, pack_ref, h_out_ref):
    fan, atoms = pack_ref.shape
    half = both_ref.shape[0] // 2
    h_out_ref[...] = h_ref[...]
    pack = transposed(folded(as_row(both_ref[:half, :]), atoms, fan)).astype(jnp.int32)
    dist = transposed(folded(as_row(both_ref[half:, :]), atoms, fan))
    pack_ref[...] = pack
    peer = (pack & 63).astype(F32)
    off = ((pack & 2047) >> 6).astype(F32)
    scaled = dist * (1.0 / 7.0)
    env = 1.0 - scaled * scaled
    env = jnp.where(((pack >> 11) & 3) > 0, env * env, 0.0)
    row = fiota((fan, atoms), 0)
    target = off * float(GROUPS) + ranked_among(off)
    env_sorted = jnp.zeros((fan, atoms), F32)
    peer_sorted = jnp.zeros((fan, atoms), F32)
    for s in range(fan):
        here = target[s : s + 1, :] == row
        env_sorted = jnp.where(here, env[s : s + 1, :], env_sorted)
        peer_sorted = jnp.where(here, peer[s : s + 1, :], peer_sorted)
    which = fiota((atoms, atoms), 0)
    parts = []
    for o in range(OFFS):
        part = jnp.zeros((atoms, atoms), F32)
        for t in range(GROUPS * o, GROUPS * (o + 1)):
            part += jnp.where(peer_sorted[t : t + 1, :] == which, env_sorted[t : t + 1, :], 0.0)
        parts.append(part)
    for m in range(OFFS // 2):
        pair = jnp.concatenate([parts[2 * m], parts[2 * m + 1]], axis=0)
        pair = jnp.concatenate([pair, jnp.zeros_like(pair)], axis=1)
        adj_ref[:, 128 * m : 128 * (m + 1)] = jnp.transpose(pair)[:atoms].astype(BF16)


def ranked_among(key):
    fan = key.shape[0]
    row = fiota(key.shape, 0)
    rank = jnp.zeros(key.shape, F32)
    for s in range(fan - 1):
        rank += jnp.where((key == key[s : s + 1, :]) & (row > float(s)), 1.0, 0.0)
    return rank


def write_hots(out_ref, index):
    cap = index.shape[0]
    lane = fiota((cap, 128), 1)
    for o in range(OFFS):
        hot = (lane == index[:, o : o + 1]) | (lane == index[:, 32 + o : 33 + o] + 64.0)
        out_ref[cap * o : cap * (o + 1), :] = one_hot(hot)


def pairs_body(
    send_ref, own_ref, nb_ref, kind_ref, recv_ref, pack_ref, hot_own_ref, hot_mir_ref, place_ref
):
    fan, atoms = pack_ref.shape
    cap = hot_own_ref.shape[0] // OFFS
    send = as_row(send_ref[...])
    own = as_row(own_ref[...]).astype(F32)
    owned = send.shape[1]
    atom_r = jnp.floor((own + 0.5) * (1.0 / fan))
    slot_r = own - fan * atom_r
    off_r = (send >> 7).astype(F32)
    pos_r = (send & 127).astype(F32)
    peer = (pack_ref[...] & 63).astype(F32)
    at_atom = fiota((atoms, owned), 0) == atom_r
    at_slot = fiota((fan, owned), 0) == slot_r
    place_ref[...] = dot_nt(
        one_hot(at_slot), jnp.where(at_atom, pos_r + 1.0, 0.0).astype(BF16)
    )
    peer_all = dot(peer.astype(BF16), one_hot(at_atom))
    peer_r = jnp.sum(jnp.where(at_slot, peer_all, 0.0), axis=0, keepdims=True)
    at_off = fiota((32, owned), 0) == off_r
    values = jnp.concatenate(
        [jnp.where(at_off, atom_r, 0.0), jnp.where(at_off, peer_r, 0.0)], axis=0
    ).astype(BF16)
    write_hots(hot_own_ref, dot_nt(one_hot(fiota((cap, owned), 0) == pos_r), values))

    ids = as_row(jnp.where(kind_ref[...] == 2, nb_ref[...], 64 * 31))
    slots = ids.shape[1]
    atom_s = jnp.floor((fiota((1, slots), 1) + 0.5) * (1.0 / fan))
    peer_s = (ids & 63).astype(F32)
    off_s = (ids >> 6).astype(F32)
    pos_s = as_row(recv_ref[...] & 127).astype(F32)
    at_off = fiota((32, slots), 0) == off_s
    values = jnp.concatenate(
        [jnp.where(at_off, atom_s, 0.0), jnp.where(at_off, peer_s, 0.0)], axis=0
    ).astype(BF16)
    write_hots(hot_mir_ref, dot_nt(one_hot(fiota((cap, slots), 0) == pos_s), values))


def places_body(
    pack_ref, place_ref, wb_ref, pick_own_ref, pick_mir_ref, perm_ref, owned_ref, wcat_ref
):
    fan, atoms = pack_ref.shape
    cap = pick_own_ref.shape[0] // OFFS
    pack = pack_ref[...]
    off = ((pack & 2047) >> 6).astype(F32)
    kind = (pack >> 11) & 3
    pos_in = (pack >> 13).astype(F32)
    place = place_ref[...]
    owned = jnp.where(place > 0.5, 1.0, 0.0)
    owned_ref[...] = owned
    src = jnp.where(kind == 1, place, jnp.where(kind == 2, pos_in + 1.0, 0.0))
    rank = ranked_among(off * 2.0 + owned)
    target = off * float(GROUPS) + (2.0 - 2.0 * owned) + rank
    row = fiota((fan, atoms), 0)
    sorted_src = jnp.zeros((fan, atoms), F32)
    for s in range(fan):
        sorted_src = jnp.where(target[s : s + 1, :] == row, src[s : s + 1, :], sorted_src)
    spread = one_hot((iota((cap, atoms), 0) >> 1) == iota((cap, atoms), 1))
    spread = dot_nt(spread, sorted_src.astype(BF16))
    member = iota((cap, fan), 1) & 3
    parity = iota((cap, fan), 0) & 1
    fold = one_hot((iota((fan, 32), 0) >> 2) == iota((fan, 32), 1))
    lane = fiota((cap, cap), 1)
    for shift, pick_ref in ((0, pick_own_ref), (2, pick_mir_ref)):
        kept = jnp.where(member == parity + shift, spread, 0.0).astype(BF16)
        index = dot(kept, fold) - 1.0
        for o in range(OFFS):
            pick_ref[cap * o : cap * (o + 1), :] = one_hot(index[:, o : o + 1] == lane)

    spot = off * 8.0 + (iota((fan, atoms), 1) & 3).astype(F32) * 2.0 + rank
    lane = fiota((fan, 2 * fan), 1)
    for q in range(atoms // 4):
        perm_ref[4 * fan * q : 4 * fan * (q + 1), :] = jnp.concatenate(
            [jnp.where(spot[:, 4 * q + i : 4 * q + i + 1] == lane, 1.0, 0.0) for i in range(4)],
            axis=0,
        ).astype(BF16)

    block = wb_ref.shape[0]
    row = fiota((block, block), 0)
    col = fiota((block, block), 1)
    major = jnp.floor((row + 0.5) * (1.0 / ORB))
    wcat_ref[:, :128] = wb_ref[...]
    wcat_ref[:, 128:] = dot(
        one_hot((row - ORB * major) * ORB + major == col), wb_ref[...]
    ).astype(BF16)


def node_body(layer):
    def body(adj_ref, other_ref, ghost_ref, wm_ref, wu_ref, gain_ref, out_ref):
        ghosts = ghost_ref.shape[0]
        half = ghosts // 2
        atoms = ghosts // OFFS
        mixed = dot(adj_ref[...], ghost_ref[...])
        other = dot(other_ref[:, :half], ghost_ref[half:, :])
        other += dot(other_ref[:, half:], ghost_ref[:half, :])
        mixed = jnp.concatenate([mixed, other], axis=0).astype(BF16)
        hidden = jnp.concatenate(
            [ghost_ref[atoms * 4 : atoms * 5, :], ghost_ref[atoms * 13 : atoms * 14, :]], axis=0
        )
        summed = (dot(mixed, wm_ref[layer]) * 0.125).astype(BF16)
        updated = hidden.astype(F32) + silu(dot(summed, wu_ref[layer]))
        out_ref[...] = (rms_norm(updated) * gain_ref[layer : layer + 1, :]).astype(BF16)

    return body


CHUNK = 6


def fill_table(ghost_ref, w_local, w_ghost, table):
    atoms = ghost_ref.shape[0] // OFFS
    local = dot(ghost_ref[atoms * 4 : atoms * 5, :], w_local).astype(BF16)
    distant = dot(ghost_ref[...], w_ghost).astype(BF16)
    blank = jnp.zeros((atoms, 128), BF16)
    for o in range(OFFS):
        base = 2 * atoms * o
        table[base : base + atoms, :128] = local
        table[base : base + atoms, 128:] = blank
        table[base + atoms : base + 2 * atoms, :128] = blank
        table[base + atoms : base + 2 * atoms, 128:] = distant[atoms * o : atoms * (o + 1)]


def chosen_product(hot_ref, table, c):
    cap = hot_ref.shape[0] // OFFS
    chosen = jnp.concatenate(
        [
            dot(hot_ref[cap * o : cap * (o + 1), :], table[cap * o : cap * (o + 1), :])
            for o in range(CHUNK * c, CHUNK * (c + 1))
        ],
        axis=0,
    )
    return chosen[:, :128] * chosen[:, 128:]


def edge_all(e_ref, hot_ref, ghost_ref, w_local, w_ghost, w_in, w_out, table, out_ref):
    cap = e_ref.shape[0] // OFFS
    fill_table(ghost_ref, w_local, w_ghost, table)
    for c in range(OFFS // CHUNK):
        span = slice(CHUNK * cap * c, CHUNK * cap * (c + 1))
        state = e_ref[span, :]
        gate = silu(dot(state, w_in) * chosen_product(hot_ref, table, c)).astype(BF16)
        out_ref[span, :] = rms_norm(state.astype(F32) + dot(gate, w_out)).astype(BF16)


def edge_body(layer, hand_on=False):
    def body(e_ref, hot_ref, ghost_ref, wl_ref, wg_ref, wi_ref, wo_ref, *refs):
        if hand_on:
            refs[2][...] = refs[0][...]
            refs = (refs[1], refs[3])
        out_ref, table = refs
        edge_all(
            e_ref, hot_ref, ghost_ref, wl_ref[layer], wg_ref[layer], wi_ref[layer], wo_ref[layer],
            table, out_ref,
        )

    return body


def twice(weight):
    blank = jnp.zeros_like(weight)
    return jnp.concatenate(
        [
            jnp.concatenate([weight, blank], axis=1),
            jnp.concatenate([blank, weight], axis=1),
        ],
        axis=0,
    )


def final_body(layer):
    def body(
        own_ref, mir_ref, ho_ref, hm_ref, ghost_ref, wl_ref, wr_ref, wi_ref, wo_ref,
        po_ref, pm_ref, perm_ref, owned_ref, wcat_ref,
        out_ref, table_own, table_mir, ranked, rows,
    ):
        atoms = ghost_ref.shape[0] // OFFS
        cap = own_ref.shape[0] // OFFS
        fan = out_ref.shape[1] // atoms
        w_in, w_out = twice(wi_ref[layer]), twice(wo_ref[layer])
        fill_table(ghost_ref, wl_ref[layer], wr_ref[layer], table_own)
        fill_table(ghost_ref, wr_ref[layer], wl_ref[layer], table_mir)
        for c in range(OFFS // CHUNK):
            span = slice(CHUNK * cap * c, CHUNK * cap * (c + 1))
            state = jnp.concatenate([own_ref[span, :], mir_ref[span, :]], axis=1)
            chosen = jnp.concatenate(
                [chosen_product(ho_ref, table_own, c), chosen_product(hm_ref, table_mir, c)],
                axis=1,
            )
            gate = silu(dot(state, w_in) * chosen).astype(BF16)
            renewed = state.astype(F32) + dot(gate, w_out)
            e_own = rms_norm(renewed[:, :128]).astype(BF16)
            e_mir = rms_norm(renewed[:, 128:]).astype(BF16)
            for i in range(CHUNK):
                o = CHUNK * c + i
                here = slice(cap * i, cap * (i + 1))
                span = slice(cap * o, cap * (o + 1))
                ranked[span, :128] = dot(po_ref[span, :], e_own[here])
                ranked[span, 128:] = dot(pm_ref[span, :], e_mir[here])
        for q in range(atoms // 4):
            span = slice(4 * fan * q, 4 * fan * (q + 1))
            tiles = jnp.concatenate(
                [ranked[cap * o + 8 * q : cap * o + 8 * (q + 1), :] for o in range(OFFS)], axis=0
            ).astype(BF16)
            spread = dot(perm_ref[span, :], tiles)
            mine = jnp.concatenate(
                [owned_ref[:, 4 * q + i : 4 * q + i + 1] for i in range(4)], axis=0
            )
            mine = mine > 0.5
            rows[span, :128] = jnp.where(mine, spread[:, :128], 0.0).astype(BF16)
            rows[span, 128:] = jnp.where(mine, 0.0, spread[:, 128:]).astype(BF16)
        step = 16 * fan
        for g in range(atoms // 16):
            out_ref[:, step * g : step * (g + 1)] = dot_nt(
                wcat_ref[...], rows[step * g : step * (g + 1), :]
            ).astype(BF16)

    return body


def shards(
    atom_feats, bond_embed, pair_dist, neighbours, slot_kind, own_rows, send_pos, recv_pos,
    w_left, w_right, w_edge_in, w_edge_out, w_msg, w_upd, node_gain, w_block,
):
    atoms, channels = atom_feats.shape
    slots = neighbours.shape[0]
    fan = slots // atoms
    owned = own_rows.shape[0]
    cap = owned // OFFS
    block = w_block.shape[1]
    ghosts = OFFS * atoms

    def array(*shape, dtype=BF16):
        return jax.ShapeDtypeStruct(shape, dtype)

    def tiles(values):
        return values.reshape(-1, 128)

    send, own = tiles(send_pos), tiles(own_rows)
    nb, kind, recv, dist = map(tiles, (neighbours, slot_kind, recv_pos, pair_dist))
    opposite = swapped(atom_feats, "layer")
    both = jnp.concatenate(
        [(nb | (kind << 11) | ((recv & 127) << 13)).astype(F32), dist], axis=0
    )
    adjacency, pack, hidden = call(
        slots_body,
        (array(atoms, ghosts), array(fan, atoms, dtype=jnp.int32), array(atoms, channels)),
        both, atom_feats,
        us=2.0,
    )
    other = swapped(adjacency, "layer")
    sheets = jnp.concatenate([hidden, opposite], axis=0)
    ordered, centre = call(
        order_body,
        (array(owned, channels), array(2 * atoms, channels)),
        send, bond_embed, sheets,
        us=2.0,
    )
    outgoing = ordered.reshape(2, 3, 3, cap, channels)
    rowed = across_rows(outgoing)
    columned = across_columns(rowed)
    mirror = jnp.stack([columned[0], swapped(columned[1], "layer")]).reshape(owned, channels)
    hot_own, hot_mir, place = call(
        pairs_body,
        (array(owned, 128), array(owned, 128), array(fan, atoms, dtype=F32)),
        send, own, nb, kind, recv, pack,
        after=(ordered,),
        us=2.5,
    )
    pick_own, pick_mir, perm, mine, w_cat = call(
        places_body,
        (
            array(owned, cap),
            array(owned, cap),
            array(slots, 2 * fan),
            array(fan, atoms, dtype=F32),
            array(block, 2 * channels),
        ),
        pack, place, w_block.T,
        us=2.5,
    )
    table = pltpu.VMEM((2 * ghosts, 2 * channels), BF16)
    state = array(owned, channels)

    def framed_sheets(value):
        return value.reshape(2, 1, 1, atoms, channels)

    def edge(layer, own, after=(), hand_on=()):
        values = (ordered, hot_own) if own else (mirror, hot_mir)
        weights = (w_left, w_right) if own else (w_right, w_left)
        outs = (state,) + tuple(array(*v.shape) for v in hand_on) if hand_on else state
        return call(
            edge_body(layer, bool(hand_on)),
            outs,
            *values, ghosts_at[layer], *weights, w_edge_in, w_edge_out, *hand_on,
            after=after,
            scratch=[table],
            us=1.4,
        )

    def node(layer, after):
        return call(
            node_body(layer),
            array(2 * atoms, channels),
            adjacency, other, ghosts_at[layer], w_msg, w_upd, node_gain,
            after=after,
            us=0.6,
        )

    ghosts_at = [ghosts_of(framed_sheets(sheets), framed_sheets(centre))]
    sheets = node(0, (hot_own,))
    ordered, centre = edge(0, True, after=(rowed,), hand_on=(sheets,))
    ghosts_at.append(ghosts_of(framed_sheets(sheets), framed_sheets(centre)))
    sheets = node(1, (perm, columned))
    ordered, centre = edge(1, True, hand_on=(sheets,))
    mirror = edge(0, False)
    rows = rows_of(framed_sheets(sheets), framed_sheets(centre))
    mirror, middle = edge(1, False, hand_on=(rows.reshape(6 * atoms, channels),))
    ghost = columns_of(rows, middle.reshape(rows.shape))
    return call(
        final_body(2),
        array(block, slots),
        ordered, mirror, hot_own, hot_mir, ghost, w_left, w_right, w_edge_in, w_edge_out,
        pick_own, pick_mir, perm, mine, w_cat,
        scratch=[
            table,
            table,
            pltpu.VMEM((owned, 2 * channels), F32),
            pltpu.VMEM((slots, 2 * channels), BF16),
        ],
        us=7.0,
    )


def solution(mesh):
    axes = ("gx", "gy", "layer")
    rows = P(axes, None)
    flat = P(axes)
    placed = (rows, rows) + (flat,) * 6 + (P(),) * 8
    return jax.shard_map(
        shards,
        mesh=mesh,
        in_specs=placed,
        out_specs=P(None, axes),
        check_vma=False,
    )
```

```python
import jax
import jax.numpy as jnp
from jax import lax
from jax.experimental import pallas as pl
from jax.experimental.pallas import tpu as pltpu
from jax.sharding import PartitionSpec as P

ORB = 13
GROUPS = 4
OFFS = 18
F32 = jnp.float32
BF16 = jnp.bfloat16
VMEM_LIMIT = 24 * 1024 * 1024


def swapped(value, axis):
    return lax.ppermute(value, axis, [(0, 1), (1, 0)])


def moved(value, axis, steps):
    count = lax.axis_size(axis)
    return lax.ppermute(value, axis, [(i, (i + steps) % count) for i in range(count)])


def with_halo(block, axis, dim):
    low = moved(block, axis, 1)
    high = moved(block, axis, -1)
    return jnp.concatenate([low, block, high], axis=dim)


def rows_of(sheets, centre):
    low, high = moved(sheets, "gx", 1), moved(sheets, "gx", -1)
    return jnp.concatenate([low, centre, high], axis=1)


def columns_of(rows, middle=None):
    low, high = moved(rows, "gy", 1), moved(rows, "gy", -1)
    table = jnp.concatenate([low, rows if middle is None else middle, high], axis=2)
    return table.reshape(-1, rows.shape[-1])


def ghosts_of(sheets, centre):
    return columns_of(rows_of(sheets, centre))


def across_rows(outgoing, crossed):
    sheets = jnp.stack([outgoing[0], crossed])
    rows = [moved(sheets[:, i], "gx", i - 1) if i != 1 else sheets[:, i] for i in (2, 1, 0)]
    return jnp.stack(rows, axis=1)


def across_columns(shifted):
    cols = [moved(shifted[:, :, i], "gy", i - 1) if i != 1 else shifted[:, :, i] for i in (2, 1, 0)]
    return jnp.stack(cols, axis=2)


def dot(a, b):
    return jnp.dot(a, b, preferred_element_type=F32)


def dot_nt(a, b):
    return lax.dot_general(a, b, (((1,), (1,)), ((), ())), preferred_element_type=F32)


def one_hot(mask):
    return jnp.where(mask, 1.0, 0.0).astype(BF16)


def silu(v):
    return v * (0.5 * jnp.tanh(0.5 * v) + 0.5)


def rms_norm(v):
    return v * lax.rsqrt(jnp.mean(v * v, axis=-1, keepdims=True) + 1e-06)


def iota(shape, dim):
    return lax.broadcasted_iota(jnp.int32, shape, dim)


def fiota(shape, dim):
    return iota(shape, dim).astype(F32)


def call(body, outs, *args, after=(), scratch=(), us=1.0):
    used = len(args)

    def ordered_body(*refs):
        body(*refs[:used], *refs[used + len(after) :])

    return pl.pallas_call(
        ordered_body if after else body,
        out_shape=outs,
        in_specs=[pl.BlockSpec(memory_space=pltpu.VMEM)] * used
        + [pl.BlockSpec(memory_space=pl.ANY)] * len(after),
        scratch_shapes=list(scratch),
        compiler_params=pltpu.CompilerParams(vmem_limit_bytes=VMEM_LIMIT),
        cost_estimate=pl.CostEstimate(
            flops=int(us * 1.1e9), bytes_accessed=int(us * 3.6e6), transcendentals=0
        ),
    )(*args, *after)


def as_row(tiles):
    return jnp.concatenate([tiles[i : i + 1] for i in range(tiles.shape[0])], axis=1)


def folded(row, count, fan):
    return jnp.concatenate([row[:, fan * n : fan * (n + 1)] for n in range(count)], axis=0)


def transposed(values):
    rows, cols = values.shape
    filler = jnp.zeros((rows, 128 - cols), F32)
    return jnp.transpose(jnp.concatenate([values, filler], axis=1))[:cols]


def order_body(send_ref, bond_ref, h_ref, out_ref, h_out_ref):
    owned = bond_ref.shape[0]
    half = owned // 2
    cap = owned // OFFS
    h_out_ref[...] = h_ref[...]
    bond = jnp.concatenate([bond_ref[:half, :], bond_ref[half:, :]], axis=1)
    send = as_row(send_ref[...])
    low = one_hot(iota((cap, owned), 0) == (send & 127))
    high = send >> 7
    late = iota((32, owned), 1) >= half
    late = dot_nt(low, one_hot((iota((32, owned), 0) == high) & late))

    def masked(o):
        mask = jnp.where(high == o, 1.0, 0.0)
        mask = jnp.broadcast_to(mask, (16, owned)).astype(BF16)
        kept = [low[16 * i : 16 * (i + 1)] * mask for i in range(cap // 16)]
        return [k[:, :half] + k[:, half:] for k in kept]

    for i in range(OFFS // 2):
        both = dot(jnp.concatenate(masked(2 * i) + masked(2 * i + 1), axis=0), bond)
        column = jnp.concatenate([late[:, 2 * i : 2 * i + 1], late[:, 2 * i + 1 : 2 * i + 2]], axis=0)
        out_ref[2 * cap * i : 2 * cap * (i + 1), :] = jnp.where(
            column > 0.5, both[:, 128:], both[:, :128]
        ).astype(BF16)


def slots_body(both_ref, h_ref, adj_ref, pack_ref, h_out_ref):
    fan, atoms = pack_ref.shape
    half = both_ref.shape[0] // 2
    h_out_ref[...] = h_ref[...]
    pack = transposed(folded(as_row(both_ref[:half, :]), atoms, fan)).astype(jnp.int32)
    dist = transposed(folded(as_row(both_ref[half:, :]), atoms, fan))
    pack_ref[...] = pack
    peer = (pack & 63).astype(F32)
    off = ((pack & 2047) >> 6).astype(F32)
    scaled = dist * (1.0 / 7.0)
    env = 1.0 - scaled * scaled
    env = jnp.where(((pack >> 11) & 3) > 0, env * env, 0.0)
    row = fiota((fan, atoms), 0)
    target = off * float(GROUPS) + ranked_among(off)
    env_sorted = jnp.zeros((fan, atoms), F32)
    peer_sorted = jnp.zeros((fan, atoms), F32)
    for s in range(fan):
        here = target[s : s + 1, :] == row
        env_sorted = jnp.where(here, env[s : s + 1, :], env_sorted)
        peer_sorted = jnp.where(here, peer[s : s + 1, :], peer_sorted)
    which = fiota((atoms, atoms), 0)
    parts = []
    for o in range(OFFS):
        part = jnp.zeros((atoms, atoms), F32)
        for t in range(GROUPS * o, GROUPS * (o + 1)):
            part += jnp.where(peer_sorted[t : t + 1, :] == which, env_sorted[t : t + 1, :], 0.0)
        parts.append(part)
    for m in range(OFFS // 2):
        pair = jnp.concatenate([parts[2 * m], parts[2 * m + 1]], axis=0)
        pair = jnp.concatenate([pair, jnp.zeros_like(pair)], axis=1)
        adj_ref[:, 128 * m : 128 * (m + 1)] = jnp.transpose(pair)[:atoms].astype(BF16)


def ranked_among(key):
    fan = key.shape[0]
    row = fiota(key.shape, 0)
    rank = jnp.zeros(key.shape, F32)
    for s in range(fan - 1):
        rank += jnp.where((key == key[s : s + 1, :]) & (row > float(s)), 1.0, 0.0)
    return rank


def write_hots(out_ref, index):
    cap = index.shape[0]
    lane = fiota((cap, 128), 1)
    for o in range(OFFS):
        hot = (lane == index[:, o : o + 1]) | (lane == index[:, 32 + o : 33 + o] + 64.0)
        out_ref[cap * o : cap * (o + 1), :] = one_hot(hot)


def pairs_body(
    send_ref, own_ref, nb_ref, kind_ref, recv_ref, pack_ref, hot_own_ref, hot_mir_ref, place_ref
):
    fan, atoms = pack_ref.shape
    cap = hot_own_ref.shape[0] // OFFS
    send = as_row(send_ref[...])
    own = as_row(own_ref[...]).astype(F32)
    owned = send.shape[1]
    atom_r = jnp.floor((own + 0.5) * (1.0 / fan))
    slot_r = own - fan * atom_r
    off_r = (send >> 7).astype(F32)
    pos_r = (send & 127).astype(F32)
    peer = (pack_ref[...] & 63).astype(F32)
    at_atom = fiota((atoms, owned), 0) == atom_r
    at_slot = fiota((fan, owned), 0) == slot_r
    place_ref[...] = dot_nt(
        one_hot(at_slot), jnp.where(at_atom, pos_r + 1.0, 0.0).astype(BF16)
    )
    peer_all = dot(peer.astype(BF16), one_hot(at_atom))
    peer_r = jnp.sum(jnp.where(at_slot, peer_all, 0.0), axis=0, keepdims=True)
    at_off = fiota((32, owned), 0) == off_r
    values = jnp.concatenate(
        [jnp.where(at_off, atom_r, 0.0), jnp.where(at_off, peer_r, 0.0)], axis=0
    ).astype(BF16)
    write_hots(hot_own_ref, dot_nt(one_hot(fiota((cap, owned), 0) == pos_r), values))

    ids = as_row(jnp.where(kind_ref[...] == 2, nb_ref[...], 64 * 31))
    slots = ids.shape[1]
    atom_s = jnp.floor((fiota((1, slots), 1) + 0.5) * (1.0 / fan))
    peer_s = (ids & 63).astype(F32)
    off_s = (ids >> 6).astype(F32)
    pos_s = as_row(recv_ref[...] & 127).astype(F32)
    at_off = fiota((32, slots), 0) == off_s
    values = jnp.concatenate(
        [jnp.where(at_off, atom_s, 0.0), jnp.where(at_off, peer_s, 0.0)], axis=0
    ).astype(BF16)
    write_hots(hot_mir_ref, dot_nt(one_hot(fiota((cap, slots), 0) == pos_s), values))


def places_body(
    pack_ref, place_ref, wb_ref, pick_own_ref, pick_mir_ref, perm_ref, owned_ref, wcat_ref
):
    fan, atoms = pack_ref.shape
    cap = pick_own_ref.shape[0] // OFFS
    pack = pack_ref[...]
    off = ((pack & 2047) >> 6).astype(F32)
    kind = (pack >> 11) & 3
    pos_in = (pack >> 13).astype(F32)
    place = place_ref[...]
    owned = jnp.where(place > 0.5, 1.0, 0.0)
    owned_ref[...] = owned
    src = jnp.where(kind == 1, place, jnp.where(kind == 2, pos_in + 1.0, 0.0))
    rank = ranked_among(off * 2.0 + owned)
    target = off * float(GROUPS) + (2.0 - 2.0 * owned) + rank
    row = fiota((fan, atoms), 0)
    sorted_src = jnp.zeros((fan, atoms), F32)
    for s in range(fan):
        sorted_src = jnp.where(target[s : s + 1, :] == row, src[s : s + 1, :], sorted_src)
    spread = one_hot((iota((cap, atoms), 0) >> 1) == iota((cap, atoms), 1))
    spread = dot_nt(spread, sorted_src.astype(BF16))
    member = iota((cap, fan), 1) & 3
    parity = iota((cap, fan), 0) & 1
    fold = one_hot((iota((fan, 32), 0) >> 2) == iota((fan, 32), 1))
    lane = fiota((cap, cap), 1)
    for shift, pick_ref in ((0, pick_own_ref), (2, pick_mir_ref)):
        kept = jnp.where(member == parity + shift, spread, 0.0).astype(BF16)
        index = dot(kept, fold) - 1.0
        for o in range(OFFS):
            pick_ref[cap * o : cap * (o + 1), :] = one_hot(index[:, o : o + 1] == lane)

    spot = off * 8.0 + (iota((fan, atoms), 1) & 3).astype(F32) * 2.0 + rank
    lane = fiota((fan, 2 * fan), 1)
    for q in range(atoms // 4):
        perm_ref[4 * fan * q : 4 * fan * (q + 1), :] = jnp.concatenate(
            [jnp.where(spot[:, 4 * q + i : 4 * q + i + 1] == lane, 1.0, 0.0) for i in range(4)],
            axis=0,
        ).astype(BF16)

    block = wb_ref.shape[0]
    row = fiota((block, block), 0)
    col = fiota((block, block), 1)
    major = jnp.floor((row + 0.5) * (1.0 / ORB))
    wcat_ref[:, :128] = wb_ref[...]
    wcat_ref[:, 128:] = dot(
        one_hot((row - ORB * major) * ORB + major == col), wb_ref[...]
    ).astype(BF16)


def node_body(layer):
    def body(adj_ref, other_ref, ghost_ref, wm_ref, wu_ref, gain_ref, out_ref):
        ghosts = ghost_ref.shape[0]
        half = ghosts // 2
        atoms = ghosts // OFFS
        mixed = dot(adj_ref[...], ghost_ref[...])
        other = dot(other_ref[:, :half], ghost_ref[half:, :])
        other += dot(other_ref[:, half:], ghost_ref[:half, :])
        mixed = jnp.concatenate([mixed, other], axis=0).astype(BF16)
        hidden = jnp.concatenate(
            [ghost_ref[atoms * 4 : atoms * 5, :], ghost_ref[atoms * 13 : atoms * 14, :]], axis=0
        )
        summed = (dot(mixed, wm_ref[layer]) * 0.125).astype(BF16)
        updated = hidden.astype(F32) + silu(dot(summed, wu_ref[layer]))
        out_ref[...] = (rms_norm(updated) * gain_ref[layer : layer + 1, :]).astype(BF16)

    return body


CHUNK = 6


def fill_table(ghost_ref, w_local, w_ghost, table):
    atoms = ghost_ref.shape[0] // OFFS
    local = dot(ghost_ref[atoms * 4 : atoms * 5, :], w_local).astype(BF16)
    distant = dot(ghost_ref[...], w_ghost).astype(BF16)
    blank = jnp.zeros((atoms, 128), BF16)
    for o in range(OFFS):
        base = 2 * atoms * o
        table[base : base + atoms, :128] = local
        table[base : base + atoms, 128:] = blank
        table[base + atoms : base + 2 * atoms, :128] = blank
        table[base + atoms : base + 2 * atoms, 128:] = distant[atoms * o : atoms * (o + 1)]


def chosen_product(hot_ref, table, c):
    cap = hot_ref.shape[0] // OFFS
    chosen = jnp.concatenate(
        [
            dot(hot_ref[cap * o : cap * (o + 1), :], table[cap * o : cap * (o + 1), :])
            for o in range(CHUNK * c, CHUNK * (c + 1))
        ],
        axis=0,
    )
    return chosen[:, :128] * chosen[:, 128:]


def edge_all(e_ref, hot_ref, ghost_ref, w_local, w_ghost, w_in, w_out, table, out_ref):
    cap = e_ref.shape[0] // OFFS
    fill_table(ghost_ref, w_local, w_ghost, table)
    for c in range(OFFS // CHUNK):
        span = slice(CHUNK * cap * c, CHUNK * cap * (c + 1))
        state = e_ref[span, :]
        gate = silu(dot(state, w_in) * chosen_product(hot_ref, table, c)).astype(BF16)
        out_ref[span, :] = rms_norm(state.astype(F32) + dot(gate, w_out)).astype(BF16)


def edge_body(layer, hand_on=False):
    def body(e_ref, hot_ref, ghost_ref, wl_ref, wg_ref, wi_ref, wo_ref, *refs):
        if hand_on:
            refs[2][...] = refs[0][...]
            refs = (refs[1], refs[3])
        out_ref, table = refs
        edge_all(
            e_ref, hot_ref, ghost_ref, wl_ref[layer], wg_ref[layer], wi_ref[layer], wo_ref[layer],
            table, out_ref,
        )

    return body


def twice(weight):
    blank = jnp.zeros_like(weight)
    return jnp.concatenate(
        [
            jnp.concatenate([weight, blank], axis=1),
            jnp.concatenate([blank, weight], axis=1),
        ],
        axis=0,
    )


def final_body(layer):
    def body(
        own_ref, mir_ref, ho_ref, hm_ref, ghost_ref, wl_ref, wr_ref, wi_ref, wo_ref,
        po_ref, pm_ref, perm_ref, owned_ref, wcat_ref,
        out_ref, table_own, table_mir, ranked, rows,
    ):
        atoms = ghost_ref.shape[0] // OFFS
        cap = own_ref.shape[0] // OFFS
        fan = out_ref.shape[1] // atoms
        w_in, w_out = twice(wi_ref[layer]), twice(wo_ref[layer])
        fill_table(ghost_ref, wl_ref[layer], wr_ref[layer], table_own)
        fill_table(ghost_ref, wr_ref[layer], wl_ref[layer], table_mir)
        for c in range(OFFS // CHUNK):
            span = slice(CHUNK * cap * c, CHUNK * cap * (c + 1))
            state = jnp.concatenate([own_ref[span, :], mir_ref[span, :]], axis=1)
            chosen = jnp.concatenate(
                [chosen_product(ho_ref, table_own, c), chosen_product(hm_ref, table_mir, c)],
                axis=1,
            )
            gate = silu(dot(state, w_in) * chosen).astype(BF16)
            renewed = state.astype(F32) + dot(gate, w_out)
            e_own = rms_norm(renewed[:, :128]).astype(BF16)
            e_mir = rms_norm(renewed[:, 128:]).astype(BF16)
            for i in range(CHUNK):
                o = CHUNK * c + i
                here = slice(cap * i, cap * (i + 1))
                span = slice(cap * o, cap * (o + 1))
                ranked[span, :128] = dot(po_ref[span, :], e_own[here])
                ranked[span, 128:] = dot(pm_ref[span, :], e_mir[here])
        for q in range(atoms // 4):
            span = slice(4 * fan * q, 4 * fan * (q + 1))
            tiles = jnp.concatenate(
                [ranked[cap * o + 8 * q : cap * o + 8 * (q + 1), :] for o in range(OFFS)], axis=0
            ).astype(BF16)
            spread = dot(perm_ref[span, :], tiles)
            mine = jnp.concatenate(
                [owned_ref[:, 4 * q + i : 4 * q + i + 1] for i in range(4)], axis=0
            )
            mine = mine > 0.5
            rows[span, :128] = jnp.where(mine, spread[:, :128], 0.0).astype(BF16)
            rows[span, 128:] = jnp.where(mine, 0.0, spread[:, 128:]).astype(BF16)
        step = 16 * fan
        for g in range(atoms // 16):
            out_ref[:, step * g : step * (g + 1)] = dot_nt(
                wcat_ref[...], rows[step * g : step * (g + 1), :]
            ).astype(BF16)

    return body


def shards(
    atom_feats, bond_embed, pair_dist, neighbours, slot_kind, own_rows, send_pos, recv_pos,
    w_left, w_right, w_edge_in, w_edge_out, w_msg, w_upd, node_gain, w_block,
):
    atoms, channels = atom_feats.shape
    slots = neighbours.shape[0]
    fan = slots // atoms
    owned = own_rows.shape[0]
    cap = owned // OFFS
    block = w_block.shape[1]
    ghosts = OFFS * atoms

    def array(*shape, dtype=BF16):
        return jax.ShapeDtypeStruct(shape, dtype)

    def tiles(values):
        return values.reshape(-1, 128)

    send, own = tiles(send_pos), tiles(own_rows)
    nb, kind, recv, dist = map(tiles, (neighbours, slot_kind, recv_pos, pair_dist))
    opposite = swapped(atom_feats, "layer")
    both = jnp.concatenate(
        [(nb | (kind << 11) | ((recv & 127) << 13)).astype(F32), dist], axis=0
    )
    adjacency, pack, hidden = call(
        slots_body,
        (array(atoms, ghosts), array(fan, atoms, dtype=jnp.int32), array(atoms, channels)),
        both, atom_feats,
        us=2.0,
    )
    other = swapped(adjacency, "layer")
    sheets = jnp.concatenate([hidden, opposite], axis=0)
    ordered, centre = call(
        order_body,
        (array(owned, channels), array(2 * atoms, channels)),
        send, bond_embed, sheets,
        us=2.0,
    )
    outgoing = ordered.reshape(2, 3, 3, cap, channels)
    crossed = swapped(outgoing[1], "layer")
    shifted = across_rows(outgoing, crossed)
    mirror = across_columns(shifted).reshape(owned, channels)
    hot_own, hot_mir, place = call(
        pairs_body,
        (array(owned, 128), array(owned, 128), array(fan, atoms, dtype=F32)),
        send, own, nb, kind, recv, pack,
        after=(ordered,),
        us=2.5,
    )
    pick_own, pick_mir, perm, mine, w_cat = call(
        places_body,
        (
            array(owned, cap),
            array(owned, cap),
            array(slots, 2 * fan),
            array(fan, atoms, dtype=F32),
            array(block, 2 * channels),
        ),
        pack, place, w_block.T,
        us=2.5,
    )
    table = pltpu.VMEM((2 * ghosts, 2 * channels), BF16)
    state = array(owned, channels)

    def framed_sheets(value):
        return value.reshape(2, 1, 1, atoms, channels)

    def edge(layer, own, after=(), hand_on=()):
        values = (ordered, hot_own) if own else (mirror, hot_mir)
        weights = (w_left, w_right) if own else (w_right, w_left)
        outs = (state,) + tuple(array(*v.shape) for v in hand_on) if hand_on else state
        return call(
            edge_body(layer, bool(hand_on)),
            outs,
            *values, ghosts_at[layer], *weights, w_edge_in, w_edge_out, *hand_on,
            after=after,
            scratch=[table],
            us=1.4,
        )

    def node(layer, after):
        return call(
            node_body(layer),
            array(2 * atoms, channels),
            adjacency, other, ghosts_at[layer], w_msg, w_upd, node_gain,
            after=after,
            us=0.6,
        )

    ghosts_at = [ghosts_of(framed_sheets(sheets), framed_sheets(centre))]
    sheets = node(0, (crossed,))
    ghosts_at.append(ghosts_of(framed_sheets(sheets), framed_sheets(sheets)))
    ordered = edge(0, True)
    sheets = node(1, (perm, ordered, shifted))
    ordered, centre = edge(1, True, hand_on=(sheets,))
    mirror = edge(0, False)
    rows = rows_of(framed_sheets(sheets), framed_sheets(centre))
    mirror, middle = edge(1, False, hand_on=(rows.reshape(6 * atoms, channels),))
    ghost = columns_of(rows, middle.reshape(rows.shape))
    return call(
        final_body(2),
        array(block, slots),
        ordered, mirror, hot_own, hot_mir, ghost, w_left, w_right, w_edge_in, w_edge_out,
        pick_own, pick_mir, perm, mine, w_cat,
        scratch=[
            table,
            table,
            pltpu.VMEM((owned, 2 * channels), F32),
            pltpu.VMEM((slots, 2 * channels), BF16),
        ],
        us=7.0,
    )


def solution(mesh):
    axes = ("gx", "gy", "layer")
    rows = P(axes, None)
    flat = P(axes)
    placed = (rows, rows) + (flat,) * 6 + (P(),) * 8
    return jax.shard_map(
        shards,
        mesh=mesh,
        in_specs=placed,
        out_specs=P(None, axes),
        check_vma=False,
    )
```

```python
import jax
import jax.numpy as jnp
from jax import lax
from jax.experimental import pallas as pl
from jax.experimental.pallas import tpu as pltpu
from jax.sharding import PartitionSpec as P

ORB = 13
GROUPS = 4
OFFS = 18
F32 = jnp.float32
BF16 = jnp.bfloat16
VMEM_LIMIT = 24 * 1024 * 1024


def swapped(value, axis):
    return lax.ppermute(value, axis, [(0, 1), (1, 0)])


def moved(value, axis, steps):
    count = lax.axis_size(axis)
    return lax.ppermute(value, axis, [(i, (i + steps) % count) for i in range(count)])


def with_halo(block, axis, dim):
    low = moved(block, axis, 1)
    high = moved(block, axis, -1)
    return jnp.concatenate([low, block, high], axis=dim)


def rows_of(sheets, centre):
    low, high = moved(sheets, "gx", 1), moved(sheets, "gx", -1)
    return jnp.concatenate([low, centre, high], axis=1)


def columns_of(rows, middle=None):
    low, high = moved(rows, "gy", 1), moved(rows, "gy", -1)
    table = jnp.concatenate([low, rows if middle is None else middle, high], axis=2)
    return table.reshape(-1, rows.shape[-1])


def ghosts_of(sheets, centre):
    return columns_of(rows_of(sheets, centre))


def across_rows(blocks):
    return jnp.stack([moved(blocks[i], "gx", i - 1) if i != 1 else blocks[i] for i in (2, 1, 0)])


def across_columns(shifted):
    cols = [moved(shifted[:, :, i], "gy", i - 1) if i != 1 else shifted[:, :, i] for i in (2, 1, 0)]
    return jnp.stack(cols, axis=2)


def dot(a, b):
    return jnp.dot(a, b, preferred_element_type=F32)


def dot_nt(a, b):
    return lax.dot_general(a, b, (((1,), (1,)), ((), ())), preferred_element_type=F32)


def one_hot(mask):
    return jnp.where(mask, 1.0, 0.0).astype(BF16)


def silu(v):
    return v * (0.5 * jnp.tanh(0.5 * v) + 0.5)


def rms_norm(v):
    return v * lax.rsqrt(jnp.mean(v * v, axis=-1, keepdims=True) + 1e-06)


def iota(shape, dim):
    return lax.broadcasted_iota(jnp.int32, shape, dim)


def fiota(shape, dim):
    return iota(shape, dim).astype(F32)


def call(body, outs, *args, after=(), scratch=(), us=1.0):
    used = len(args)

    def ordered_body(*refs):
        body(*refs[:used], *refs[used + len(after) :])

    return pl.pallas_call(
        ordered_body if after else body,
        out_shape=outs,
        in_specs=[pl.BlockSpec(memory_space=pltpu.VMEM)] * used
        + [pl.BlockSpec(memory_space=pl.ANY)] * len(after),
        scratch_shapes=list(scratch),
        compiler_params=pltpu.CompilerParams(vmem_limit_bytes=VMEM_LIMIT),
        cost_estimate=pl.CostEstimate(
            flops=int(us * 1.1e9), bytes_accessed=int(us * 3.6e6), transcendentals=0
        ),
    )(*args, *after)


def as_row(tiles):
    return jnp.concatenate([tiles[i : i + 1] for i in range(tiles.shape[0])], axis=1)


def folded(row, count, fan):
    return jnp.concatenate([row[:, fan * n : fan * (n + 1)] for n in range(count)], axis=0)


def transposed(values):
    rows, cols = values.shape
    filler = jnp.zeros((rows, 128 - cols), F32)
    return jnp.transpose(jnp.concatenate([values, filler], axis=1))[:cols]


def order_body(send_ref, bond_ref, h_ref, out_ref, h_out_ref):
    owned = bond_ref.shape[0]
    half = owned // 2
    cap = owned // OFFS
    h_out_ref[...] = h_ref[...]
    bond = jnp.concatenate([bond_ref[:half, :], bond_ref[half:, :]], axis=1)
    send = as_row(send_ref[...])
    low = one_hot(iota((cap, owned), 0) == (send & 127))
    high = send >> 7
    late = iota((32, owned), 1) >= half
    late = dot_nt(low, one_hot((iota((32, owned), 0) == high) & late))

    def masked(o):
        mask = jnp.where(high == o, 1.0, 0.0)
        mask = jnp.broadcast_to(mask, (16, owned)).astype(BF16)
        kept = [low[16 * i : 16 * (i + 1)] * mask for i in range(cap // 16)]
        return [k[:, :half] + k[:, half:] for k in kept]

    for i in range(OFFS // 2):
        both = dot(jnp.concatenate(masked(2 * i) + masked(2 * i + 1), axis=0), bond)
        column = jnp.concatenate([late[:, 2 * i : 2 * i + 1], late[:, 2 * i + 1 : 2 * i + 2]], axis=0)
        out_ref[2 * cap * i : 2 * cap * (i + 1), :] = jnp.where(
            column > 0.5, both[:, 128:], both[:, :128]
        ).astype(BF16)


def slots_body(both_ref, h_ref, adj_ref, pack_ref, h_out_ref):
    fan, atoms = pack_ref.shape
    half = both_ref.shape[0] // 2
    h_out_ref[...] = h_ref[...]
    pack = transposed(folded(as_row(both_ref[:half, :]), atoms, fan)).astype(jnp.int32)
    dist = transposed(folded(as_row(both_ref[half:, :]), atoms, fan))
    pack_ref[...] = pack
    peer = (pack & 63).astype(F32)
    off = ((pack & 2047) >> 6).astype(F32)
    scaled = dist * (1.0 / 7.0)
    env = 1.0 - scaled * scaled
    env = jnp.where(((pack >> 11) & 3) > 0, env * env, 0.0)
    row = fiota((fan, atoms), 0)
    target = off * float(GROUPS) + ranked_among(off)
    env_sorted = jnp.zeros((fan, atoms), F32)
    peer_sorted = jnp.zeros((fan, atoms), F32)
    for s in range(fan):
        here = target[s : s + 1, :] == row
        env_sorted = jnp.where(here, env[s : s + 1, :], env_sorted)
        peer_sorted = jnp.where(here, peer[s : s + 1, :], peer_sorted)
    which = fiota((atoms, atoms), 0)
    parts = []
    for o in range(OFFS):
        part = jnp.zeros((atoms, atoms), F32)
        for t in range(GROUPS * o, GROUPS * (o + 1)):
            part += jnp.where(peer_sorted[t : t + 1, :] == which, env_sorted[t : t + 1, :], 0.0)
        parts.append(part)
    for m in range(OFFS // 2):
        pair = jnp.concatenate([parts[2 * m], parts[2 * m + 1]], axis=0)
        pair = jnp.concatenate([pair, jnp.zeros_like(pair)], axis=1)
        adj_ref[:, 128 * m : 128 * (m + 1)] = jnp.transpose(pair)[:atoms].astype(BF16)


def ranked_among(key):
    fan = key.shape[0]
    row = fiota(key.shape, 0)
    rank = jnp.zeros(key.shape, F32)
    for s in range(fan - 1):
        rank += jnp.where((key == key[s : s + 1, :]) & (row > float(s)), 1.0, 0.0)
    return rank


def write_hots(out_ref, index):
    cap = index.shape[0]
    lane = fiota((cap, 128), 1)
    for o in range(OFFS):
        hot = (lane == index[:, o : o + 1]) | (lane == index[:, 32 + o : 33 + o] + 64.0)
        out_ref[cap * o : cap * (o + 1), :] = one_hot(hot)


def pairs_body(
    send_ref, own_ref, nb_ref, kind_ref, recv_ref, pack_ref, e_ref,
    hot_own_ref, hot_mir_ref, place_ref, near_ref,
):
    near_ref[...] = e_ref[: near_ref.shape[0], :]
    fan, atoms = pack_ref.shape
    cap = hot_own_ref.shape[0] // OFFS
    send = as_row(send_ref[...])
    own = as_row(own_ref[...]).astype(F32)
    owned = send.shape[1]
    atom_r = jnp.floor((own + 0.5) * (1.0 / fan))
    slot_r = own - fan * atom_r
    off_r = (send >> 7).astype(F32)
    pos_r = (send & 127).astype(F32)
    peer = (pack_ref[...] & 63).astype(F32)
    at_atom = fiota((atoms, owned), 0) == atom_r
    at_slot = fiota((fan, owned), 0) == slot_r
    place_ref[...] = dot_nt(
        one_hot(at_slot), jnp.where(at_atom, pos_r + 1.0, 0.0).astype(BF16)
    )
    peer_all = dot(peer.astype(BF16), one_hot(at_atom))
    peer_r = jnp.sum(jnp.where(at_slot, peer_all, 0.0), axis=0, keepdims=True)
    at_off = fiota((32, owned), 0) == off_r
    values = jnp.concatenate(
        [jnp.where(at_off, atom_r, 0.0), jnp.where(at_off, peer_r, 0.0)], axis=0
    ).astype(BF16)
    write_hots(hot_own_ref, dot_nt(one_hot(fiota((cap, owned), 0) == pos_r), values))

    ids = as_row(jnp.where(kind_ref[...] == 2, nb_ref[...], 64 * 31))
    slots = ids.shape[1]
    atom_s = jnp.floor((fiota((1, slots), 1) + 0.5) * (1.0 / fan))
    peer_s = (ids & 63).astype(F32)
    off_s = (ids >> 6).astype(F32)
    pos_s = as_row(recv_ref[...] & 127).astype(F32)
    at_off = fiota((32, slots), 0) == off_s
    values = jnp.concatenate(
        [jnp.where(at_off, atom_s, 0.0), jnp.where(at_off, peer_s, 0.0)], axis=0
    ).astype(BF16)
    write_hots(hot_mir_ref, dot_nt(one_hot(fiota((cap, slots), 0) == pos_s), values))


def places_body(
    pack_ref, place_ref, wb_ref, pick_own_ref, pick_mir_ref, perm_ref, owned_ref, wcat_ref
):
    fan, atoms = pack_ref.shape
    cap = pick_own_ref.shape[0] // OFFS
    pack = pack_ref[...]
    off = ((pack & 2047) >> 6).astype(F32)
    kind = (pack >> 11) & 3
    pos_in = (pack >> 13).astype(F32)
    place = place_ref[...]
    owned = jnp.where(place > 0.5, 1.0, 0.0)
    owned_ref[...] = owned
    src = jnp.where(kind == 1, place, jnp.where(kind == 2, pos_in + 1.0, 0.0))
    rank = ranked_among(off * 2.0 + owned)
    target = off * float(GROUPS) + (2.0 - 2.0 * owned) + rank
    row = fiota((fan, atoms), 0)
    sorted_src = jnp.zeros((fan, atoms), F32)
    for s in range(fan):
        sorted_src = jnp.where(target[s : s + 1, :] == row, src[s : s + 1, :], sorted_src)
    spread = one_hot((iota((cap, atoms), 0) >> 1) == iota((cap, atoms), 1))
    spread = dot_nt(spread, sorted_src.astype(BF16))
    member = iota((cap, fan), 1) & 3
    parity = iota((cap, fan), 0) & 1
    fold = one_hot((iota((fan, 32), 0) >> 2) == iota((fan, 32), 1))
    lane = fiota((cap, cap), 1)
    for shift, pick_ref in ((0, pick_own_ref), (2, pick_mir_ref)):
        kept = jnp.where(member == parity + shift, spread, 0.0).astype(BF16)
        index = dot(kept, fold) - 1.0
        for o in range(OFFS):
            pick_ref[cap * o : cap * (o + 1), :] = one_hot(index[:, o : o + 1] == lane)

    spot = off * 8.0 + (iota((fan, atoms), 1) & 3).astype(F32) * 2.0 + rank
    lane = fiota((fan, 2 * fan), 1)
    for q in range(atoms // 4):
        perm_ref[4 * fan * q : 4 * fan * (q + 1), :] = jnp.concatenate(
            [jnp.where(spot[:, 4 * q + i : 4 * q + i + 1] == lane, 1.0, 0.0) for i in range(4)],
            axis=0,
        ).astype(BF16)

    block = wb_ref.shape[0]
    row = fiota((block, block), 0)
    col = fiota((block, block), 1)
    major = jnp.floor((row + 0.5) * (1.0 / ORB))
    wcat_ref[:, :128] = wb_ref[...]
    wcat_ref[:, 128:] = dot(
        one_hot((row - ORB * major) * ORB + major == col), wb_ref[...]
    ).astype(BF16)


def node_body(layer):
    def body(adj_ref, other_ref, ghost_ref, wm_ref, wu_ref, gain_ref, out_ref):
        ghosts = ghost_ref.shape[0]
        half = ghosts // 2
        atoms = ghosts // OFFS
        mixed = dot(adj_ref[...], ghost_ref[...])
        other = dot(other_ref[:, :half], ghost_ref[half:, :])
        other += dot(other_ref[:, half:], ghost_ref[:half, :])
        mixed = jnp.concatenate([mixed, other], axis=0).astype(BF16)
        hidden = jnp.concatenate(
            [ghost_ref[atoms * 4 : atoms * 5, :], ghost_ref[atoms * 13 : atoms * 14, :]], axis=0
        )
        summed = (dot(mixed, wm_ref[layer]) * 0.125).astype(BF16)
        updated = hidden.astype(F32) + silu(dot(summed, wu_ref[layer]))
        out_ref[...] = (rms_norm(updated) * gain_ref[layer : layer + 1, :]).astype(BF16)

    return body


CHUNK = 6


def fill_table(ghost_ref, w_local, w_ghost, table):
    atoms = ghost_ref.shape[0] // OFFS
    local = dot(ghost_ref[atoms * 4 : atoms * 5, :], w_local).astype(BF16)
    distant = dot(ghost_ref[...], w_ghost).astype(BF16)
    blank = jnp.zeros((atoms, 128), BF16)
    for o in range(OFFS):
        base = 2 * atoms * o
        table[base : base + atoms, :128] = local
        table[base : base + atoms, 128:] = blank
        table[base + atoms : base + 2 * atoms, :128] = blank
        table[base + atoms : base + 2 * atoms, 128:] = distant[atoms * o : atoms * (o + 1)]


def chosen_product(hot_ref, table, c):
    cap = hot_ref.shape[0] // OFFS
    chosen = jnp.concatenate(
        [
            dot(hot_ref[cap * o : cap * (o + 1), :], table[cap * o : cap * (o + 1), :])
            for o in range(CHUNK * c, CHUNK * (c + 1))
        ],
        axis=0,
    )
    return chosen[:, :128] * chosen[:, 128:]


def edge_all(e_ref, hot_ref, ghost_ref, w_local, w_ghost, w_in, w_out, table, out_ref):
    cap = e_ref.shape[0] // OFFS
    fill_table(ghost_ref, w_local, w_ghost, table)
    for c in range(OFFS // CHUNK):
        span = slice(CHUNK * cap * c, CHUNK * cap * (c + 1))
        state = e_ref[span, :]
        gate = silu(dot(state, w_in) * chosen_product(hot_ref, table, c)).astype(BF16)
        out_ref[span, :] = rms_norm(state.astype(F32) + dot(gate, w_out)).astype(BF16)


def edge_body(layer, hand_on=False):
    def body(e_ref, hot_ref, ghost_ref, wl_ref, wg_ref, wi_ref, wo_ref, *refs):
        if hand_on:
            refs[2][...] = refs[0][...]
            refs = (refs[1], refs[3])
        out_ref, table = refs
        edge_all(
            e_ref, hot_ref, ghost_ref, wl_ref[layer], wg_ref[layer], wi_ref[layer], wo_ref[layer],
            table, out_ref,
        )

    return body


def twice(weight):
    blank = jnp.zeros_like(weight)
    return jnp.concatenate(
        [
            jnp.concatenate([weight, blank], axis=1),
            jnp.concatenate([blank, weight], axis=1),
        ],
        axis=0,
    )


def final_body(layer):
    def body(
        own_ref, mir_ref, ho_ref, hm_ref, ghost_ref, wl_ref, wr_ref, wi_ref, wo_ref,
        po_ref, pm_ref, perm_ref, owned_ref, wcat_ref,
        out_ref, table_own, table_mir, ranked, rows,
    ):
        atoms = ghost_ref.shape[0] // OFFS
        cap = own_ref.shape[0] // OFFS
        fan = out_ref.shape[1] // atoms
        w_in, w_out = twice(wi_ref[layer]), twice(wo_ref[layer])
        fill_table(ghost_ref, wl_ref[layer], wr_ref[layer], table_own)
        fill_table(ghost_ref, wr_ref[layer], wl_ref[layer], table_mir)
        for c in range(OFFS // CHUNK):
            span = slice(CHUNK * cap * c, CHUNK * cap * (c + 1))
            state = jnp.concatenate([own_ref[span, :], mir_ref[span, :]], axis=1)
            chosen = jnp.concatenate(
                [chosen_product(ho_ref, table_own, c), chosen_product(hm_ref, table_mir, c)],
                axis=1,
            )
            gate = silu(dot(state, w_in) * chosen).astype(BF16)
            renewed = state.astype(F32) + dot(gate, w_out)
            e_own = rms_norm(renewed[:, :128]).astype(BF16)
            e_mir = rms_norm(renewed[:, 128:]).astype(BF16)
            for i in range(CHUNK):
                o = CHUNK * c + i
                here = slice(cap * i, cap * (i + 1))
                span = slice(cap * o, cap * (o + 1))
                ranked[span, :128] = dot(po_ref[span, :], e_own[here])
                ranked[span, 128:] = dot(pm_ref[span, :], e_mir[here])
        for q in range(atoms // 4):
            span = slice(4 * fan * q, 4 * fan * (q + 1))
            tiles = jnp.concatenate(
                [ranked[cap * o + 8 * q : cap * o + 8 * (q + 1), :] for o in range(OFFS)], axis=0
            ).astype(BF16)
            spread = dot(perm_ref[span, :], tiles)
            mine = jnp.concatenate(
                [owned_ref[:, 4 * q + i : 4 * q + i + 1] for i in range(4)], axis=0
            )
            mine = mine > 0.5
            rows[span, :128] = jnp.where(mine, spread[:, :128], 0.0).astype(BF16)
            rows[span, 128:] = jnp.where(mine, 0.0, spread[:, 128:]).astype(BF16)
        step = 16 * fan
        for g in range(atoms // 16):
            out_ref[:, step * g : step * (g + 1)] = dot_nt(
                wcat_ref[...], rows[step * g : step * (g + 1), :]
            ).astype(BF16)

    return body


def shards(
    atom_feats, bond_embed, pair_dist, neighbours, slot_kind, own_rows, send_pos, recv_pos,
    w_left, w_right, w_edge_in, w_edge_out, w_msg, w_upd, node_gain, w_block,
):
    atoms, channels = atom_feats.shape
    slots = neighbours.shape[0]
    fan = slots // atoms
    owned = own_rows.shape[0]
    cap = owned // OFFS
    block = w_block.shape[1]
    ghosts = OFFS * atoms

    def array(*shape, dtype=BF16):
        return jax.ShapeDtypeStruct(shape, dtype)

    def tiles(values):
        return values.reshape(-1, 128)

    send, own = tiles(send_pos), tiles(own_rows)
    nb, kind, recv, dist = map(tiles, (neighbours, slot_kind, recv_pos, pair_dist))
    opposite = swapped(atom_feats, "layer")
    both = jnp.concatenate(
        [(nb | (kind << 11) | ((recv & 127) << 13)).astype(F32), dist], axis=0
    )
    adjacency, pack, hidden = call(
        slots_body,
        (array(atoms, ghosts), array(fan, atoms, dtype=jnp.int32), array(atoms, channels)),
        both, atom_feats,
        us=2.0,
    )
    other = swapped(adjacency, "layer")
    sheets = jnp.concatenate([hidden, opposite], axis=0)
    ordered, centre = call(
        order_body,
        (array(owned, channels), array(2 * atoms, channels)),
        send, bond_embed, sheets,
        us=2.0,
    )
    outgoing = ordered.reshape(2, 3, 3, cap, channels)
    crossed = swapped(outgoing[1], "layer")
    hot_own, hot_mir, place, near = call(
        pairs_body,
        (
            array(owned, 128),
            array(owned, 128),
            array(fan, atoms, dtype=F32),
            array(owned // 2, channels),
        ),
        send, own, nb, kind, recv, pack, ordered,
        after=(other,),
        us=2.5,
    )
    near_rows = across_rows(near.reshape(3, 3, cap, channels))
    shifted = jnp.stack([near_rows, across_rows(crossed)])
    mirror = across_columns(shifted).reshape(owned, channels)
    rows = rows_of(
        sheets.reshape(2, 1, 1, atoms, channels), centre.reshape(2, 1, 1, atoms, channels)
    )
    pick_own, pick_mir, perm, mine, w_cat = call(
        places_body,
        (
            array(owned, cap),
            array(owned, cap),
            array(slots, 2 * fan),
            array(fan, atoms, dtype=F32),
            array(block, 2 * channels),
        ),
        pack, place, w_block.T,
        after=(rows,),
        us=2.5,
    )
    table = pltpu.VMEM((2 * ghosts, 2 * channels), BF16)
    state = array(owned, channels)

    def framed_sheets(value):
        return value.reshape(2, 1, 1, atoms, channels)

    def edge(layer, own, after=(), hand_on=()):
        values = (ordered, hot_own) if own else (mirror, hot_mir)
        weights = (w_left, w_right) if own else (w_right, w_left)
        outs = (state,) + tuple(array(*v.shape) for v in hand_on) if hand_on else state
        return call(
            edge_body(layer, bool(hand_on)),
            outs,
            *values, ghosts_at[layer], *weights, w_edge_in, w_edge_out, *hand_on,
            after=after,
            scratch=[table],
            us=1.4,
        )

    def node(layer, after):
        return call(
            node_body(layer),
            array(2 * atoms, channels),
            adjacency, other, ghosts_at[layer], w_msg, w_upd, node_gain,
            after=after,
            us=0.6,
        )

    ghosts_at = [columns_of(rows)]
    sheets = node(0, (crossed, near_rows))
    ghosts_at.append(ghosts_of(framed_sheets(sheets), framed_sheets(sheets)))
    ordered = edge(0, True, after=(sheets,))
    sheets = node(1, (perm, ordered, shifted))
    ordered, centre = edge(1, True, hand_on=(sheets,))
    mirror = edge(0, False)
    rows = rows_of(framed_sheets(sheets), framed_sheets(centre))
    mirror, middle = edge(1, False, hand_on=(rows.reshape(6 * atoms, channels),))
    ghost = columns_of(rows, middle.reshape(rows.shape))
    return call(
        final_body(2),
        array(block, slots),
        ordered, mirror, hot_own, hot_mir, ghost, w_left, w_right, w_edge_in, w_edge_out,
        pick_own, pick_mir, perm, mine, w_cat,
        scratch=[
            table,
            table,
            pltpu.VMEM((owned, 2 * channels), F32),
            pltpu.VMEM((slots, 2 * channels), BF16),
        ],
        us=7.0,
    )


def solution(mesh):
    axes = ("gx", "gy", "layer")
    rows = P(axes, None)
    flat = P(axes)
    placed = (rows, rows) + (flat,) * 6 + (P(),) * 8
    return jax.shard_map(
        shards,
        mesh=mesh,
        in_specs=placed,
        out_specs=P(None, axes),
        check_vma=False,
    )
```

```python
import jax
import jax.numpy as jnp
from jax import lax
from jax.experimental import pallas as pl
from jax.experimental.pallas import tpu as pltpu
from jax.sharding import PartitionSpec as P

ORB = 13
GROUPS = 4
OFFS = 18
F32 = jnp.float32
BF16 = jnp.bfloat16
VMEM_LIMIT = 24 * 1024 * 1024


def swapped(value, axis):
    return lax.ppermute(value, axis, [(0, 1), (1, 0)])


def moved(value, axis, steps):
    count = lax.axis_size(axis)
    return lax.ppermute(value, axis, [(i, (i + steps) % count) for i in range(count)])


def with_halo(block, axis, dim):
    low = moved(block, axis, 1)
    high = moved(block, axis, -1)
    return jnp.concatenate([low, block, high], axis=dim)


def rows_of(sheets, centre):
    low, high = moved(sheets, "gx", 1), moved(sheets, "gx", -1)
    return jnp.concatenate([low, centre, high], axis=1)


def columns_of(rows, middle=None):
    low, high = moved(rows, "gy", 1), moved(rows, "gy", -1)
    table = jnp.concatenate([low, rows if middle is None else middle, high], axis=2)
    return table.reshape(-1, rows.shape[-1])


def ghosts_of(sheets, centre):
    return columns_of(rows_of(sheets, centre))


def across_rows(outgoing, crossed):
    sheets = jnp.stack([outgoing[0], crossed])
    rows = [moved(sheets[:, i], "gx", i - 1) if i != 1 else sheets[:, i] for i in (2, 1, 0)]
    return jnp.stack(rows, axis=1)


def across_columns(shifted):
    cols = [moved(shifted[:, :, i], "gy", i - 1) if i != 1 else shifted[:, :, i] for i in (2, 1, 0)]
    return jnp.stack(cols, axis=2)


def dot(a, b):
    return jnp.dot(a, b, preferred_element_type=F32)


def dot_nt(a, b):
    return lax.dot_general(a, b, (((1,), (1,)), ((), ())), preferred_element_type=F32)


def one_hot(mask):
    return jnp.where(mask, 1.0, 0.0).astype(BF16)


def silu(v):
    return v * (0.5 * jnp.tanh(0.5 * v) + 0.5)


def rms_norm(v):
    return v * lax.rsqrt(jnp.mean(v * v, axis=-1, keepdims=True) + 1e-06)


def iota(shape, dim):
    return lax.broadcasted_iota(jnp.int32, shape, dim)


def fiota(shape, dim):
    return iota(shape, dim).astype(F32)


def call(body, outs, *args, after=(), scratch=(), us=1.0):
    used = len(args)

    def ordered_body(*refs):
        body(*refs[:used], *refs[used + len(after) :])

    return pl.pallas_call(
        ordered_body if after else body,
        out_shape=outs,
        in_specs=[pl.BlockSpec(memory_space=pltpu.VMEM)] * used
        + [pl.BlockSpec(memory_space=pl.ANY)] * len(after),
        scratch_shapes=list(scratch),
        compiler_params=pltpu.CompilerParams(vmem_limit_bytes=VMEM_LIMIT),
        cost_estimate=pl.CostEstimate(
            flops=int(us * 1.1e9), bytes_accessed=int(us * 3.6e6), transcendentals=0
        ),
    )(*args, *after)


def as_row(tiles):
    return jnp.concatenate([tiles[i : i + 1] for i in range(tiles.shape[0])], axis=1)


def folded(row, count, fan):
    return jnp.concatenate([row[:, fan * n : fan * (n + 1)] for n in range(count)], axis=0)


def transposed(values):
    rows, cols = values.shape
    filler = jnp.zeros((rows, 128 - cols), F32)
    return jnp.transpose(jnp.concatenate([values, filler], axis=1))[:cols]


def order_body(send_ref, bond_ref, h_ref, out_ref, h_out_ref):
    owned = bond_ref.shape[0]
    half = owned // 2
    cap = owned // OFFS
    h_out_ref[...] = h_ref[...]
    bond = jnp.concatenate([bond_ref[:half, :], bond_ref[half:, :]], axis=1)
    send = as_row(send_ref[...])
    low = one_hot(iota((cap, owned), 0) == (send & 127))
    high = send >> 7
    late = iota((32, owned), 1) >= half
    late = dot_nt(low, one_hot((iota((32, owned), 0) == high) & late))

    def masked(o):
        mask = jnp.where(high == o, 1.0, 0.0)
        mask = jnp.broadcast_to(mask, (16, owned)).astype(BF16)
        kept = [low[16 * i : 16 * (i + 1)] * mask for i in range(cap // 16)]
        return [k[:, :half] + k[:, half:] for k in kept]

    for i in range(OFFS // 2):
        both = dot(jnp.concatenate(masked(2 * i) + masked(2 * i + 1), axis=0), bond)
        column = jnp.concatenate([late[:, 2 * i : 2 * i + 1], late[:, 2 * i + 1 : 2 * i + 2]], axis=0)
        out_ref[2 * cap * i : 2 * cap * (i + 1), :] = jnp.where(
            column > 0.5, both[:, 128:], both[:, :128]
        ).astype(BF16)


def slots_body(both_ref, h_ref, adj_ref, pack_ref, h_out_ref):
    fan, atoms = pack_ref.shape
    half = both_ref.shape[0] // 2
    h_out_ref[...] = h_ref[...]
    pack = transposed(folded(as_row(both_ref[:half, :]), atoms, fan)).astype(jnp.int32)
    dist = transposed(folded(as_row(both_ref[half:, :]), atoms, fan))
    pack_ref[...] = pack
    peer = (pack & 63).astype(F32)
    off = ((pack & 2047) >> 6).astype(F32)
    scaled = dist * (1.0 / 7.0)
    env = 1.0 - scaled * scaled
    env = jnp.where(((pack >> 11) & 3) > 0, env * env, 0.0)
    row = fiota((fan, atoms), 0)
    target = off * float(GROUPS) + ranked_among(off)
    env_sorted = jnp.zeros((fan, atoms), F32)
    peer_sorted = jnp.zeros((fan, atoms), F32)
    for s in range(fan):
        here = target[s : s + 1, :] == row
        env_sorted = jnp.where(here, env[s : s + 1, :], env_sorted)
        peer_sorted = jnp.where(here, peer[s : s + 1, :], peer_sorted)
    which = fiota((atoms, atoms), 0)
    parts = []
    for o in range(OFFS):
        part = jnp.zeros((atoms, atoms), F32)
        for t in range(GROUPS * o, GROUPS * (o + 1)):
            part += jnp.where(peer_sorted[t : t + 1, :] == which, env_sorted[t : t + 1, :], 0.0)
        parts.append(part)
    for m in range(OFFS // 2):
        pair = jnp.concatenate([parts[2 * m], parts[2 * m + 1]], axis=0)
        pair = jnp.concatenate([pair, jnp.zeros_like(pair)], axis=1)
        adj_ref[:, 128 * m : 128 * (m + 1)] = jnp.transpose(pair)[:atoms].astype(BF16)


def ranked_among(key):
    fan = key.shape[0]
    row = fiota(key.shape, 0)
    rank = jnp.zeros(key.shape, F32)
    for s in range(fan - 1):
        rank += jnp.where((key == key[s : s + 1, :]) & (row > float(s)), 1.0, 0.0)
    return rank


def write_hots(out_ref, index):
    cap = index.shape[0]
    lane = fiota((cap, 128), 1)
    for o in range(OFFS):
        hot = (lane == index[:, o : o + 1]) | (lane == index[:, 32 + o : 33 + o] + 64.0)
        out_ref[cap * o : cap * (o + 1), :] = one_hot(hot)


def pairs_body(
    send_ref, own_ref, nb_ref, kind_ref, recv_ref, pack_ref, hot_own_ref, hot_mir_ref, place_ref
):
    fan, atoms = pack_ref.shape
    cap = hot_own_ref.shape[0] // OFFS
    send = as_row(send_ref[...])
    own = as_row(own_ref[...]).astype(F32)
    owned = send.shape[1]
    atom_r = jnp.floor((own + 0.5) * (1.0 / fan))
    slot_r = own - fan * atom_r
    off_r = (send >> 7).astype(F32)
    pos_r = (send & 127).astype(F32)
    peer = (pack_ref[...] & 63).astype(F32)
    at_atom = fiota((atoms, owned), 0) == atom_r
    at_slot = fiota((fan, owned), 0) == slot_r
    place_ref[...] = dot_nt(
        one_hot(at_slot), jnp.where(at_atom, pos_r + 1.0, 0.0).astype(BF16)
    )
    peer_all = dot(peer.astype(BF16), one_hot(at_atom))
    peer_r = jnp.sum(jnp.where(at_slot, peer_all, 0.0), axis=0, keepdims=True)
    at_off = fiota((32, owned), 0) == off_r
    values = jnp.concatenate(
        [jnp.where(at_off, atom_r, 0.0), jnp.where(at_off, peer_r, 0.0)], axis=0
    ).astype(BF16)
    write_hots(hot_own_ref, dot_nt(one_hot(fiota((cap, owned), 0) == pos_r), values))

    ids = as_row(jnp.where(kind_ref[...] == 2, nb_ref[...], 64 * 31))
    slots = ids.shape[1]
    atom_s = jnp.floor((fiota((1, slots), 1) + 0.5) * (1.0 / fan))
    peer_s = (ids & 63).astype(F32)
    off_s = (ids >> 6).astype(F32)
    pos_s = as_row(recv_ref[...] & 127).astype(F32)
    at_off = fiota((32, slots), 0) == off_s
    values = jnp.concatenate(
        [jnp.where(at_off, atom_s, 0.0), jnp.where(at_off, peer_s, 0.0)], axis=0
    ).astype(BF16)
    write_hots(hot_mir_ref, dot_nt(one_hot(fiota((cap, slots), 0) == pos_s), values))


def places_body(
    pack_ref, place_ref, wb_ref, pick_own_ref, pick_mir_ref, perm_ref, owned_ref, wcat_ref
):
    fan, atoms = pack_ref.shape
    cap = pick_own_ref.shape[0] // OFFS
    pack = pack_ref[...]
    off = ((pack & 2047) >> 6).astype(F32)
    kind = (pack >> 11) & 3
    pos_in = (pack >> 13).astype(F32)
    place = place_ref[...]
    owned = jnp.where(place > 0.5, 1.0, 0.0)
    owned_ref[...] = owned
    src = jnp.where(kind == 1, place, jnp.where(kind == 2, pos_in + 1.0, 0.0))
    rank = ranked_among(off * 2.0 + owned)
    target = off * float(GROUPS) + (2.0 - 2.0 * owned) + rank
    row = fiota((fan, atoms), 0)
    sorted_src = jnp.zeros((fan, atoms), F32)
    for s in range(fan):
        sorted_src = jnp.where(target[s : s + 1, :] == row, src[s : s + 1, :], sorted_src)
    spread = one_hot((iota((cap, atoms), 0) >> 1) == iota((cap, atoms), 1))
    spread = dot_nt(spread, sorted_src.astype(BF16))
    member = iota((cap, fan), 1) & 3
    parity = iota((cap, fan), 0) & 1
    fold = one_hot((iota((fan, 32), 0) >> 2) == iota((fan, 32), 1))
    lane = fiota((cap, cap), 1)
    for shift, pick_ref in ((0, pick_own_ref), (2, pick_mir_ref)):
        kept = jnp.where(member == parity + shift, spread, 0.0).astype(BF16)
        index = dot(kept, fold) - 1.0
        for o in range(OFFS):
            pick_ref[cap * o : cap * (o + 1), :] = one_hot(index[:, o : o + 1] == lane)

    spot = off * 8.0 + (iota((fan, atoms), 1) & 3).astype(F32) * 2.0 + rank
    lane = fiota((fan, 2 * fan), 1)
    for q in range(atoms // 4):
        perm_ref[4 * fan * q : 4 * fan * (q + 1), :] = jnp.concatenate(
            [jnp.where(spot[:, 4 * q + i : 4 * q + i + 1] == lane, 1.0, 0.0) for i in range(4)],
            axis=0,
        ).astype(BF16)

    block = wb_ref.shape[0]
    row = fiota((block, block), 0)
    col = fiota((block, block), 1)
    major = jnp.floor((row + 0.5) * (1.0 / ORB))
    wcat_ref[:, :128] = wb_ref[...]
    wcat_ref[:, 128:] = dot(
        one_hot((row - ORB * major) * ORB + major == col), wb_ref[...]
    ).astype(BF16)


def node_body(layer):
    def body(adj_ref, other_ref, ghost_ref, wm_ref, wu_ref, gain_ref, out_ref):
        ghosts = ghost_ref.shape[0]
        half = ghosts // 2
        atoms = ghosts // OFFS
        mixed = dot(adj_ref[...], ghost_ref[...])
        other = dot(other_ref[:, :half], ghost_ref[half:, :])
        other += dot(other_ref[:, half:], ghost_ref[:half, :])
        mixed = jnp.concatenate([mixed, other], axis=0).astype(BF16)
        hidden = jnp.concatenate(
            [ghost_ref[atoms * 4 : atoms * 5, :], ghost_ref[atoms * 13 : atoms * 14, :]], axis=0
        )
        summed = (dot(mixed, wm_ref[layer]) * 0.125).astype(BF16)
        updated = hidden.astype(F32) + silu(dot(summed, wu_ref[layer]))
        out_ref[...] = (rms_norm(updated) * gain_ref[layer : layer + 1, :]).astype(BF16)

    return body


CHUNK = 6


def fill_table(ghost_ref, w_local, w_ghost, table):
    atoms = ghost_ref.shape[0] // OFFS
    local = dot(ghost_ref[atoms * 4 : atoms * 5, :], w_local).astype(BF16)
    distant = dot(ghost_ref[...], w_ghost).astype(BF16)
    blank = jnp.zeros((atoms, 128), BF16)
    for o in range(OFFS):
        base = 2 * atoms * o
        table[base : base + atoms, :128] = local
        table[base : base + atoms, 128:] = blank
        table[base + atoms : base + 2 * atoms, :128] = blank
        table[base + atoms : base + 2 * atoms, 128:] = distant[atoms * o : atoms * (o + 1)]


def chosen_product(hot_ref, table, c):
    cap = hot_ref.shape[0] // OFFS
    chosen = jnp.concatenate(
        [
            dot(hot_ref[cap * o : cap * (o + 1), :], table[cap * o : cap * (o + 1), :])
            for o in range(CHUNK * c, CHUNK * (c + 1))
        ],
        axis=0,
    )
    return chosen[:, :128] * chosen[:, 128:]


def edge_all(e_ref, hot_ref, ghost_ref, w_local, w_ghost, w_in, w_out, table, out_ref):
    cap = e_ref.shape[0] // OFFS
    fill_table(ghost_ref, w_local, w_ghost, table)
    for c in range(OFFS // CHUNK):
        span = slice(CHUNK * cap * c, CHUNK * cap * (c + 1))
        state = e_ref[span, :]
        gate = silu(dot(state, w_in) * chosen_product(hot_ref, table, c)).astype(BF16)
        out_ref[span, :] = rms_norm(state.astype(F32) + dot(gate, w_out)).astype(BF16)


def edge_body(layer, hand_on=False):
    def body(e_ref, hot_ref, ghost_ref, wl_ref, wg_ref, wi_ref, wo_ref, *refs):
        if hand_on:
            refs[2][...] = refs[0][...]
            refs = (refs[1], refs[3])
        out_ref, table = refs
        edge_all(
            e_ref, hot_ref, ghost_ref, wl_ref[layer], wg_ref[layer], wi_ref[layer], wo_ref[layer],
            table, out_ref,
        )

    return body


def twice(weight):
    blank = jnp.zeros_like(weight)
    return jnp.concatenate(
        [
            jnp.concatenate([weight, blank], axis=1),
            jnp.concatenate([blank, weight], axis=1),
        ],
        axis=0,
    )


def final_body(layer):
    def body(
        own_ref, mir_ref, ho_ref, hm_ref, ghost_ref, wl_ref, wr_ref, wi_ref, wo_ref,
        po_ref, pm_ref, perm_ref, owned_ref, wcat_ref,
        out_ref, table_own, table_mir, ranked, rows,
    ):
        atoms = ghost_ref.shape[0] // OFFS
        cap = own_ref.shape[0] // OFFS
        fan = out_ref.shape[1] // atoms
        w_in, w_out = twice(wi_ref[layer]), twice(wo_ref[layer])
        fill_table(ghost_ref, wl_ref[layer], wr_ref[layer], table_own)
        fill_table(ghost_ref, wr_ref[layer], wl_ref[layer], table_mir)
        for c in range(OFFS // CHUNK):
            span = slice(CHUNK * cap * c, CHUNK * cap * (c + 1))
            state = jnp.concatenate([own_ref[span, :], mir_ref[span, :]], axis=1)
            chosen = jnp.concatenate(
                [chosen_product(ho_ref, table_own, c), chosen_product(hm_ref, table_mir, c)],
                axis=1,
            )
            gate = silu(dot(state, w_in) * chosen).astype(BF16)
            renewed = state.astype(F32) + dot(gate, w_out)
            e_own = rms_norm(renewed[:, :128]).astype(BF16)
            e_mir = rms_norm(renewed[:, 128:]).astype(BF16)
            for i in range(CHUNK):
                o = CHUNK * c + i
                here = slice(cap * i, cap * (i + 1))
                span = slice(cap * o, cap * (o + 1))
                ranked[span, :128] = dot(po_ref[span, :], e_own[here])
                ranked[span, 128:] = dot(pm_ref[span, :], e_mir[here])
        for q in range(atoms // 4):
            span = slice(4 * fan * q, 4 * fan * (q + 1))
            tiles = jnp.concatenate(
                [ranked[cap * o + 8 * q : cap * o + 8 * (q + 1), :] for o in range(OFFS)], axis=0
            ).astype(BF16)
            spread = dot(perm_ref[span, :], tiles)
            mine = jnp.concatenate(
                [owned_ref[:, 4 * q + i : 4 * q + i + 1] for i in range(4)], axis=0
            )
            mine = mine > 0.5
            rows[span, :128] = jnp.where(mine, spread[:, :128], 0.0).astype(BF16)
            rows[span, 128:] = jnp.where(mine, 0.0, spread[:, 128:]).astype(BF16)
        step = 16 * fan
        for g in range(atoms // 16):
            out_ref[:, step * g : step * (g + 1)] = dot_nt(
                wcat_ref[...], rows[step * g : step * (g + 1), :]
            ).astype(BF16)

    return body


def shards(
    atom_feats, bond_embed, pair_dist, neighbours, slot_kind, own_rows, send_pos, recv_pos,
    w_left, w_right, w_edge_in, w_edge_out, w_msg, w_upd, node_gain, w_block,
):
    atoms, channels = atom_feats.shape
    slots = neighbours.shape[0]
    fan = slots // atoms
    owned = own_rows.shape[0]
    cap = owned // OFFS
    block = w_block.shape[1]
    ghosts = OFFS * atoms

    def array(*shape, dtype=BF16):
        return jax.ShapeDtypeStruct(shape, dtype)

    def tiles(values):
        return values.reshape(-1, 128)

    send, own = tiles(send_pos), tiles(own_rows)
    nb, kind, recv, dist = map(tiles, (neighbours, slot_kind, recv_pos, pair_dist))
    opposite = swapped(atom_feats, "layer")
    both = jnp.concatenate(
        [(nb | (kind << 11) | ((recv & 127) << 13)).astype(F32), dist], axis=0
    )
    adjacency, pack, hidden = call(
        slots_body,
        (array(atoms, ghosts), array(fan, atoms, dtype=jnp.int32), array(atoms, channels)),
        both, atom_feats,
        us=2.0,
    )
    other = swapped(adjacency, "layer")
    sheets = jnp.concatenate([hidden, opposite], axis=0)
    ordered, centre = call(
        order_body,
        (array(owned, channels), array(2 * atoms, channels)),
        send, bond_embed, sheets,
        us=2.0,
    )
    outgoing = ordered.reshape(2, 3, 3, cap, channels)
    crossed = swapped(outgoing[1], "layer")
    shifted = across_rows(outgoing, crossed)
    mirror = across_columns(shifted).reshape(owned, channels)
    rows = rows_of(
        sheets.reshape(2, 1, 1, atoms, channels), centre.reshape(2, 1, 1, atoms, channels)
    )
    hot_own, hot_mir, place = call(
        pairs_body,
        (array(owned, 128), array(owned, 128), array(fan, atoms, dtype=F32)),
        send, own, nb, kind, recv, pack,
        after=(rows,),
        us=2.5,
    )
    table = pltpu.VMEM((2 * ghosts, 2 * channels), BF16)
    state = array(owned, channels)

    def framed_sheets(value):
        return value.reshape(2, 1, 1, atoms, channels)

    def edge(layer, own, after=(), hand_on=()):
        values = (ordered, hot_own) if own else (mirror, hot_mir)
        weights = (w_left, w_right) if own else (w_right, w_left)
        outs = (state,) + tuple(array(*v.shape) for v in hand_on) if hand_on else state
        return call(
            edge_body(layer, bool(hand_on)),
            outs,
            *values, ghosts_at[layer], *weights, w_edge_in, w_edge_out, *hand_on,
            after=after,
            scratch=[table],
            us=1.4,
        )

    def node(layer, after):
        return call(
            node_body(layer),
            array(2 * atoms, channels),
            adjacency, other, ghosts_at[layer], w_msg, w_upd, node_gain,
            after=after,
            us=0.6,
        )

    ghosts_at = [columns_of(rows)]
    sheets = node(0, (crossed,))
    pick_own, pick_mir, perm, mine, w_cat = call(
        places_body,
        (
            array(owned, cap),
            array(owned, cap),
            array(slots, 2 * fan),
            array(fan, atoms, dtype=F32),
            array(block, 2 * channels),
        ),
        pack, place, w_block.T,
        after=(sheets,),
        us=2.5,
    )
    ghosts_at.append(ghosts_of(framed_sheets(sheets), framed_sheets(sheets)))
    ordered = edge(0, True)
    sheets = node(1, (perm, ordered, shifted))
    ordered, centre = edge(1, True, hand_on=(sheets,))
    mirror = edge(0, False)
    rows = rows_of(framed_sheets(sheets), framed_sheets(centre))
    mirror, middle = edge(1, False, hand_on=(rows.reshape(6 * atoms, channels),))
    ghost = columns_of(rows, middle.reshape(rows.shape))
    return call(
        final_body(2),
        array(block, slots),
        ordered, mirror, hot_own, hot_mir, ghost, w_left, w_right, w_edge_in, w_edge_out,
        pick_own, pick_mir, perm, mine, w_cat,
        scratch=[
            table,
            table,
            pltpu.VMEM((owned, 2 * channels), F32),
            pltpu.VMEM((slots, 2 * channels), BF16),
        ],
        us=7.0,
    )


def solution(mesh):
    axes = ("gx", "gy", "layer")
    rows = P(axes, None)
    flat = P(axes)
    placed = (rows, rows) + (flat,) * 6 + (P(),) * 8
    return jax.shard_map(
        shards,
        mesh=mesh,
        in_specs=placed,
        out_specs=P(None, axes),
        check_vma=False,
    )
```
